32 devices in a mesh: pipe: 2 (over core), dp: 16 (over z, y, x).
Axes of the slice: x: 2, y: 2, z: 4, core: 2. Of those that a mesh axis runs over, the one named last changes fastest.
Arguments:
- tokens: bfloat16 [4, 8192, 384], P(None, 'dp'), may hold values from -6 to 6
- centres: float32 [4, 3, 8192], P(None, None, 'dp'), may hold values from -4 to 4
- visible: int32 [4, 8192], P(None, 'dp'), may hold values 0 or 1
- lengths: int32 [4, 128], P(None, 'dp'), may hold values from 0 to 512, as said below
- cotangent: bfloat16 [4, 8192, 384], P(None, 'dp'), may hold values from -6 to 6
- attend_gain: float32 [2, 384], P('pipe'), may hold values from 0.5 to 1.5
- attend_shift: float32 [2, 384], P('pipe'), may hold values from -1.75 to 1.75
- joint_weight: bfloat16 [2, 384, 1152], P('pipe'), may hold values from -0.3125 to 0.3125
- output_weight: bfloat16 [2, 384, 384], P('pipe'), may hold values from -1.25 to 1.25
- output_bias: float32 [2, 384], P('pipe'), may hold values from -1.75 to 1.75
- feed_gain: float32 [2, 384], P('pipe'), may hold values from 0.5 to 1.5
- feed_shift: float32 [2, 384], P('pipe'), may hold values from -1.75 to 1.75
- expand_weight: bfloat16 [2, 384, 1536], P('pipe'), may hold values from -0.3125 to 0.3125
- expand_bias: float32 [2, 1536], P('pipe'), may hold values from -1.75 to 1.75
- reduce_weight: bfloat16 [2, 1536, 384], P('pipe'), may hold values from -0.15625 to 0.15625
- reduce_bias: float32 [2, 384], P('pipe'), may hold values from -1.75 to 1.75
- place_weight: float32 [2, 3, 128], P('pipe'), may hold values from -3.5 to 3.5
- place_bias: float32 [2, 128], P('pipe'), may hold values from -3 to 3
- embed_weight: bfloat16 [2, 128, 384], P('pipe'), may hold values from -0.5 to 0.5
- mask_token: float32 [384], replicated, may hold values from -6 to 6
Outputs:
- phase_out: bfloat16 [2, 4, 8192, 384], P('pipe', None, 'dp')
- phase_in_grad: float32 [2, 4, 8192, 384], P('pipe', None, 'dp')
- attend_gain_grad: float32 [2, 384], P('pipe')
- attend_shift_grad: float32 [2, 384], P('pipe')
- joint_weight_grad: float32 [2, 384, 1152], P('pipe')
- output_weight_grad: float32 [2, 384, 384], P('pipe')
- output_bias_grad: float32 [2, 384], P('pipe')
- feed_gain_grad: float32 [2, 384], P('pipe')
- feed_shift_grad: float32 [2, 384], P('pipe')
- expand_weight_grad: float32 [2, 384, 1536], P('pipe')
- expand_bias_grad: float32 [2, 1536], P('pipe')
- reduce_weight_grad: float32 [2, 1536, 384], P('pipe')
- reduce_bias_grad: float32 [2, 384], P('pipe')
- place_weight_grad: float32 [2, 3, 128], P('pipe')
- place_bias_grad: float32 [2, 128], P('pipe')
- embed_weight_grad: float32 [2, 128, 384], P('pipe')
- mask_token_grad: float32 [384], replicated
The draws below stay inside these ranges and needn't reach their ends.
Inputs may be any that keep to these rules, and one draw needn't show every extreme that they name: `lengths`: each aligned group of 8 entries (one index of dp in one micro-batch) sums to 512: either one scan of 512 patches followed by zeros, or 8 objects of 33 to 95 patches; every micro-batch holds at least one scan.
All inputs are finite; a program needn't handle non-finite values. No bound on the sum of `visible` on one device may be relied on, other than what follows from the above.
Results may differ from the reference program's by a relative error of at most 0.014.
Values may be sent and summed in bfloat16 or wider, within the bound.
No kernel may reach another device: no remote copies, remote signals or barrier semaphores. Data moves between devices by JAX's collectives and lax.ppermute only.
A program may use at most 256 MiB of HBM per device.

```python
import jax
import jax.numpy as jnp
from jax import lax

D = 384
HEADS = 6
HD = 64
FF = 1536
PH = 128
OBJ = 64
MB = 4
TOK_DEV = 512
SLOTS = 8
TOKENS = 8192
N_DP = 16


def draw_lengths(key, part):
    key = jax.random.fold_in(key, 7)
    slot_count = TOK_DEV // OBJ
    per_batch = TOKENS // TOK_DEV
    first_key, second_key, third_key = jax.random.split(key, 3)
    offsets = jax.random.randint(first_key, (MB, per_batch, slot_count // 2), -(OBJ // 2 - 1), OBJ // 2)
    paired = jnp.stack([OBJ + offsets, OBJ - offsets], axis=-1).reshape(MB, per_batch, slot_count)
    scan_flag = jax.random.randint(second_key, (MB, per_batch), 0, 8) == 0
    chosen = jax.random.randint(third_key, (MB,), 0, per_batch)
    scan_flag = scan_flag | (jnp.arange(per_batch)[None, :] == chosen[:, None])
    whole = jnp.where(jnp.arange(slot_count) == 0, TOK_DEV, 0)
    merged = jnp.where(scan_flag[:, :, None], whole[None, None, :], paired)
    return merged.reshape(MB, per_batch * slot_count).astype(jnp.int32)


def set_ends(values, key, low, largest):
    longest = values.shape.index(max(values.shape))
    spots = []
    for shift in (0, 1):
        where = [jax.random.randint(jax.random.fold_in(key, axis), (), 0, length) for axis, length in enumerate(values.shape)]
        where[longest] = (where[longest] + shift) % values.shape[longest]
        spots.append(tuple(where))
    return values.at[spots[0]].set(low).at[spots[1]].set(largest)


def shard_levels(key, dims, cuts, low, high):
    factor_of = 1.0
    for position, blocks in cuts:
        draws = jax.random.uniform(jax.random.fold_in(jax.random.fold_in(key, 6), position), (blocks,), jnp.float32, low / len(cuts), high / len(cuts))
        factor_of = factor_of * jnp.repeat(jnp.exp(draws), dims[position] // blocks).reshape((-1,) + (1,) * (len(dims) - 1 - position))
    return factor_of


def normal_values(own_key, dims, deviation, limit, cuts=(), kind=jnp.bfloat16):
    level = shard_levels(own_key, dims, cuts, -0.22, 0.18) if cuts else 1.0
    values = jax.random.normal(own_key, dims, jnp.float32) * deviation * level
    return jnp.minimum(jnp.maximum(values, -limit), limit).astype(kind)


def setup_inputs(seed: int = 0) -> dict:
    seeds = jax.random.split(jax.random.key(seed), 21)
    tokens = normal_values(seeds[0], (MB, TOKENS, D), 1.0, 6.0, ((1, 16),))
    centres = normal_values(seeds[1], (MB, 3, TOKENS), 1.0, 4.0, ((2, 16),), jnp.float32)
    visible = set_ends((jax.random.randint(seeds[2], (MB, TOKENS), 0, 5) < 2).astype(jnp.int32), jax.random.fold_in(seeds[2], 1), 0, 1)
    lengths = draw_lengths(jax.random.fold_in(seeds[20], 71), 0)
    cotangent = normal_values(seeds[4], (MB, TOKENS, D), 1.0, 6.0, ((1, 16),))
    attend_gain = jnp.clip(1.0 + 0.1 * jax.random.normal(seeds[5], (2, D), jnp.float32), 0.5, 1.5)
    attend_shift = normal_values(seeds[6], (2, D), 0.3, 1.75, ((0, 2),), jnp.float32)
    joint_weight = normal_values(seeds[7], (2, D, 3 * D), D ** -0.5, 0.3125, ((0, 2),))
    output_weight = normal_values(seeds[8], (2, D, D), (D // 16) ** -0.5, 1.25, ((0, 2),))
    output_bias = normal_values(seeds[9], (2, D), 0.3, 1.75, ((0, 2),), jnp.float32)
    feed_gain = jnp.clip(1.0 + 0.1 * jax.random.normal(seeds[10], (2, D), jnp.float32), 0.5, 1.5)
    feed_shift = normal_values(seeds[11], (2, D), 0.3, 1.75, ((0, 2),), jnp.float32)
    expand_weight = normal_values(seeds[12], (2, D, FF), D ** -0.5, 0.3125, ((0, 2),))
    expand_bias = normal_values(seeds[13], (2, FF), 0.3, 1.75, ((0, 2),), jnp.float32)
    reduce_weight = normal_values(seeds[14], (2, FF, D), FF ** -0.5, 0.15625, ((0, 2),))
    reduce_bias = normal_values(seeds[15], (2, D), 0.3, 1.75, ((0, 2),), jnp.float32)
    place_weight = normal_values(seeds[16], (2, 3, PH), 3 ** -0.5, 3.5, ((0, 2),), jnp.float32)
    place_bias = normal_values(seeds[17], (2, PH), 0.5, 3.0, ((0, 2),), jnp.float32)
    embed_weight = normal_values(seeds[18], (2, PH, D), PH ** -0.5, 0.5, ((0, 2),))
    mask_token = normal_values(seeds[19], (D,), 1.0, 6.0, (), jnp.float32)
    return dict(tokens=tokens, centres=centres, visible=visible, lengths=lengths, cotangent=cotangent, attend_gain=attend_gain, attend_shift=attend_shift, joint_weight=joint_weight, output_weight=output_weight, output_bias=output_bias, feed_gain=feed_gain, feed_shift=feed_shift, expand_weight=expand_weight, expand_bias=expand_bias, reduce_weight=reduce_weight, reduce_bias=reduce_bias, place_weight=place_weight, place_bias=place_bias, embed_weight=embed_weight, mask_token=mask_token)


@jax.custom_vjp
def low(v):
    return lax.optimization_barrier(v.astype(jnp.bfloat16)).astype(jnp.float32)

@jax.custom_vjp
def low_back(v):
    return v

def low_keep(v):
    return (low(v), None)

def low_pass(kept, grad):
    return (grad,)

def back_keep(v):
    return (v, None)

def back_low(kept, grad):
    return (low(grad),)
low.defvjp(low_keep, low_pass)
low_back.defvjp(back_keep, back_low)
HIGH_MODE = lax.Precision.HIGHEST
NEG_FILL = -1e+30

def rounded_both(values):
    return low_back(low(values))

def matmul(left_side, right_side):
    return jnp.dot(left_side, right_side, precision=HIGH_MODE)

def smooth(values):
    return jax.nn.gelu(values, approximate=True)

def layer_norm(values, gain, shift):
    centred = values - lax.optimization_barrier(jnp.mean(values, -1, keepdims=True))
    variance = lax.optimization_barrier(jnp.mean(centred * centred, -1, keepdims=True))
    return centred * lax.rsqrt(variance + 1e-05) * gain + shift

def allowed_mask(object_lengths, key_flags):
    row_count = key_flags.shape[0]
    places = jnp.arange(row_count, dtype=jnp.int32)
    object_ends = jnp.cumsum(object_lengths).astype(jnp.int32)
    segment = lax.optimization_barrier(jnp.sum((places[:, None] >= object_ends[None, :]).astype(jnp.int32), axis=1))
    same_object = segment[:, None] == segment[None, :]
    return same_object & ((key_flags[None, :] > 0) | (places[:, None] == places[None, :]))

def layer(phase_weights, inputs, key_flags, object_lengths):
    row_count = inputs.shape[0]
    first_low = low(layer_norm(inputs, phase_weights[0], phase_weights[1]))
    joint = rounded_both(matmul(first_low, phase_weights[2]))
    queries = joint[:, :D].reshape(row_count, HEADS, HD)
    keys_part = joint[:, D:2 * D].reshape(row_count, HEADS, HD)
    values_part = joint[:, 2 * D:].reshape(row_count, HEADS, HD)
    raw_scores = low_back(jnp.einsum('qhd,khd->hqk', queries, keys_part, precision=HIGH_MODE))
    allowed = allowed_mask(object_lengths, key_flags)
    scores = jnp.where(allowed[None], raw_scores * HD ** (-0.5), NEG_FILL)
    row_max = lax.optimization_barrier(jnp.max(scores, -1, keepdims=True))
    raised = jnp.exp(scores - row_max)
    soft_low = low(raised / lax.optimization_barrier(jnp.sum(raised, -1, keepdims=True)))
    mixed = jnp.einsum('hqk,khd->qhd', soft_low, values_part, precision=HIGH_MODE).reshape(row_count, D)
    mixed_low = rounded_both(mixed)
    middle = inputs + low_back(matmul(mixed_low, phase_weights[3]) + phase_weights[4])
    second_low = low(layer_norm(middle, phase_weights[5], phase_weights[6]))
    hidden = low_back(matmul(second_low, phase_weights[7]) + phase_weights[8])
    act_low = low(smooth(hidden))
    return middle + low_back(matmul(act_low, phase_weights[9]) + phase_weights[10])

def stack_blocks(phase_weights, inputs, key_flags, object_lengths):
    blocks = inputs.reshape(N_DP, TOK_DEV, D)
    flag_blocks = key_flags.reshape(N_DP, TOK_DEV)
    length_blocks = object_lengths.reshape(N_DP, SLOTS)

    def one_block(packed):
        return layer(phase_weights, packed[0], packed[1], packed[2])
    return lax.map(jax.checkpoint(one_block), (blocks, flag_blocks, length_blocks)).reshape(TOKENS, D)

def place_embed(phase_weights, centre_rows):
    pre = jnp.dot(centre_rows.T, phase_weights[11], precision=HIGH_MODE) + phase_weights[12]
    return low_back(matmul(low(smooth(pre)), phase_weights[13]))

def forward(params, token_rows, spare, mask_row, centre_rows, visible_rows, object_lengths):
    encoder = [piece[0] for piece in params]
    decoder = [piece[1] for piece in params]
    enc_in = token_rows + place_embed(encoder, centre_rows)
    enc_out = rounded_both(stack_blocks(encoder, enc_in, visible_rows, object_lengths))
    dec_in = jnp.where(visible_rows[:, None] > 0, enc_out, mask_row[None, :]) + place_embed(decoder, centre_rows) + spare
    dec_out = stack_blocks(decoder, dec_in, jnp.ones_like(visible_rows), object_lengths)
    return (enc_out, dec_out)

def reference(tokens, centres, visible, lengths, cotangent, attend_gain, attend_shift, joint_weight, output_weight, output_bias, feed_gain, feed_shift, expand_weight, expand_bias, reduce_weight, reduce_bias, place_weight, place_bias, embed_weight, mask_token):
    params = [piece.astype(jnp.float32) for piece in (attend_gain, attend_shift, joint_weight, output_weight, output_bias, feed_gain, feed_shift, expand_weight, expand_bias, reduce_weight, reduce_bias, place_weight, place_bias, embed_weight)]
    mask_row = mask_token.astype(jnp.float32)

    def step(carry, inputs):
        token_rows, centre_rows, visible_rows, object_lengths, upstream = inputs
        spare = jnp.zeros((TOKENS, D), jnp.float32)

        def local(param_list, rows_in, spare_in, mask_in):
            return forward(param_list, rows_in, spare_in, mask_in, centre_rows, visible_rows, object_lengths)
        outputs, pull = jax.vjp(local, params, token_rows.astype(jnp.float32), spare, mask_row)
        grad_params, grad_tokens, grad_spare, grad_mask = pull((jnp.zeros_like(outputs[0]), upstream.astype(jnp.float32)))
        new_params = [running + addend for running, addend in zip(carry[0], grad_params)]
        return ((new_params, carry[1] + grad_mask), (outputs[0].astype(jnp.bfloat16), outputs[1].astype(jnp.bfloat16), grad_tokens, grad_spare))
    start = ([jnp.zeros_like(piece) for piece in params], jnp.zeros_like(mask_row))
    (grads, mask_grad), (enc_rows, dec_rows, token_grads, dec_grads) = lax.scan(step, start, (tokens, centres, visible, lengths, cotangent))
    phase_out = jnp.stack([enc_rows, dec_rows])
    phase_in_grad = jnp.stack([token_grads, dec_grads])
    return (phase_out, phase_in_grad, grads[0], grads[1], grads[2], grads[3], grads[4], grads[5], grads[6], grads[7], grads[8], grads[9], grads[10], grads[11], grads[12], grads[13], mask_grad)
```

```python
import math

import jax
import jax.numpy as jnp
from jax import lax
from jax.experimental import pallas as pl
from jax.experimental.pallas import tpu as pltpu
from jax.sharding import PartitionSpec as P

HEADS = 6
NEG_FILL = -1e30
NORM_EPS = 1e-05
GELU_A = math.sqrt(2.0 / math.pi)
GELU_B = GELU_A * 0.044715
BF = jnp.bfloat16
F32 = jnp.float32
VMEM_LIMIT = 56 * 2**20


def dot(a, b):
    return jnp.dot(a, b, preferred_element_type=F32)


def dot_rt(a, b):
    return lax.dot_general(a, b, (((1,), (1,)), ((), ())), preferred_element_type=F32)


def dot_lt(a, b):
    return lax.dot_general(a, b, (((0,), (0,)), ((), ())), preferred_element_type=F32)


def gelu_both(v):
    v2 = v * v
    h = 0.5 * jnp.tanh(v * (GELU_A + GELU_B * v2)) + 0.5
    slope = h + (h - h * h) * (v * (2.0 * GELU_A + 6.0 * GELU_B * v2))
    return v * h, slope


def gelu_only(v):
    return v * (0.5 * jnp.tanh(v * (GELU_A + GELU_B * (v * v))) + 0.5)


def norm_parts(x):
    scale = 1.0 / x.shape[-1]
    centred = x - jnp.sum(x, -1, keepdims=True) * scale
    var = jnp.sum(centred * centred, -1, keepdims=True) * scale
    inverse = lax.rsqrt(var + NORM_EPS)
    return centred * inverse, inverse


def norm_back(u, z, inverse, gain):
    scale = 1.0 / u.shape[-1]
    w = u * gain
    m1 = jnp.sum(w, -1, keepdims=True) * scale
    m2 = jnp.sum(w * z, -1, keepdims=True) * scale
    return inverse * (w - m1 - z * m2)


def place_pre(centre, place_weight, place_bias):
    pre = lax.dot_general(
        centre,
        place_weight,
        (((0,), (0,)), ((), ())),
        precision=lax.Precision.HIGHEST,
        preferred_element_type=F32,
    )
    return pre + place_bias


def column_of(row, width):
    rows = lax.broadcasted_iota(jnp.int32, (16, row.shape[1]), 0)
    top = jnp.where(rows == 0, jnp.broadcast_to(row, rows.shape), 0).astype(F32)
    return dot_lt(top.astype(BF), jnp.ones((16, width), BF))


def segments(lengths, micro_index, slots, places):
    total = jnp.int32(0)
    seg = jnp.zeros(places.shape, jnp.int32)
    for slot in range(slots):
        total = total + lengths[micro_index, slot]
        seg = seg + (places >= total).astype(jnp.int32)
    return seg


def lane_low(shape, half):
    return lax.broadcasted_iota(jnp.int32, shape, 1) < half


def attend_forward(decoding, rows_at_once, sel, lengths, *refs):
    (x_in, centres, visible, mask_token, ag, ash, wj, wo, bo, pw, pb, we) = refs[:12]
    (x_out, joint_out, e_out, inv_out, mixed_out, mid_out, bias) = refs[12:]
    step = pl.program_id(0)
    micro_index = sel[0] + step
    rows, width = x_in.shape[1], x_in.shape[2]
    slots = lengths.shape[1]
    head = width // HEADS
    pair = 2 * head

    pre = place_pre(centres[0], pw[...], pb[...])
    embed = dot(gelu_only(pre).astype(BF), we[...])
    seen = visible[pl.ds(micro_index, 1), :]
    source = x_in[0].astype(F32)
    if decoding:
        shown = column_of(seen, 128)[:, :1] > 0.5
        source = jnp.where(shown, source, mask_token[...])
    x = source + embed
    x_out[0] = x
    z, _ = norm_parts(x)
    low = (z * ag[...] + ash[...]).astype(BF)
    joint_out[0] = dot(low, wj[...]).astype(BF)

    places_k = lax.broadcasted_iota(jnp.int32, (1, rows), 1)
    seg_k = segments(lengths, micro_index, slots, places_k)
    seg_col = column_of(seg_k, 128)[:, :1].astype(jnp.int32)
    allowed = seg_col == seg_k
    if not decoding:
        places_q = lax.broadcasted_iota(jnp.int32, (rows, rows), 0)
        places_kk = lax.broadcasted_iota(jnp.int32, (rows, rows), 1)
        allowed = allowed & ((seen > 0) | (places_q == places_kk))
    bias[...] = jnp.where(allowed, 0.0, NEG_FILL)

    low_k = lane_low((rows, pair), head)
    low_q = lane_low((rows_at_once, pair), head)
    for p in range(HEADS // 2):
        qp = joint_out[0, :, p * pair : (p + 1) * pair] * BF(head**-0.5)
        kp = joint_out[0, :, width + p * pair : width + (p + 1) * pair]
        vp = joint_out[0, :, 2 * width + p * pair : 2 * width + (p + 1) * pair]
        v_low = jnp.where(low_k, vp, BF(1))
        v_high = jnp.where(low_k, BF(1), vp)
        for r0 in range(0, rows, rows_at_once):
            span = slice(r0, r0 + rows_at_once)
            q_rows = qp[span]
            out = []
            for side in range(2):
                q_one = jnp.where(low_q == (side == 0), q_rows, BF(0))
                s = dot_rt(q_one, kp) + bias[span, :]
                e = jnp.exp(s - jnp.max(s, -1, keepdims=True)).astype(BF)
                e_out[0, 2 * p + side, span, :] = e
                out.append(dot(e, v_high if side else v_low))
            inv = 1.0 / pltpu.roll(jnp.where(low_q, out[1], out[0]), head, 1)
            mixed = jnp.where(low_q, out[0], out[1]) * inv
            inv_out[0, span, p * pair : (p + 1) * pair] = inv
            mixed_out[0, span, p * pair : (p + 1) * pair] = mixed.astype(BF)
    mid_out[0] = x + (dot(mixed_out[0], wo[...]) + bo[...])


def attend_backward(decoding, rows_at_once, sel, lengths, *refs):
    (dmid_in, x_in, centres, visible, joint_in, e_in, inv_in, mixed_in) = refs[:8]
    (ag, ash, wj, wo, pw, pb, we) = refs[8:15]
    dx_out, send_back, joint_g, output_g, embed_g, small_g = refs[15:21]
    dl, mu, dj, ds = refs[21:25]
    step = pl.program_id(0)
    micro_index = sel[0] + step
    rows, width = x_in.shape[1], x_in.shape[2]
    head = width // HEADS
    pair = 2 * head
    hidden = pw.shape[1]

    @pl.when(step == 0)
    def _():
        joint_g[...] = jnp.zeros(joint_g.shape, F32)
        output_g[...] = jnp.zeros(output_g.shape, F32)
        embed_g[...] = jnp.zeros(embed_g.shape, F32)
        small_g[...] = jnp.zeros(small_g.shape, F32)

    dmid = dmid_in[0]
    dm = dmid.astype(BF)
    output_g[...] += dot_lt(mixed_in[0], dm)
    small_g[2:3, :] += jnp.sum(dm.astype(F32), 0, keepdims=True)
    dmix = dot_rt(dm, wo[...])
    low_dl = (dmix * inv_in[0]).astype(BF)
    dl[...] = low_dl
    mu[...] = (low_dl.astype(F32) * -mixed_in[0].astype(F32)).astype(BF)

    low_k = lane_low((rows, pair), head)
    ones = jnp.ones((rows, pair), BF)
    for p in range(HEADS // 2):
        cols = slice(p * pair, (p + 1) * pair)
        qp = joint_in[0, :, p * pair : (p + 1) * pair] * BF(head**-0.5)
        kp = joint_in[0, :, width + p * pair : width + (p + 1) * pair]
        vp = joint_in[0, :, 2 * width + p * pair : 2 * width + (p + 1) * pair]
        v_ext = jnp.concatenate([vp, ones], axis=1)
        dlp = dl[:, cols]
        mup = mu[:, cols]
        dq = dk = dv = None
        for side in range(2):
            mine = low_k == (side == 0)
            d_one = jnp.where(mine, dlp, BF(0))
            u_one = jnp.where(mine, mup, BF(0))
            ext = jnp.concatenate([d_one, u_one], axis=1)
            for r0 in range(0, rows, rows_at_once):
                span = slice(r0, r0 + rows_at_once)
                dp = dot_rt(ext[span], v_ext)
                ds[side, span, :] = (e_in[0, 2 * p + side, span, :].astype(F32) * dp).astype(BF)
            q_one = jnp.where(mine, qp, BF(0))
            k_one = jnp.where(mine, kp, BF(0))
            dv_one = dot_lt(e_in[0, 2 * p + side], d_one)
            dk_one = dot_lt(ds[side], q_one)
            dq_one = dot(ds[side], k_one)
            dv = dv_one if dv is None else dv + dv_one
            dk = dk_one if dk is None else dk + dk_one
            dq = dq_one if dq is None else dq + dq_one
        dj[:, p * pair : (p + 1) * pair] = (dq * head**-0.5).astype(BF)
        dj[:, width + p * pair : width + (p + 1) * pair] = dk.astype(BF)
        dj[:, 2 * width + p * pair : 2 * width + (p + 1) * pair] = dv.astype(BF)

    z, inverse = norm_parts(x_in[0])
    low = (z * ag[...] + ash[...]).astype(BF)
    joint_g[...] += dot_lt(low, dj[...])
    dn = dot_rt(dj[...], wj[...])
    small_g[0:1, :] += jnp.sum(dn * z, 0, keepdims=True)
    small_g[1:2, :] += jnp.sum(dn, 0, keepdims=True)
    dx = dmid + norm_back(dn, z, inverse, ag[...])
    dx_out[0] = dx
    if decoding:
        shown = column_of(visible[pl.ds(micro_index, 1), :], 128)[:, :1] > 0.5
        send_back[0] = jnp.where(shown, dx, 0.0).astype(BF)
        small_g[3:4, :] += jnp.sum(jnp.where(shown, 0.0, dx), 0, keepdims=True)

    pre = place_pre(centres[0], pw[...], pb[...])
    act, slope = gelu_both(pre)
    ge = dx.astype(BF)
    embed_g[...] += dot_lt(act.astype(BF), ge)
    dpre = slope * dot_rt(ge, we[...])
    place = jnp.dot(centres[0], dpre, precision=lax.Precision.HIGHEST, preferred_element_type=F32)
    small_g[4:7, 0:hidden] += place
    small_g[7:8, 0:hidden] += jnp.sum(dpre, 0, keepdims=True)


def feed_forward(mid_in, fg, fsh, w1, b1, w2, b2, out, act_out, slope_out, low, acc):
    step = pl.program_id(0)
    steps = pl.num_programs(0)

    @pl.when(step == 0)
    def _():
        z, _ = norm_parts(mid_in[...])
        low[...] = (z * fg[...] + fsh[...]).astype(BF)
        acc[...] = mid_in[...] + b2[...]

    hidden = dot(low[...], w1[...]) + b1[...]
    act, slope = gelu_both(hidden)
    act_low = act.astype(BF)
    act_out[...] = act_low
    slope_out[...] = slope.astype(BF)
    acc[...] += dot(act_low, w2[...])

    @pl.when(step == steps - 1)
    def _():
        out[...] = acc[...].astype(BF)


def feed_tail(g, dn_acc, mid_in, fg, dmid_out, small_g):
    z, inverse = norm_parts(mid_in[...])
    dn = dn_acc[...]
    dmid_out[...] = g + norm_back(dn, z, inverse, fg[...])
    small_g[0:1, :] = jnp.sum(dn * z, 0, keepdims=True)
    small_g[1:2, :] = jnp.sum(dn, 0, keepdims=True)
    small_g[2:3, :] = jnp.sum(g, 0, keepdims=True)


def feed_backward_chunk(low, act_low, slope, g, w1, w2, w1_g, w2_g, b1_g, dn_acc):
    dh = (slope * dot_rt(g, w2[...])).astype(BF)
    w2_g[...] = dot_lt(act_low, g)
    w1_g[...] = dot_lt(low, dh)
    b1_g[...] = jnp.sum(dh.astype(F32), 0, keepdims=True)
    dn_acc[...] += dot_rt(dh, w1[...])


def feed_both(mid_in, g_in, fg, fsh, w1, b1, w2, b2, out, dmid_out, w1_g, w2_g, b1_g, small_g, low, acc, dn_acc):
    step = pl.program_id(0)
    steps = pl.num_programs(0)

    @pl.when(step == 0)
    def _():
        z, _ = norm_parts(mid_in[...])
        low[...] = (z * fg[...] + fsh[...]).astype(BF)
        acc[...] = mid_in[...] + b2[...]
        dn_acc[...] = jnp.zeros(dn_acc.shape, F32)

    hidden = dot(low[...], w1[...]) + b1[...]
    act, slope = gelu_both(hidden)
    act_low = act.astype(BF)
    acc[...] += dot(act_low, w2[...])
    feed_backward_chunk(low[...], act_low, slope, g_in[...], w1, w2, w1_g, w2_g, b1_g, dn_acc)

    @pl.when(step == steps - 1)
    def _():
        out[...] = acc[...].astype(BF)
        feed_tail(g_in[...].astype(F32), dn_acc, mid_in, fg, dmid_out, small_g)


def feed_backward(mid_in, g_in, act_in, slope_in, fg, fsh, w1, w2, dmid_out, w1_g, w2_g, b1_g, small_g, low, dn_acc):
    step = pl.program_id(0)
    steps = pl.num_programs(0)

    @pl.when(step == 0)
    def _():
        z, _ = norm_parts(mid_in[...])
        low[...] = (z * fg[...] + fsh[...]).astype(BF)
        dn_acc[...] = jnp.zeros(dn_acc.shape, F32)

    feed_backward_chunk(low[...], act_in[...], slope_in[...].astype(F32), g_in[...], w1, w2, w1_g, w2_g, b1_g, dn_acc)

    @pl.when(step == steps - 1)
    def _():
        feed_tail(g_in[...].astype(F32), dn_acc, mid_in, fg, dmid_out, small_g)


def params():
    return pltpu.CompilerParams(vmem_limit_bytes=VMEM_LIMIT)


def whole(shape):
    return pl.BlockSpec(shape, lambda *_: (0,) * len(shape))


def sds(shape, kind):
    return jax.ShapeDtypeStruct(shape, kind)


def call_attend_forward(decoding, half, sel, lengths, x_in, centres, visible, mask_token, weights, rows_at_once=512):
    _, rows, width = x_in.shape
    ag, ash, wj, wo, bo, pw, pb, we = weights
    if decoding:
        x_spec = pl.BlockSpec((1, rows, width), lambda i, s, n: (i, 0, 0))
    else:
        x_spec = pl.BlockSpec((1, rows, width), lambda i, s, n: (s[0] + i, 0, 0))
    block = lambda *shape: pl.BlockSpec((1,) + shape, lambda i, s, n: (i,) + (0,) * len(shape))
    flops = 2 * rows * half * (width * 4 * width + 2 * HEADS * rows * 128)
    return pl.pallas_call(
        lambda *refs: attend_forward(decoding, rows_at_once, *refs),
        grid_spec=pltpu.PrefetchScalarGridSpec(
            num_scalar_prefetch=2,
            grid=(half,),
            in_specs=[
                x_spec,
                pl.BlockSpec((1,) + centres.shape[1:], lambda i, s, n: (s[0] + i, 0, 0)),
                whole(visible.shape),
                whole(mask_token.shape),
            ]
            + [whole(w.shape) for w in weights],
            out_specs=[
                block(rows, width),
                block(rows, 3 * width),
                block(HEADS, rows, rows),
                block(rows, width),
                block(rows, width),
                block(rows, width),
            ],
            scratch_shapes=[pltpu.VMEM((rows, rows), F32)],
        ),
        out_shape=[
            sds((half, rows, width), F32),
            sds((half, rows, 3 * width), BF),
            sds((half, HEADS, rows, rows), BF),
            sds((half, rows, width), F32),
            sds((half, rows, width), BF),
            sds((half, rows, width), F32),
        ],
        compiler_params=params(),
        cost_estimate=pl.CostEstimate(flops=flops, bytes_accessed=20 * 2**20, transcendentals=0),
        name="attend_forward_dec" if decoding else "attend_forward_enc",
    )(sel, lengths, x_in, centres, visible, mask_token, *weights)


def call_attend_backward(decoding, half, sel, lengths, dmid, x, centres, visible, joint, e, inv, mixed, weights, rows_at_once=512):
    _, rows, width = x.shape
    hidden = weights[4].shape[1]
    block = lambda *shape: pl.BlockSpec((1,) + shape, lambda i, s, n: (i,) + (0,) * len(shape))
    back = (half, rows, width) if decoding else (1, 16, width)
    return pl.pallas_call(
        lambda *refs: attend_backward(decoding, rows_at_once, *refs),
        grid_spec=pltpu.PrefetchScalarGridSpec(
            num_scalar_prefetch=2,
            grid=(half,),
            in_specs=[
                block(rows, width),
                block(rows, width),
                pl.BlockSpec((1,) + centres.shape[1:], lambda i, s, n: (s[0] + i, 0, 0)),
                whole(visible.shape),
                block(rows, 3 * width),
                block(HEADS, rows, rows),
                block(rows, width),
                block(rows, width),
            ]
            + [whole(w.shape) for w in weights],
            out_specs=[
                block(rows, width),
                block(rows, width) if decoding else whole(back),
                whole((width, 3 * width)),
                whole((width, width)),
                whole((hidden, width)),
                whole((8, width)),
            ],
            scratch_shapes=[
                pltpu.VMEM((rows, width), BF),
                pltpu.VMEM((rows, width), BF),
                pltpu.VMEM((rows, 3 * width), BF),
                pltpu.VMEM((2, rows, rows), BF),
            ],
        ),
        out_shape=[
            sds((half, rows, width), F32),
            sds(back, BF),
            sds((width, 3 * width), F32),
            sds((width, width), F32),
            sds((hidden, width), F32),
            sds((8, width), F32),
        ],
        compiler_params=params(),
        name="attend_backward_dec" if decoding else "attend_backward_enc",
    )(sel, lengths, dmid, x, centres, visible, joint, e, inv, mixed, *weights)


def feed_specs(rows, width, ff, chunk):
    w1 = pl.BlockSpec((width, chunk), lambda i: (0, i))
    b1 = pl.BlockSpec((1, chunk), lambda i: (0, i))
    w2 = pl.BlockSpec((chunk, width), lambda i: (i, 0))
    wide = pl.BlockSpec((rows, chunk), lambda i: (0, i))
    return w1, b1, w2, wide


def call_feed_forward(mid, fg, fsh, w1, b1, w2, b2, chunk=768):
    rows, width = mid.shape
    ff = w1.shape[1]
    s1, sb, s2, wide = feed_specs(rows, width, ff, chunk)
    row = whole((1, width))
    return pl.pallas_call(
        feed_forward,
        grid=(ff // chunk,),
        in_specs=[whole((rows, width)), row, row, s1, sb, s2, row],
        out_specs=[whole((rows, width)), wide, wide],
        out_shape=[sds((rows, width), BF), sds((rows, ff), BF), sds((rows, ff), BF)],
        scratch_shapes=[pltpu.VMEM((rows, width), BF), pltpu.VMEM((rows, width), F32)],
        compiler_params=params(),
        name="feed_forward_enc",
    )(mid, fg, fsh, w1, b1, w2, b2)


def call_feed_both(mid, g, fg, fsh, w1, b1, w2, b2, chunk=768):
    rows, width = mid.shape
    ff = w1.shape[1]
    s1, sb, s2, wide = feed_specs(rows, width, ff, chunk)
    row = whole((1, width))
    full = whole((rows, width))
    return pl.pallas_call(
        feed_both,
        grid=(ff // chunk,),
        in_specs=[full, full, row, row, s1, sb, s2, row],
        out_specs=[full, full, s1, s2, sb, whole((8, width))],
        out_shape=[
            sds((rows, width), BF),
            sds((rows, width), F32),
            sds((width, ff), F32),
            sds((ff, width), F32),
            sds((1, ff), F32),
            sds((8, width), F32),
        ],
        scratch_shapes=[pltpu.VMEM((rows, width), BF), pltpu.VMEM((rows, width), F32), pltpu.VMEM((rows, width), F32)],
        compiler_params=params(),
        name="feed_both_dec",
    )(mid, g, fg, fsh, w1, b1, w2, b2)


def call_feed_backward(mid, g, act, slope, fg, fsh, w1, w2, chunk=768):
    rows, width = mid.shape
    ff = w1.shape[1]
    s1, sb, s2, wide = feed_specs(rows, width, ff, chunk)
    row = whole((1, width))
    full = whole((rows, width))
    return pl.pallas_call(
        feed_backward,
        grid=(ff // chunk,),
        in_specs=[full, full, wide, wide, row, row, s1, s2],
        out_specs=[full, s1, s2, sb, whole((8, width))],
        out_shape=[
            sds((rows, width), F32),
            sds((width, ff), F32),
            sds((ff, width), F32),
            sds((1, ff), F32),
            sds((8, width), F32),
        ],
        scratch_shapes=[pltpu.VMEM((rows, width), BF), pltpu.VMEM((rows, width), F32)],
        compiler_params=params(),
        name="feed_backward_enc",
    )(mid, g, act, slope, fg, fsh, w1, w2)


def shards(
    tokens,
    centres,
    visible,
    lengths,
    cotangent,
    attend_gain,
    attend_shift,
    joint_weight,
    output_weight,
    output_bias,
    feed_gain,
    feed_shift,
    expand_weight,
    expand_bias,
    reduce_weight,
    reduce_bias,
    place_weight,
    place_bias,
    embed_weight,
    mask_token,
):
    phase = lax.axis_index("pipe")
    encoding = phase == 0
    micro, rows, width = tokens.shape
    half = micro // 2
    swap = [(0, 1), (1, 0)]
    own = [
        attend_gain, attend_shift, joint_weight[0], output_weight[0], output_bias, feed_gain, feed_shift,
        expand_weight[0], expand_bias, reduce_weight[0], reduce_bias, place_weight[0], place_bias, embed_weight[0],
    ]
    other = [lax.ppermute(piece, "pipe", swap) for piece in own]
    enc = [jnp.where(encoding, mine, theirs) for mine, theirs in zip(own, other)]
    dec = [jnp.where(encoding, theirs, mine) for mine, theirs in zip(own, other)]
    sel = jnp.reshape(phase * half, (1,)).astype(jnp.int32)
    mask_row = mask_token[None, :]
    given = lax.dynamic_slice_in_dim(cotangent, phase * half, half, 0).reshape(half * rows, width)

    def forward_weights(w):
        return [w[0], w[1], w[2], w[3], w[4], w[11], w[12], w[13]]

    def backward_weights(w):
        return [w[0], w[1], w[2], w[3], w[11], w[12], w[13]]

    ex, ej, ee, ei, em, emid = call_attend_forward(
        False, half, sel, lengths, tokens, centres, visible, mask_row, forward_weights(enc)
    )
    emid2 = emid.reshape(half * rows, width)
    enc_out, act, slope = call_feed_forward(emid2, enc[5], enc[6], enc[7], enc[8], enc[9], enc[10])
    enc_out = enc_out.reshape(half, rows, width)
    dx_, dj, de, di, dm, dmid = call_attend_forward(
        True, half, sel, lengths, enc_out, centres, visible, mask_row, forward_weights(dec)
    )
    dec_out, dback, d_w1, d_w2, d_b1, d_small = call_feed_both(
        dmid.reshape(half * rows, width), given, dec[5], dec[6], dec[7], dec[8], dec[9], dec[10]
    )
    ddx, enc_back, d_joint, d_output, d_embed, d_small2 = call_attend_backward(
        True, half, sel, lengths, dback.reshape(half, rows, width), dx_, centres, visible, dj, de, di, dm,
        backward_weights(dec),
    )
    eback, e_w1, e_w2, e_b1, e_small = call_feed_backward(
        emid2, enc_back.reshape(half * rows, width), act, slope, enc[5], enc[6], enc[7], enc[9]
    )
    edx, _, e_joint, e_output, e_embed, e_small2 = call_attend_backward(
        False, half, sel, lengths, eback.reshape(half, rows, width), ex, centres, visible, ej, ee, ei, em,
        backward_weights(enc),
    )

    def grads(joint, output, embed, w1, b1, w2, small, small2):
        hidden = place_weight.shape[2]
        return [
            small2[0], small2[1], joint, output, small2[2], small[0], small[1], w1, b1[0], w2, small[2],
            small2[4:7, :hidden], small2[7, :hidden], embed,
        ]

    g_enc = grads(e_joint, e_output, e_embed, e_w1, e_b1, e_w2, e_small, e_small2)
    g_dec = grads(d_joint, d_output, d_embed, d_w1, d_b1, d_w2, d_small, d_small2)
    mine = [jnp.where(encoding, a, b) for a, b in zip(g_enc, g_dec)]
    sent = [jnp.where(encoding, b, a) for a, b in zip(g_enc, g_dec)]
    came = [lax.ppermute(piece, "pipe", swap) for piece in sent]
    summed = list(lax.psum(tuple(a + b for a, b in zip(mine, came)), "dp"))
    mask_grad = lax.psum(d_small2[3], ("pipe", "dp"))

    def joined(enc_part, dec_part):
        got = lax.ppermute(jnp.where(encoding, dec_part, enc_part), "pipe", swap)
        first = jnp.where(encoding, enc_part, got)
        second = jnp.where(encoding, got, dec_part)
        return jnp.concatenate([first, second], 0)[None]

    phase_out = joined(enc_out, dec_out.reshape(half, rows, width))
    phase_in_grad = joined(edx, ddx)
    return tuple([phase_out, phase_in_grad] + [piece[None] for piece in summed] + [mask_grad])


def solution(mesh):
    in_specs = (
        P(None, "dp", None),
        P(None, None, "dp"),
        P(None, "dp"),
        P(None, "dp"),
        P(None, "dp", None),
        P("pipe", None),
        P("pipe", None),
        P("pipe", None, None),
        P("pipe", None, None),
        P("pipe", None),
        P("pipe", None),
        P("pipe", None),
        P("pipe", None, None),
        P("pipe", None),
        P("pipe", None, None),
        P("pipe", None),
        P("pipe", None, None),
        P("pipe", None),
        P("pipe", None, None),
        P(),
    )
    out_specs = (
        P("pipe", None, "dp", None),
        P("pipe", None, "dp", None),
        P("pipe", None),
        P("pipe", None),
        P("pipe", None, None),
        P("pipe", None, None),
        P("pipe", None),
        P("pipe", None),
        P("pipe", None),
        P("pipe", None, None),
        P("pipe", None),
        P("pipe", None, None),
        P("pipe", None),
        P("pipe", None, None),
        P("pipe", None),
        P("pipe", None, None),
        P(),
    )
    return jax.shard_map(shards, mesh=mesh, in_specs=in_specs, out_specs=out_specs, check_vma=False)
```

```python
import math

import jax
import jax.numpy as jnp
from jax import lax
from jax.experimental import pallas as pl
from jax.experimental.pallas import tpu as pltpu
from jax.sharding import PartitionSpec as P

HEADS = 6
NEG_FILL = -1e30
NORM_EPS = 1e-05
GELU_A = math.sqrt(2.0 / math.pi)
GELU_B = GELU_A * 0.044715
BF = jnp.bfloat16
F32 = jnp.float32
VMEM_LIMIT = 16 * 2**20


def dot(a, b):
    return jnp.dot(a, b, preferred_element_type=F32)


def dot_rt(a, b):
    return lax.dot_general(a, b, (((1,), (1,)), ((), ())), preferred_element_type=F32)


def dot_lt(a, b):
    return lax.dot_general(a, b, (((0,), (0,)), ((), ())), preferred_element_type=F32)


def gelu_both(v):
    v2 = v * v
    h = 0.5 * jnp.tanh(v * (GELU_A + GELU_B * v2)) + 0.5
    slope = h + (h - h * h) * (v * (2.0 * GELU_A + 6.0 * GELU_B * v2))
    return v * h, slope


def gelu_only(v):
    return v * (0.5 * jnp.tanh(v * (GELU_A + GELU_B * (v * v))) + 0.5)


def norm_parts(x):
    scale = 1.0 / x.shape[-1]
    centred = x - jnp.sum(x, -1, keepdims=True) * scale
    var = jnp.sum(centred * centred, -1, keepdims=True) * scale
    inverse = lax.rsqrt(var + NORM_EPS)
    return centred * inverse, inverse


def norm_back(u, z, inverse, gain):
    scale = 1.0 / u.shape[-1]
    w = u * gain
    m1 = jnp.sum(w, -1, keepdims=True) * scale
    m2 = jnp.sum(w * z, -1, keepdims=True) * scale
    return inverse * (w - m1 - z * m2)


def place_pre(centre, place_weight, place_bias):
    pre = lax.dot_general(
        centre,
        place_weight,
        (((0,), (0,)), ((), ())),
        precision=lax.Precision.HIGHEST,
        preferred_element_type=F32,
    )
    return pre + place_bias


def column_of(row, width):
    rows = lax.broadcasted_iota(jnp.int32, (16, row.shape[1]), 0)
    top = jnp.where(rows == 0, jnp.broadcast_to(row, rows.shape), 0).astype(F32)
    return dot_lt(top.astype(BF), jnp.ones((16, width), BF))


def segments(lengths, micro_index, slots, places):
    total = jnp.int32(0)
    seg = jnp.zeros(places.shape, jnp.int32)
    for slot in range(slots):
        total = total + lengths[micro_index, slot]
        seg = seg + (places >= total).astype(jnp.int32)
    return seg


def lane_low(shape, half):
    return lax.broadcasted_iota(jnp.int32, shape, 1) < half


SMALL = ("attend_gain", "attend_shift", "output_bias", "feed_gain", "feed_shift", "reduce_bias")


def small_row(values, name):
    place = SMALL.index(name)
    return values[place : place + 1, :]


def place_rows(values, hidden):
    return values[8:11, :hidden], values[11:12, :hidden]


def expand_row(values, width, ff):
    return [values[12 + part : 13 + part, :] for part in range(ff // width)]


def chosen(mine, own, other):
    return jnp.where(mine, own[...], other[...])


def attend_forward(decoding, rows, core, lengths, *refs):
    (x_in, centres, visible, mask_token, small_own, small_other, wj_own, wj_other) = refs[:8]
    (wo_own, wo_other, we_own, we_other) = refs[8:12]
    (x_out, joint_out, e_out, inv_out, mixed_out, mid_out, bias) = refs[12:]
    total, width = x_in.shape
    half = total // rows
    slots = lengths.shape[1]
    head = width // HEADS
    pair = 2 * head
    mine = core[0] == int(decoding)
    small = chosen(mine, small_own, small_other)
    ag, ash, bo = (small_row(small, name) for name in SMALL[:3])
    we = chosen(mine, we_own, we_other)
    pw, pb = place_rows(small, we.shape[0])

    for block in range(half):
        span = slice(block * rows, (block + 1) * rows)
        micro_index = core[0] * half + block
        embed = dot(gelu_only(place_pre(centres[micro_index], pw, pb)).astype(BF), we)
        seen = visible[pl.ds(micro_index, 1), :]
        source = x_in[span, :].astype(F32)
        if decoding:
            shown = column_of(seen, 128)[:, :1] > 0.5
            source = jnp.where(shown, source, mask_token[...])
        x_out[span, :] = source + embed
        places_k = lax.broadcasted_iota(jnp.int32, (1, rows), 1)
        seg_k = segments(lengths, micro_index, slots, places_k)
        allowed = column_of(seg_k, 128)[:, :1].astype(jnp.int32) == seg_k
        if not decoding:
            places_q = lax.broadcasted_iota(jnp.int32, (rows, rows), 0)
            places_kk = lax.broadcasted_iota(jnp.int32, (rows, rows), 1)
            allowed = allowed & ((seen > 0) | (places_q == places_kk))
        bias[block] = jnp.where(allowed, 0.0, NEG_FILL)

    z, _ = norm_parts(x_out[...])
    joint_out[...] = dot((z * ag + ash).astype(BF), chosen(mine, wj_own, wj_other)).astype(BF)

    low_k = lane_low((rows, pair), head)
    for block in range(half):
        span = slice(block * rows, (block + 1) * rows)
        for p in range(HEADS // 2):
            cols = slice(p * pair, (p + 1) * pair)
            qp = joint_out[span, cols] * BF(head**-0.5)
            kp = joint_out[span, width + p * pair : width + (p + 1) * pair]
            vp = joint_out[span, 2 * width + p * pair : 2 * width + (p + 1) * pair]
            out = []
            for side in range(2):
                mine_k = low_k == (side == 0)
                s = dot_rt(jnp.where(mine_k, qp, BF(0)), kp) + bias[block]
                e = jnp.exp(s - jnp.max(s, -1, keepdims=True)).astype(BF)
                e_out[block * HEADS + 2 * p + side] = e
                out.append(dot(e, jnp.where(mine_k, vp, BF(1))))
            inv = 1.0 / pltpu.roll(jnp.where(low_k, out[1], out[0]), head, 1)
            inv_out[span, cols] = inv
            mixed_out[span, cols] = (jnp.where(low_k, out[0], out[1]) * inv).astype(BF)
    wo = chosen(mine, wo_own, wo_other)
    mid_out[...] = x_out[...] + (dot(mixed_out[...], wo) + bo)


def pack_plan(width, hidden, half_rows):
    plan = ([], [])
    place = 0
    for which, (rows, columns) in enumerate(((width, 3 * width), (width, width), (hidden, width), (16, width))):
        for column in range(columns // 128):
            done = 0
            while done < rows:
                half, at = divmod(place, half_rows)
                count = min(rows - done, half_rows - at)
                plan[half].append((which, column, done, count, at))
                done += count
                place += count
    return plan


def packed_half_rows(width, hidden, unit):
    total = (3 * width * width + width * width + hidden * width + 16 * width) // 128
    return -(-total // (2 * unit)) * unit


def attend_backward(decoding, rows, core, *refs):
    (dmid_in, x_in, centres, visible, joint_in, e_in, inv_in, mixed_in) = refs[:8]
    (small_own, small_other, wj_own, wj_other, wo_own, wo_other, we_own, we_other) = refs[8:16]
    (small_feed, extra) = refs[16:18]
    dx_out, send_back, keep_g, send_g, mask_g = refs[18:23]
    dl, mu, dj, ds, joint_g, output_g, embed_g, small_g = refs[23:]
    total, width = x_in.shape
    half = total // rows
    head = width // HEADS
    pair = 2 * head
    mine = core[0] == int(decoding)
    small = chosen(mine, small_own, small_other)
    ag, ash = (small_row(small, name) for name in SMALL[:2])
    we = chosen(mine, we_own, we_other)
    hidden = we.shape[0]
    pw, pb = place_rows(small, hidden)

    dm = dmid_in[...].astype(BF)
    output_g[...] = dot_lt(mixed_in[...], dm)
    low_dl = (dot_rt(dm, chosen(mine, wo_own, wo_other)) * inv_in[...]).astype(BF)
    dl[...] = low_dl
    mu[...] = (low_dl.astype(F32) * -mixed_in[...].astype(F32)).astype(BF)
    small_g[...] = jnp.zeros(small_g.shape, F32)
    small_g[2:3, :] = jnp.sum(dm.astype(F32), 0, keepdims=True)

    low_k = lane_low((rows, pair), head)
    ones = jnp.ones((rows, pair), BF)
    for block in range(half):
        span = slice(block * rows, (block + 1) * rows)
        for p in range(HEADS // 2):
            cols = slice(p * pair, (p + 1) * pair)
            qp = joint_in[span, cols] * BF(head**-0.5)
            kp = joint_in[span, width + p * pair : width + (p + 1) * pair]
            vp = joint_in[span, 2 * width + p * pair : 2 * width + (p + 1) * pair]
            v_ext = jnp.concatenate([vp, ones], axis=1)
            dlp = dl[span, cols]
            mup = mu[span, cols]
            dq = dk = dv = None
            for side in range(2):
                mine_k = low_k == (side == 0)
                place = 2 * p + side
                d_one = jnp.where(mine_k, dlp, BF(0))
                u_one = jnp.where(mine_k, mup, BF(0))
                dp = dot_rt(jnp.concatenate([d_one, u_one], axis=1), v_ext)
                ds[place % 2] = (e_in[block * HEADS + place].astype(F32) * dp).astype(BF)
                q_one = jnp.where(mine_k, qp, BF(0))
                k_one = jnp.where(mine_k, kp, BF(0))
                dv_one = dot_lt(e_in[block * HEADS + place], d_one)
                dk_one = dot_lt(ds[place % 2], q_one)
                dq_one = dot(ds[place % 2], k_one)
                dv = dv_one if dv is None else dv + dv_one
                dk = dk_one if dk is None else dk + dk_one
                dq = dq_one if dq is None else dq + dq_one
            dj[span, cols] = (dq * head**-0.5).astype(BF)
            dj[span, width + p * pair : width + (p + 1) * pair] = dk.astype(BF)
            dj[span, 2 * width + p * pair : 2 * width + (p + 1) * pair] = dv.astype(BF)

    z, inverse = norm_parts(x_in[...])
    joint_g[...] = dot_lt((z * ag + ash).astype(BF), dj[...])
    dn = dot_rt(dj[...], chosen(mine, wj_own, wj_other))
    small_g[0:1, :] = jnp.sum(dn * z, 0, keepdims=True)
    small_g[1:2, :] = jnp.sum(dn, 0, keepdims=True)
    dx = dmid_in[...] + norm_back(dn, z, inverse, ag)
    dx_out[...] = dx
    ge = dx.astype(BF)
    acts = []
    for block in range(half):
        span = slice(block * rows, (block + 1) * rows)
        micro_index = core[0] * half + block
        if decoding:
            shown = column_of(visible[pl.ds(micro_index, 1), :], 128)[:, :1] > 0.5
            send_back[span, :] = jnp.where(shown, dx[span], 0.0).astype(BF)
            small_g[3:4, :] += jnp.sum(jnp.where(shown, 0.0, dx[span]), 0, keepdims=True)
        act, slope = gelu_both(place_pre(centres[micro_index], pw, pb))
        acts.append(act.astype(BF))
        dpre = slope * dot_rt(ge[span], we)
        place = jnp.dot(centres[micro_index], dpre, precision=lax.Precision.HIGHEST, preferred_element_type=F32)
        small_g[4:7, 0:hidden] += place
        small_g[7:8, 0:hidden] += jnp.sum(dpre, 0, keepdims=True)
    embed_g[...] = dot_lt(jnp.concatenate(acts, axis=0), ge)

    mask_g[...] = small_g[3:4, :]
    if not decoding:
        small_g[3:4, :] = extra[...]
    small_g[8:15, :] = small_feed[0:7, :]
    sources = (joint_g, output_g, embed_g, small_g)
    for here, target in ((0, keep_g), (1, send_g)):
        for side in range(2):

            @pl.when((core[0] == side) == (here == 0))
            def _(side=side, target=target):
                for which, column, first, count, at in pack_plan(width, hidden, target.shape[0])[side]:
                    lanes = slice(column * 128, column * 128 + 128)
                    target[at : at + count, :] = sources[which][first : first + count, lanes].astype(BF)


def feed_start(mid_in, small, low):
    z, _ = norm_parts(mid_in[...])
    low[...] = (z * small_row(small, "feed_gain") + small_row(small, "feed_shift")).astype(BF)


def feed_bias(small, width, first, chunk):
    rows = [small[12 + part : 13 + part, :] for part in range(first // width, (first + chunk) // width)]
    return jnp.concatenate(rows, axis=1) if len(rows) > 1 else rows[0]


def row_blocks(total, rows):
    return [slice(first, first + rows) for first in range(0, total, rows)]


def feed_forward(chunk, rows, core, mid_in, *refs):
    small_own, small_other, w1_own, w1_other, w2_own, w2_other, out, act_out, slope_out, low, acc = refs
    total, width = mid_in.shape
    mine = core[0] == 0
    small = chosen(mine, small_own, small_other)
    feed_start(mid_in, small, low)
    acc[...] = mid_in[...] + small_row(small, "reduce_bias")
    for first in range(0, act_out.shape[1], chunk):
        cols = slice(first, first + chunk)
        w1 = jnp.where(mine, w1_own[:, cols], w1_other[:, cols])
        w2 = jnp.where(mine, w2_own[cols, :], w2_other[cols, :])
        bias = feed_bias(small, width, first, chunk)
        for span in row_blocks(total, rows):
            act, slope = gelu_both(dot(low[span, :], w1) + bias)
            act_low = act.astype(BF)
            act_out[span, cols] = act_low
            slope_out[span, cols] = slope.astype(BF)
            acc[span, :] += dot(act_low, w2)
    out[...] = acc[...].astype(BF)


def feed_weight_grads(cols, low, act_low, dh, g, outs, small_g):
    width = g.shape[1]
    w1_g = dot_lt(low, dh).astype(BF)
    w2_g = dot_lt(act_low, g).astype(BF)
    for here, w1_to, w2_to in outs:

        @pl.when(here)
        def _(w1_to=w1_to, w2_to=w2_to):
            for first in range(0, cols.stop - cols.start, width):
                w1_to[cols.start + first : cols.start + first + width, :] = w1_g[:, first : first + width]
            w2_to[cols, :] = w2_g

    column_sum = jnp.sum(dh.astype(F32), 0, keepdims=True)
    for first in range(0, cols.stop - cols.start, width):
        row = 3 + (cols.start + first) // width
        small_g[row : row + 1, :] = column_sum[:, first : first + width]


def feed_tail(g_in, dn_acc, mid_in, small, dmid_out, small_g, rows):
    total = mid_in.shape[0]
    sums = None
    for span in row_blocks(total, rows):
        z, inverse = norm_parts(mid_in[span, :])
        g = g_in[span, :].astype(F32)
        dn = dn_acc[span, :]
        dmid_out[span, :] = g + norm_back(dn, z, inverse, small_row(small, "feed_gain"))
        new = [jnp.sum(value, 0, keepdims=True) for value in (dn * z, dn, g)]
        sums = new if sums is None else [a + b for a, b in zip(sums, new)]
    for row, value in enumerate(sums):
        small_g[row : row + 1, :] = value


def feed_both(chunk, rows, core, mid_in, g_in, *refs):
    small_own, small_other, w1_own, w1_other, w2_own, w2_other = refs[:6]
    out, dmid_out, keep_g, send_g, small_g, low, acc, dn_acc, act_low, dh = refs[6:]
    outs = [(core[0] == 0, keep_g, send_g), (core[0] != 0, send_g, keep_g)]
    total, width = mid_in.shape
    ff = w1_own.shape[1]
    mine = core[0] == 1
    small = chosen(mine, small_own, small_other)
    feed_start(mid_in, small, low)
    acc[...] = mid_in[...] + small_row(small, "reduce_bias")
    for first in range(0, ff, chunk):
        cols = slice(first, first + chunk)
        w1 = jnp.where(mine, w1_own[:, cols], w1_other[:, cols])
        w2 = jnp.where(mine, w2_own[cols, :], w2_other[cols, :])
        bias = feed_bias(small, width, first, chunk)
        for span in row_blocks(total, rows):
            act, slope = gelu_both(dot(low[span, :], w1) + bias)
            act = act.astype(BF)
            act_low[span, :] = act
            acc[span, :] += dot(act, w2)
            dh_rows = (slope * dot_rt(g_in[span, :], w2)).astype(BF)
            dh[span, :] = dh_rows
            dn = dot_rt(dh_rows, w1)
            dn_acc[span, :] = dn if first == 0 else dn_acc[span, :] + dn
        feed_weight_grads(cols, low[...], act_low[...], dh[...], g_in[...], outs, small_g)
    out[...] = acc[...].astype(BF)
    feed_tail(g_in, dn_acc, mid_in, small, dmid_out, small_g, rows)


def feed_backward(chunk, rows, core, mid_in, g_in, act_in, slope_in, *refs):
    small_own, small_other, w1_own, w1_other, w2_own, w2_other = refs[:6]
    dmid_out, keep_g, send_g, small_g, low, dn_acc, dh = refs[6:]
    total, width = mid_in.shape
    ff = w1_own.shape[1]
    mine = core[0] == 0
    small = chosen(mine, small_own, small_other)
    feed_start(mid_in, small, low)
    outs = [(core[0] == 0, keep_g, send_g), (core[0] != 0, send_g, keep_g)]
    for first in range(0, ff, chunk):
        cols = slice(first, first + chunk)
        w1 = jnp.where(mine, w1_own[:, cols], w1_other[:, cols])
        w2 = jnp.where(mine, w2_own[cols, :], w2_other[cols, :])
        for span in row_blocks(total, rows):
            dh_rows = (slope_in[span, cols].astype(F32) * dot_rt(g_in[span, :], w2)).astype(BF)
            dh[span, :] = dh_rows
            dn = dot_rt(dh_rows, w1)
            dn_acc[span, :] = dn if first == 0 else dn_acc[span, :] + dn
        feed_weight_grads(cols, low[...], act_in[:, cols], dh[...], g_in[...], outs, small_g)
    feed_tail(g_in, dn_acc, mid_in, small, dmid_out, small_g, rows)


def params():
    return pltpu.CompilerParams(vmem_limit_bytes=VMEM_LIMIT)


def sds(shape, kind):
    return jax.ShapeDtypeStruct(shape, kind)


def scalar():
    return pl.BlockSpec(memory_space=pltpu.SMEM)


def cost(microseconds):
    return pl.CostEstimate(flops=int(microseconds * 1e9), bytes_accessed=2**20, transcendentals=0)


def anywhere():
    return pl.BlockSpec(memory_space=pl.ANY)


def anywhere():
    return pl.BlockSpec(memory_space=pl.ANY)


def vmem():
    return pl.BlockSpec(memory_space=pltpu.VMEM)


def kernel_call(body, scalars, arrays, outs, scratch, limit, time, name):
    return pl.pallas_call(
        body,
        in_specs=[scalar() for _ in scalars] + [vmem() for _ in arrays],
        out_specs=[vmem() for _ in outs],
        out_shape=[sds(shape, kind) for shape, kind in outs],
        scratch_shapes=[pltpu.VMEM(shape, kind) for shape, kind in scratch],
        compiler_params=pltpu.CompilerParams(vmem_limit_bytes=limit * 2**20),
        cost_estimate=cost(time),
        name=name,
    )(*scalars, *arrays)


LIMITS = dict(af=16, ab=20, ff=16, fb=20, fw=16)


def call_attend_forward(decoding, rows, core, lengths, x_in, centres, visible, mask_token, weights):
    total, width = x_in.shape
    half = total // rows
    return kernel_call(
        lambda *refs: attend_forward(decoding, rows, *refs),
        [core, lengths],
        [x_in, centres, visible, mask_token, *weights],
        [
            ((total, width), F32),
            ((total, 3 * width), BF),
            ((half * HEADS, rows, rows), BF),
            ((total, width), F32),
            ((total, width), BF),
            ((total, width), F32),
        ],
        [((half, rows, rows), F32)],
        LIMITS["af"],
        9,
        "attend_forward_dec" if decoding else "attend_forward_enc",
    )


def call_attend_backward(decoding, rows, core, dmid, x, centres, visible, joint, e, inv, mixed, weights, small_feed, extra, unit):
    total, width = x.shape
    hidden = weights[6].shape[0]
    packed = (packed_half_rows(width, hidden, unit), 128)
    return kernel_call(
        lambda *refs: attend_backward(decoding, rows, *refs),
        [core],
        [dmid, x, centres, visible, joint, e, inv, mixed, *weights, small_feed, extra],
        [((total, width), F32), ((total, width) if decoding else (16, width), BF), (packed, BF), (packed, BF), ((1, width), F32)],
        [
            ((total, width), BF),
            ((total, width), BF),
            ((total, 3 * width), BF),
            ((2, rows, rows), BF),
            ((width, 3 * width), F32),
            ((width, width), F32),
            ((hidden, width), F32),
            ((16, width), F32),
        ],
        LIMITS["ab"],
        15,
        "attend_backward_dec" if decoding else "attend_backward_enc",
    )


def call_feed_forward(core, mid, weights, chunk=768, rows=512):
    total, width = mid.shape
    ff = weights[2].shape[1]
    return kernel_call(
        lambda *refs: feed_forward(chunk, rows, *refs),
        [core],
        [mid, *weights],
        [((total, width), BF), ((total, ff), BF), ((total, ff), BF)],
        [((total, width), BF), ((total, width), F32)],
        LIMITS["ff"],
        7,
        "feed_forward_enc",
    )


def call_feed_both(core, mid, g, weights, chunk=768, rows=512):
    total, width = mid.shape
    ff = weights[2].shape[1]
    return kernel_call(
        lambda *refs: feed_both(chunk, rows, *refs),
        [core],
        [mid, g, *weights],
        [((total, width), BF), ((total, width), F32), ((ff, width), BF), ((ff, width), BF), ((8, width), F32)],
        [((total, width), BF), ((total, width), F32), ((total, width), F32), ((total, chunk), BF), ((total, chunk), BF)],
        LIMITS["fb"],
        14,
        "feed_both_dec",
    )


def call_feed_backward(core, mid, g, act, slope, weights, chunk=768, rows=512):
    total, width = mid.shape
    ff = weights[2].shape[1]
    return kernel_call(
        lambda *refs: feed_backward(chunk, rows, *refs),
        [core],
        [mid, g, act, slope, *weights],
        [((total, width), F32), ((ff, width), BF), ((ff, width), BF), ((8, width), F32)],
        [((total, width), BF), ((total, width), F32), ((total, chunk), BF)],
        LIMITS["fw"],
        9,
        "feed_backward_enc",
    )


def at_rows(start, count):
    return pl.ds(pl.multiple_of(start * count, 16), count)


def add_all(parts):
    total = parts[0].astype(F32)
    for part in parts[1:]:
        total = total + part.astype(F32)
    return total.astype(BF)


def first_split(side, count, sources, digit, *refs):
    outs = refs[2 * sources :][-side:]
    pairs = [refs[2 * n : 2 * n + 2] for n in range(sources)]
    for t in range(side):
        base = lax.bitwise_xor(digit[0], t) * (count // side)
        at = 0
        for i in range(count // side):
            for pair in pairs:
                n = pair[0].shape[0] // count
                for column in range(pair[0].shape[1] // 128):
                    lanes = slice(column * 128, column * 128 + 128)
                    outs[t][at : at + n, :] = add_all([ref[at_rows(base + i, n), lanes] for ref in pair])
                    at += n


def next_split(terms, side, digit, *refs):
    outs = refs[-side:]
    n = outs[0].shape[0]
    for t in range(side):
        rows = at_rows(lax.bitwise_xor(digit[0], t), n)
        outs[t][...] = add_all([ref[rows, :] for ref in refs[:terms]])


def last_sum(terms, *refs):
    refs[-1][...] = add_all([ref[...] for ref in refs[:terms]])


def join(side, digit, *refs):
    out = refs[-1]
    n = refs[0].shape[0]
    for t in range(side):
        out[at_rows(lax.bitwise_xor(digit[0], t), n), :] = refs[t][...]


def last_join(side, count, digit, core, *refs):
    mine, send = refs[-2:]
    n = mine.shape[0] // count
    for t in range(side):
        base = lax.bitwise_xor(digit[0], t) * (count // side)
        for i in range(count // side):
            rows = at_rows(base + i, n)
            mine[rows, :] = refs[t][at_rows(2 * i + 1 - core[0], n), :]
            send[rows, :] = refs[t][at_rows(2 * i + core[0], n), :]


def small_call(body, scalars, arrays, after, outs, name):
    return pl.pallas_call(
        body,
        in_specs=[scalar() for _ in scalars] + [vmem() for _ in arrays] + [anywhere() for _ in after],
        out_specs=[vmem() for _ in outs],
        out_shape=[sds(shape, BF) for shape in outs],
        compiler_params=params(),
        cost_estimate=cost(1),
        name=name,
    )(*scalars, *arrays, *after)


def exchange_route(count, first, second):
    return [(i, i ^ first) for i in range(count)] + [(count + i, count + (i ^ second)) for i in range(count)]


def piece_count(count):
    side = math.isqrt(count)
    return count if side * side == count and side & (side - 1) == 0 else 1


class Reduction:
    def __init__(self, phase, core, alternate):
        self.pairs = []
        count = lax.axis_size("dp")
        self.pieces = piece_count(count)
        self.side = side = math.isqrt(self.pieces)
        self.core = core
        place = lax.axis_index("dp")
        low, high = place % side, place // side
        swapped = (phase == 1) & alternate
        self.digits = [jnp.where(swapped, b, a).reshape(1).astype(jnp.int32) for a, b in ((low, high), (high, low))]
        near, far = range(1, side), range(side, side * side, side)
        self.routes = [
            [exchange_route(count, k, other) for k, other in zip(near, far if alternate else near)],
            [exchange_route(count, k, other) for k, other in zip(far, near if alternate else far)],
        ]

    def start(self, keep, send):
        self.pairs.append((keep, lax.ppermute(send, "pipe", [(0, 1), (1, 0)])))

    def trade(self, which, sends):
        return [lax.ppermute(send, ("pipe", "dp"), route) for send, route in zip(sends, self.routes[which])]

    def split_first(self, after):
        arrays = [ref for pair in self.pairs for ref in pair]
        rows = sum(a.shape[0] * a.shape[1] // 128 for a, _ in self.pairs)
        side, sources, pieces = self.side, len(self.pairs), self.pieces
        outs = small_call(
            lambda *refs: first_split(side, pieces, sources, *refs),
            [self.digits[0]], arrays, after, [(rows // side, 128)] * side, "first_split",
        )
        if pieces == 1:
            outs = [lax.psum(outs[0].astype(F32), "dp").astype(BF)]
        self.got = [outs[0]] + self.trade(0, outs[1:])
        return [outs[0]]

    def split_second(self, after):
        side, terms = self.side, len(self.got)
        shape = (self.got[0].shape[0] // side, 128)
        outs = small_call(
            lambda *refs: next_split(terms, side, *refs), [self.digits[1]], self.got, after, [shape] * side, "next_split"
        )
        self.got = [outs[0]] + self.trade(1, outs[1:])
        return [outs[0]]

    def sum_last(self, after):
        terms = len(self.got)
        (piece,) = small_call(lambda *refs: last_sum(terms, *refs), [], self.got, after, [self.got[0].shape], "last_sum")
        self.got = [piece] + self.trade(1, [piece] * (self.side - 1))
        return [piece]

    def join_first(self, after):
        side = self.side
        shape = (self.got[0].shape[0] * side, 128)
        (block,) = small_call(lambda *refs: join(side, *refs), [self.digits[1]], self.got, after, [shape], "join")
        self.got = [block] + self.trade(0, [block] * (side - 1))
        return [block]

    def join_last(self, after):
        side, pieces = self.side, self.pieces
        shape = (self.got[0].shape[0] * side // 2, 128)
        mine, send = small_call(
            lambda *refs: last_join(side, pieces, *refs),
            [self.digits[0], self.core], self.got, after, [shape, shape], "last_join",
        )
        self.halves = [mine, lax.ppermute(send, "pipe", [(0, 1), (1, 0)])]
        return [mine]


def unpack_feed(count, core, own, got, w1_out, w2_out):
    ff, width = w2_out.shape[1], w2_out.shape[2]
    n = ff // count
    strips = width // 128

    def spread(first, second):
        for piece in range(count):
            for strip in range(strips):
                start = (piece * strips + strip) * n
                lanes = slice(strip * 128, strip * 128 + 128)
                w2_out[0, piece * n : piece * n + n, lanes] = second[start : start + n, :].astype(F32)
                done = 0
                while done < n:
                    block, inner = divmod(piece * n + done, width)
                    take = min(n - done, width - inner)
                    lanes = slice(block * width + strip * 128, block * width + strip * 128 + 128)
                    rows = slice(start + done, start + done + take)
                    w1_out[0, inner : inner + take, lanes] = first[rows, :].astype(F32)
                    done += take

    @pl.when(core[0] == 0)
    def _():
        spread(own, got)

    @pl.when(core[0] != 0)
    def _():
        spread(got, own)


def call_unpack_feed(core, halves, count, ff, width):
    return pl.pallas_call(
        lambda *refs: unpack_feed(count, *refs),
        in_specs=[scalar()] + [vmem()] * 2,
        out_specs=[vmem()] * 2,
        out_shape=[sds((1, width, ff), F32), sds((1, ff, width), F32)],
        compiler_params=params(),
        cost_estimate=cost(4),
        name="unpack_feed",
    )(core, *halves)


def unpack_attend(core, own, got, *outs):
    (joint_out, output_out, embed_out, place_out, place_bias_out, expand_bias_out, mask_out) = outs[:7]
    rows_out, small = outs[7:13], outs[13]
    width, hidden = output_out.shape[1], embed_out.shape[1]
    plan = pack_plan(width, hidden, own.shape[0])
    targets = (joint_out.at[0], output_out.at[0], embed_out.at[0], small)

    def spread(halves):
        for half in range(2):
            for which, column, first, rows, at in plan[half]:
                lanes = slice(column * 128, column * 128 + 128)
                targets[which][first : first + rows, lanes] = halves[half][at : at + rows, :].astype(F32)

    @pl.when(core[0] == 0)
    def _():
        spread((own, got))

    @pl.when(core[0] != 0)
    def _():
        spread((got, own))

    for out, row in zip(rows_out, (0, 1, 2, 8, 9, 10)):
        out[...] = small[row : row + 1, :]
    mask_out[...] = small[3:4, :]
    place_out[0] = small[4:7, 0:hidden]
    place_bias_out[...] = small[7:8, 0:hidden]
    for part in range(expand_bias_out.shape[1] // width):
        expand_bias_out[:, part * width : (part + 1) * width] = small[11 + part : 12 + part, :]


def call_unpack_attend(core, halves, width, hidden, ff):
    shapes = [(1, width, 3 * width), (1, width, width), (1, hidden, width), (1, 3, hidden), (1, hidden), (1, ff), (1, width)]
    shapes += [(1, width)] * 6
    return pl.pallas_call(
        unpack_attend,
        in_specs=[scalar()] + [vmem()] * 2,
        out_specs=[vmem()] * len(shapes),
        out_shape=[sds(shape, F32) for shape in shapes],
        scratch_shapes=[pltpu.VMEM((16, width), F32)],
        compiler_params=params(),
        cost_estimate=cost(3),
        name="unpack_attend",
    )(core, *halves)


def shards(
    tokens,
    centres,
    visible,
    lengths,
    cotangent,
    attend_gain,
    attend_shift,
    joint_weight,
    output_weight,
    output_bias,
    feed_gain,
    feed_shift,
    expand_weight,
    expand_bias,
    reduce_weight,
    reduce_bias,
    place_weight,
    place_bias,
    embed_weight,
    mask_token,
):
    phase = lax.axis_index("pipe")
    encoding = phase == 0
    micro, rows, width = tokens.shape
    half = micro // 2
    hidden = place_weight.shape[2]
    swap = [(0, 1), (1, 0)]
    core = jnp.reshape(phase, (1,)).astype(jnp.int32)
    no_mask = jnp.zeros((1, width), F32)
    mask_row = mask_token[None, :]
    flat = lambda a: a.reshape(half * rows, a.shape[-1])
    here = lambda a: flat(lax.dynamic_slice_in_dim(a, phase * half, half, 0))
    given = here(cotangent)

    wide = lambda piece: jnp.pad(piece, ((0, 0), (0, width - hidden)))
    small = jnp.concatenate(
        [attend_gain, attend_shift, output_bias, feed_gain, feed_shift, reduce_bias, jnp.zeros((2, width), F32)]
        + [wide(place_weight[0]), wide(place_bias), expand_bias.reshape(-1, width)]
    )
    own = [small, joint_weight[0], output_weight[0], embed_weight[0], expand_weight[0], reduce_weight[0]]
    other = [lax.ppermute(piece, "pipe", swap) for piece in own]
    both = [pair for mine in zip(own, other) for pair in mine]
    attend_weights = both[:8]
    feed_weights_both = both[:2] + both[8:]

    count = piece_count(lax.axis_size("dp"))
    unit = 16 * count
    ff = expand_weight.shape[2]

    ex, ej, ee, ei, em, emid = call_attend_forward(
        False, rows, core, lengths, here(tokens), centres, visible, mask_row, attend_weights
    )
    enc_out, act, slope = call_feed_forward(core, emid, feed_weights_both)
    dx, dj, de, di, dm, dmid = call_attend_forward(
        True, rows, core, lengths, enc_out, centres, visible, mask_row, attend_weights
    )
    dec_out, dback, d_keep, d_send, d_small = call_feed_both(core, dmid, given, feed_weights_both)
    feed = Reduction(phase, core, False)
    attend = Reduction(phase, core, True)
    feed.start(d_keep, d_send)
    ddx, enc_back, d_keep, d_send, d_mask = call_attend_backward(
        True, rows, core, dback, dx, centres, visible, dj, de, di, dm, attend_weights, d_small, no_mask, unit
    )
    attend.start(d_keep, d_send)
    eback, e_keep, e_send, e_small = call_feed_backward(core, emid, enc_back, act, slope, feed_weights_both)
    feed.start(e_keep, e_send)
    edx, _, e_keep, e_send, _ = call_attend_backward(
        False, rows, core, eback, ex, centres, visible, ej, ee, ei, em, attend_weights, e_small, d_mask, unit
    )
    attend.start(e_keep, e_send)

    after = feed.split_first([edx])
    after = attend.split_first(after)
    after = feed.split_second(after)
    after = attend.split_second(after)
    after = feed.sum_last(after)
    after = attend.sum_last(after)
    after = feed.join_first(after)
    after = attend.join_first(after)
    after = feed.join_last(after)
    after = attend.join_last(after)

    w1_grad, w2_grad = call_unpack_feed(core, feed.halves, count, ff, width)
    (joint_grad, output_grad, embed_grad, place_grad, place_bias_grad, expand_bias_grad, mask_grad, *vectors) = (
        call_unpack_attend(core, attend.halves, width, hidden, ff)
    )

    def joined(enc_part, dec_part):
        got = lax.ppermute(jnp.where(encoding, dec_part, enc_part), "pipe", swap)
        front = jnp.where(encoding, enc_part, got)
        second = jnp.where(encoding, got, dec_part)
        return jnp.concatenate([front, second], 0).reshape(1, micro, rows, width)

    phase_out = joined(enc_out, dec_out)
    phase_in_grad = joined(edx, ddx)
    attend_gain_grad, attend_shift_grad, output_bias_grad, feed_gain_grad, feed_shift_grad, reduce_bias_grad = vectors
    return (
        phase_out, phase_in_grad, attend_gain_grad, attend_shift_grad, joint_grad, output_grad, output_bias_grad,
        feed_gain_grad, feed_shift_grad, w1_grad, expand_bias_grad, w2_grad, reduce_bias_grad, place_grad,
        place_bias_grad, embed_grad, mask_grad.reshape(width),
    )


def solution(mesh):
    in_specs = (
        P(None, "dp", None),
        P(None, None, "dp"),
        P(None, "dp"),
        P(None, "dp"),
        P(None, "dp", None),
        P("pipe", None),
        P("pipe", None),
        P("pipe", None, None),
        P("pipe", None, None),
        P("pipe", None),
        P("pipe", None),
        P("pipe", None),
        P("pipe", None, None),
        P("pipe", None),
        P("pipe", None, None),
        P("pipe", None),
        P("pipe", None, None),
        P("pipe", None),
        P("pipe", None, None),
        P(),
    )
    out_specs = (
        P("pipe", None, "dp", None),
        P("pipe", None, "dp", None),
        P("pipe", None),
        P("pipe", None),
        P("pipe", None, None),
        P("pipe", None, None),
        P("pipe", None),
        P("pipe", None),
        P("pipe", None),
        P("pipe", None, None),
        P("pipe", None),
        P("pipe", None, None),
        P("pipe", None),
        P("pipe", None, None),
        P("pipe", None),
        P("pipe", None, None),
        P(),
    )
    return jax.shard_map(shards, mesh=mesh, in_specs=in_specs, out_specs=out_specs, check_vma=False)
```

```python
import math

import jax
import jax.numpy as jnp
from jax import lax
from jax.experimental import pallas as pl
from jax.experimental.pallas import tpu as pltpu
from jax.sharding import PartitionSpec as P

HEADS = 6
NEG_FILL = -1e30
NORM_EPS = 1e-05
GELU_A = math.sqrt(2.0 / math.pi)
GELU_B = GELU_A * 0.044715
BF = jnp.bfloat16
F32 = jnp.float32
VMEM_LIMIT = 16 * 2**20


def dot(a, b):
    return jnp.dot(a, b, preferred_element_type=F32)


def dot_rt(a, b):
    return lax.dot_general(a, b, (((1,), (1,)), ((), ())), preferred_element_type=F32)


def dot_lt(a, b):
    return lax.dot_general(a, b, (((0,), (0,)), ((), ())), preferred_element_type=F32)


def gelu_both(v):
    v2 = v * v
    h = 0.5 * jnp.tanh(v * (GELU_A + GELU_B * v2)) + 0.5
    slope = h + (h - h * h) * (v * (2.0 * GELU_A + 6.0 * GELU_B * v2))
    return v * h, slope


def gelu_only(v):
    return v * (0.5 * jnp.tanh(v * (GELU_A + GELU_B * (v * v))) + 0.5)


def norm_parts(x):
    scale = 1.0 / x.shape[-1]
    centred = x - jnp.sum(x, -1, keepdims=True) * scale
    var = jnp.sum(centred * centred, -1, keepdims=True) * scale
    inverse = lax.rsqrt(var + NORM_EPS)
    return centred * inverse, inverse


def norm_back(u, z, inverse, gain):
    scale = 1.0 / u.shape[-1]
    w = u * gain
    m1 = jnp.sum(w, -1, keepdims=True) * scale
    m2 = jnp.sum(w * z, -1, keepdims=True) * scale
    return inverse * (w - m1 - z * m2)


def place_pre(centre, place_weight, place_bias):
    pre = lax.dot_general(
        centre,
        place_weight,
        (((0,), (0,)), ((), ())),
        precision=lax.Precision.HIGHEST,
        preferred_element_type=F32,
    )
    return pre + place_bias


def column_of(row, width):
    rows = lax.broadcasted_iota(jnp.int32, (16, row.shape[1]), 0)
    top = jnp.where(rows == 0, jnp.broadcast_to(row, rows.shape), 0).astype(F32)
    return dot_lt(top.astype(BF), jnp.ones((16, width), BF))


def segments(lengths, micro_index, slots, places):
    total = jnp.int32(0)
    seg = jnp.zeros(places.shape, jnp.int32)
    for slot in range(slots):
        total = total + lengths[micro_index, slot]
        seg = seg + (places >= total).astype(jnp.int32)
    return seg


def lane_low(shape, half):
    return lax.broadcasted_iota(jnp.int32, shape, 1) < half


SMALL = ("attend_gain", "attend_shift", "output_bias", "feed_gain", "feed_shift", "reduce_bias")


def small_row(values, name):
    place = SMALL.index(name)
    return values[place : place + 1, :]


def place_rows(values, hidden):
    return values[8:11, :hidden], values[11:12, :hidden]


def expand_row(values, width, ff):
    return [values[12 + part : 13 + part, :] for part in range(ff // width)]


def chosen(mine, own, other):
    return jnp.where(mine, own[...], other[...])


def attend_forward(decoding, rows, core, lengths, *refs):
    (x_in, centres, visible, mask_token, small_own, small_other, wj_own, wj_other) = refs[:8]
    (wo_own, wo_other, we_own, we_other) = refs[8:12]
    (x_out, joint_out, e_out, inv_out, mixed_out, mid_out, bias) = refs[12:]
    total, width = x_in.shape
    half = total // rows
    slots = lengths.shape[1]
    head = width // HEADS
    pair = 2 * head
    mine = core[0] == int(decoding)
    small = chosen(mine, small_own, small_other)
    ag, ash, bo = (small_row(small, name) for name in SMALL[:3])
    we = chosen(mine, we_own, we_other)
    pw, pb = place_rows(small, we.shape[0])

    for block in range(half):
        span = slice(block * rows, (block + 1) * rows)
        micro_index = core[0] * half + block
        embed = dot(gelu_only(place_pre(centres[micro_index], pw, pb)).astype(BF), we)
        seen = visible[pl.ds(micro_index, 1), :]
        source = x_in[span, :].astype(F32)
        if decoding:
            shown = column_of(seen, 128)[:, :1] > 0.5
            source = jnp.where(shown, source, mask_token[...])
        x_out[span, :] = source + embed
        places_k = lax.broadcasted_iota(jnp.int32, (1, rows), 1)
        seg_k = segments(lengths, micro_index, slots, places_k)
        allowed = column_of(seg_k, 128)[:, :1].astype(jnp.int32) == seg_k
        if not decoding:
            places_q = lax.broadcasted_iota(jnp.int32, (rows, rows), 0)
            places_kk = lax.broadcasted_iota(jnp.int32, (rows, rows), 1)
            allowed = allowed & ((seen > 0) | (places_q == places_kk))
        bias[block] = jnp.where(allowed, 0.0, NEG_FILL)

    z, _ = norm_parts(x_out[...])
    joint_out[...] = dot((z * ag + ash).astype(BF), chosen(mine, wj_own, wj_other)).astype(BF)

    low_k = lane_low((rows, pair), head)
    for block in range(half):
        span = slice(block * rows, (block + 1) * rows)
        for p in range(HEADS // 2):
            cols = slice(p * pair, (p + 1) * pair)
            qp = joint_out[span, cols] * BF(head**-0.5)
            kp = joint_out[span, width + p * pair : width + (p + 1) * pair]
            vp = joint_out[span, 2 * width + p * pair : 2 * width + (p + 1) * pair]
            out = []
            for side in range(2):
                mine_k = low_k == (side == 0)
                s = dot_rt(jnp.where(mine_k, qp, BF(0)), kp) + bias[block]
                e = jnp.exp(s - jnp.max(s, -1, keepdims=True)).astype(BF)
                e_out[block * HEADS + 2 * p + side] = e
                out.append(dot(e, jnp.where(mine_k, vp, BF(1))))
            inv = 1.0 / pltpu.roll(jnp.where(low_k, out[1], out[0]), head, 1)
            inv_out[span, cols] = inv.astype(BF)
            mixed_out[span, cols] = (jnp.where(low_k, out[0], out[1]) * inv).astype(BF)
    wo = chosen(mine, wo_own, wo_other)
    mid_out[...] = x_out[...] + (dot(mixed_out[...], wo) + bo)


def pack_plan(width, hidden, half_rows):
    plan = ([], [])
    place = 0
    for which, (rows, columns) in enumerate(((width, 3 * width), (width, width), (hidden, width), (16, width))):
        for column in range(columns // 128):
            done = 0
            while done < rows:
                half, at = divmod(place, half_rows)
                count = min(rows - done, half_rows - at)
                plan[half].append((which, column, done, count, at))
                done += count
                place += count
    return plan


def packed_half_rows(width, hidden, unit):
    total = (3 * width * width + width * width + hidden * width + 16 * width) // 128
    return -(-total // (2 * unit)) * unit


def attend_backward(decoding, rows, core, *refs):
    (dmid_in, x_in, centres, visible, joint_in, e_in, inv_in, mixed_in) = refs[:8]
    (small_own, small_other, wj_own, wj_other, wo_own, wo_other, we_own, we_other) = refs[8:16]
    (small_feed, extra) = refs[16:18]
    dx_out, send_back, mask_g, half0, half1, send_halves = refs[18:24]
    dl, mu, dj, ds, joint_g, output_g, embed_g, small_g = refs[24:]
    total, width = x_in.shape
    half = total // rows
    head = width // HEADS
    pair = 2 * head
    mine = core[0] == int(decoding)
    small = chosen(mine, small_own, small_other)
    ag, ash = (small_row(small, name) for name in SMALL[:2])
    we = chosen(mine, we_own, we_other)
    hidden = we.shape[0]
    pw, pb = place_rows(small, hidden)

    dm = dmid_in[...].astype(BF)
    output_g[...] = dot_lt(mixed_in[...], dm)
    low_dl = (dot_rt(dm, chosen(mine, wo_own, wo_other)) * inv_in[...].astype(F32)).astype(BF)
    dl[...] = low_dl
    mu[...] = (low_dl.astype(F32) * -mixed_in[...].astype(F32)).astype(BF)
    small_g[...] = jnp.zeros(small_g.shape, F32)
    small_g[2:3, :] = jnp.sum(dm.astype(F32), 0, keepdims=True)

    low_k = lane_low((rows, pair), head)
    ones = jnp.ones((rows, pair), BF)
    for block in range(half):
        span = slice(block * rows, (block + 1) * rows)
        for p in range(HEADS // 2):
            cols = slice(p * pair, (p + 1) * pair)
            qp = joint_in[span, cols] * BF(head**-0.5)
            kp = joint_in[span, width + p * pair : width + (p + 1) * pair]
            vp = joint_in[span, 2 * width + p * pair : 2 * width + (p + 1) * pair]
            v_ext = jnp.concatenate([vp, ones], axis=1)
            dlp = dl[span, cols]
            mup = mu[span, cols]
            dq = dk = dv = None
            for side in range(2):
                mine_k = low_k == (side == 0)
                place = 2 * p + side
                d_one = jnp.where(mine_k, dlp, BF(0))
                u_one = jnp.where(mine_k, mup, BF(0))
                dp = dot_rt(jnp.concatenate([d_one, u_one], axis=1), v_ext)
                ds[place % 2] = (e_in[block * HEADS + place].astype(F32) * dp).astype(BF)
                q_one = jnp.where(mine_k, qp, BF(0))
                k_one = jnp.where(mine_k, kp, BF(0))
                dv_one = dot_lt(e_in[block * HEADS + place], d_one)
                dk_one = dot_lt(ds[place % 2], q_one)
                dq_one = dot(ds[place % 2], k_one)
                dv = dv_one if dv is None else dv + dv_one
                dk = dk_one if dk is None else dk + dk_one
                dq = dq_one if dq is None else dq + dq_one
            dj[span, cols] = (dq * head**-0.5).astype(BF)
            dj[span, width + p * pair : width + (p + 1) * pair] = dk.astype(BF)
            dj[span, 2 * width + p * pair : 2 * width + (p + 1) * pair] = dv.astype(BF)

    z, inverse = norm_parts(x_in[...])
    joint_g[...] = dot_lt((z * ag + ash).astype(BF), dj[...])
    dn = dot_rt(dj[...], chosen(mine, wj_own, wj_other))
    small_g[0:1, :] = jnp.sum(dn * z, 0, keepdims=True)
    small_g[1:2, :] = jnp.sum(dn, 0, keepdims=True)
    dx = dmid_in[...] + norm_back(dn, z, inverse, ag)
    dx_out[...] = dx
    ge = dx.astype(BF)
    acts = []
    for block in range(half):
        span = slice(block * rows, (block + 1) * rows)
        micro_index = core[0] * half + block
        if decoding:
            shown = column_of(visible[pl.ds(micro_index, 1), :], 128)[:, :1] > 0.5
            send_back[span, :] = jnp.where(shown, dx[span], 0.0).astype(BF)
            small_g[3:4, :] += jnp.sum(jnp.where(shown, 0.0, dx[span]), 0, keepdims=True)
        act, slope = gelu_both(place_pre(centres[micro_index], pw, pb))
        acts.append(act.astype(BF))
        dpre = slope * dot_rt(ge[span], we)
        place = jnp.dot(centres[micro_index], dpre, precision=lax.Precision.HIGHEST, preferred_element_type=F32)
        small_g[4:7, 0:hidden] += place
        small_g[7:8, 0:hidden] += jnp.sum(dpre, 0, keepdims=True)
    embed_g[...] = dot_lt(jnp.concatenate(acts, axis=0), ge)

    mask_g[...] = small_g[3:4, :]
    if not decoding:
        small_g[3:4, :] = extra[...]
    small_g[8:15, :] = small_feed[0:7, :]
    sources = (joint_g, output_g, embed_g, small_g)
    for target, plan in zip((half0, half1), pack_plan(width, hidden, half0.shape[0])):
        for which, column, first, count, at in plan:
            lanes = slice(column * 128, column * 128 + 128)
            target[at : at + count, :] = sources[which][first : first + count, lanes].astype(BF)
    send_halves()


def feed_start(mid_in, small, low):
    z, _ = norm_parts(mid_in[...])
    low[...] = (z * small_row(small, "feed_gain") + small_row(small, "feed_shift")).astype(BF)


def feed_bias(small, width, first, chunk):
    rows = [small[12 + part : 13 + part, :] for part in range(first // width, (first + chunk) // width)]
    return jnp.concatenate(rows, axis=1) if len(rows) > 1 else rows[0]


def row_blocks(total, rows):
    return [slice(first, first + rows) for first in range(0, total, rows)]


def feed_forward(chunk, rows, core, mid_in, *refs):
    small_own, small_other, w1_own, w1_other, w2_own, w2_other, out, low, acc = refs
    total, width = mid_in.shape
    mine = core[0] == 0
    small = chosen(mine, small_own, small_other)
    feed_start(mid_in, small, low)
    acc[...] = mid_in[...] + small_row(small, "reduce_bias")
    for first in range(0, w1_own.shape[1], chunk):
        cols = slice(first, first + chunk)
        w1 = jnp.where(mine, w1_own[:, cols], w1_other[:, cols])
        w2 = jnp.where(mine, w2_own[cols, :], w2_other[cols, :])
        bias = feed_bias(small, width, first, chunk)
        for span in row_blocks(total, rows):
            acc[span, :] += dot(gelu_only(dot(low[span, :], w1) + bias).astype(BF), w2)
    out[...] = acc[...].astype(BF)


def feed_weight_grads(cols, low, act_low, dh, g, half0, half1, small_g):
    width = g.shape[1]
    ff = half0.shape[0] * 128 // width
    w1_g = dot_lt(low, dh).astype(BF)
    w2_g = dot_lt(act_low, g).astype(BF)
    for first in range(0, cols.stop - cols.start, 128):
        place = (cols.start + first) // 128 * width
        half0[place : place + width, :] = w1_g[:, first : first + 128]
    for first in range(0, width, 128):
        place = first // 128 * ff
        half1[place + cols.start : place + cols.stop, :] = w2_g[:, first : first + 128]
    column_sum = jnp.sum(dh.astype(F32), 0, keepdims=True)
    for first in range(0, cols.stop - cols.start, width):
        row = 3 + (cols.start + first) // width
        small_g[row : row + 1, :] = column_sum[:, first : first + width]


def feed_tail(g_in, dn_acc, mid_in, small, dmid_out, small_g, rows):
    total = mid_in.shape[0]
    sums = None
    for span in row_blocks(total, rows):
        z, inverse = norm_parts(mid_in[span, :])
        g = g_in[span, :].astype(F32)
        dn = dn_acc[span, :]
        dmid_out[span, :] = g + norm_back(dn, z, inverse, small_row(small, "feed_gain"))
        new = [jnp.sum(value, 0, keepdims=True) for value in (dn * z, dn, g)]
        sums = new if sums is None else [a + b for a, b in zip(sums, new)]
    for row, value in enumerate(sums):
        small_g[row : row + 1, :] = value


def feed_backward(block, chunk, rows, core, mid_in, g_in, *refs):
    small_own, small_other, w1_own, w1_other, w2_own, w2_other = refs[:6]
    refs = refs[6:]
    dmid_out, small_g = refs[:2]
    half0, half1, send_halves, low, dn_acc, act_low, dh = refs[2 + block : 9 + block]
    out, acc = (refs[2], dmid_out) if block else (None, None)
    total, width = mid_in.shape
    ff = w1_own.shape[1]
    mine = core[0] == block
    small = chosen(mine, small_own, small_other)
    feed_start(mid_in, small, low)
    if block:
        acc[...] = mid_in[...] + small_row(small, "reduce_bias")
    for first in range(0, ff, chunk):
        cols = slice(first, first + chunk)
        w1 = jnp.where(mine, w1_own[:, cols], w1_other[:, cols])
        w2 = jnp.where(mine, w2_own[cols, :], w2_other[cols, :])
        bias = feed_bias(small, width, first, chunk)
        for span in row_blocks(total, rows):
            act, slope = gelu_both(dot(low[span, :], w1) + bias)
            act = act.astype(BF)
            act_low[span, :] = act
            if block:
                acc[span, :] += dot(act, w2)
            dh_rows = (slope * dot_rt(g_in[span, :], w2)).astype(BF)
            dh[span, :] = dh_rows
            dn = dot_rt(dh_rows, w1)
            dn_acc[span, :] = dn if first == 0 else dn_acc[span, :] + dn
        feed_weight_grads(cols, low[...], act_low[...], dh[...], g_in[...], half0, half1, small_g)
    send_halves()
    if block:
        out[...] = acc[...].astype(BF)
    feed_tail(g_in, dn_acc, mid_in, small, dmid_out, small_g, rows)


def params():
    return pltpu.CompilerParams(vmem_limit_bytes=VMEM_LIMIT)


def sds(shape, kind):
    return jax.ShapeDtypeStruct(shape, kind)


def scalar():
    return pl.BlockSpec(memory_space=pltpu.SMEM)


def cost(microseconds):
    return pl.CostEstimate(flops=int(microseconds * 1e9), bytes_accessed=2**20, transcendentals=0)


def anywhere():
    return pl.BlockSpec(memory_space=pl.ANY)


def anywhere():
    return pl.BlockSpec(memory_space=pl.ANY)


def vmem():
    return pl.BlockSpec(memory_space=pltpu.VMEM)


def anywhere():
    return pl.BlockSpec(memory_space=pl.ANY)


def in_hbm():
    return pl.BlockSpec(memory_space=pltpu.HBM)


def kernel_call(body, scalars, arrays, outs, scratch, limit, time, name, shared):
    arrays = list(arrays)
    in_specs = [scalar() for _ in scalars] + [vmem() for _ in arrays]
    out_specs = [vmem() for _ in outs]
    out_shape = [sds(shape, kind) for shape, kind in outs]
    scratch_shapes = [pltpu.VMEM(shape, kind) for shape, kind in scratch]
    aliases = {}
    targets, first_row, rows = shared
    given = not isinstance(targets[0], tuple)
    if given:
        aliases = {len(in_specs) + n: len(out_specs) + n for n in range(2)}
        arrays += targets
        in_specs += [in_hbm()] * 2
    shapes = [target.shape if given else target for target in targets]
    out_specs += [in_hbm()] * 2
    out_shape += [pltpu.HBM(shape, BF) for shape in shapes]
    scratch_shapes += [pltpu.VMEM((rows, 128), BF)] * 2 + [pltpu.SemaphoreType.DMA((2,))]
    first = len(in_specs)

    def run(*refs):
        core = refs[0]
        ins = refs[: first - 2 * given]
        results = refs[first : first + len(outs)]
        keep, send = refs[first + len(outs) : first + len(outs) + 2]
        *held, half0, half1, sems = refs[first + len(outs) + 2 :]
        place = pl.ds(first_row, rows)

        def both(act):
            for n, pair in enumerate(((keep, send), (send, keep))):

                @pl.when(core[0] == n)
                def _(pair=pair):
                    for slot, half in enumerate((half0, half1)):
                        act(pltpu.make_async_copy(half, pair[slot].at[place, :], sems.at[slot]))

        body(*ins, *results, half0, half1, lambda: both(lambda copy: copy.start()), *held)
        both(lambda copy: copy.wait())

    return pl.pallas_call(
        run,
        in_specs=in_specs,
        out_specs=out_specs,
        out_shape=out_shape,
        scratch_shapes=scratch_shapes,
        input_output_aliases=aliases,
        compiler_params=pltpu.CompilerParams(vmem_limit_bytes=limit * 2**20),
        cost_estimate=cost(time),
        name=name,
    )(*scalars, *arrays)


def plain_call(body, scalars, arrays, outs, scratch, limit, time, name):
    return pl.pallas_call(
        body,
        in_specs=[scalar() for _ in scalars] + [vmem() for _ in arrays],
        out_specs=[vmem() for _ in outs],
        out_shape=[sds(shape, kind) for shape, kind in outs],
        scratch_shapes=[pltpu.VMEM(shape, kind) for shape, kind in scratch],
        compiler_params=pltpu.CompilerParams(vmem_limit_bytes=limit * 2**20),
        cost_estimate=cost(time),
        name=name,
    )(*scalars, *arrays)


LIMITS = dict(af=8, ab=13, ff=6, fb=15)


def call_attend_forward(decoding, rows, core, lengths, x_in, centres, visible, mask_token, weights):
    total, width = x_in.shape
    half = total // rows
    return plain_call(
        lambda *refs: attend_forward(decoding, rows, *refs),
        [core, lengths],
        [x_in, centres, visible, mask_token, *weights],
        [
            ((total, width), F32),
            ((total, 3 * width), BF),
            ((half * HEADS, rows, rows), BF),
            ((total, width), BF),
            ((total, width), BF),
            ((total, width), F32),
        ],
        [((half, rows, rows), F32)],
        LIMITS["af"],
        9,
        "attend_forward_dec" if decoding else "attend_forward_enc",
    )


def call_attend_backward(decoding, rows, core, dmid, x, centres, visible, joint, e, inv, mixed, weights, small_feed, extra, shared):
    total, width = x.shape
    hidden = weights[6].shape[0]
    return kernel_call(
        lambda *refs: attend_backward(decoding, rows, *refs),
        [core],
        [dmid, x, centres, visible, joint, e, inv, mixed, *weights, small_feed, extra],
        [((total, width), F32), ((total, width) if decoding else (16, width), BF), ((1, width), F32)],
        [
            ((total, width), BF),
            ((total, width), BF),
            ((total, 3 * width), BF),
            ((2, rows, rows), BF),
            ((width, 3 * width), F32),
            ((width, width), F32),
            ((hidden, width), F32),
            ((16, width), F32),
        ],
        LIMITS["ab"],
        15,
        "attend_backward_dec" if decoding else "attend_backward_enc",
        shared,
    )


def call_feed_forward(core, mid, weights, chunk=768, rows=256):
    total, width = mid.shape
    return plain_call(
        lambda *refs: feed_forward(chunk, rows, *refs),
        [core],
        [mid, *weights],
        [((total, width), BF)],
        [((total, width), BF), ((total, width), F32)],
        LIMITS["ff"],
        6,
        "feed_forward_enc",
    )[0]


def call_feed_backward(block, core, mid, g, weights, shared, chunk=768, rows=256):
    total, width = mid.shape
    outs = [((total, width), F32), ((8, width), F32)]
    scratch = [((total, width), BF), ((total, width), F32), ((total, chunk), BF), ((total, chunk), BF)]
    if block:
        outs.append(((total, width), BF))
    return kernel_call(
        lambda *refs: feed_backward(block, chunk, rows, *refs),
        [core],
        [mid, g, *weights],
        outs,
        scratch,
        LIMITS["fb"],
        14,
        "feed_backward_dec" if block else "feed_backward_enc",
        shared,
    )


def plus(*parts):
    total = parts[0].astype(F32)
    for part in parts[1:]:
        total = total + part.astype(F32)
    return total.astype(BF)


SWAP = [(0, 1), (1, 0)]


def split(side, digit, keep, got, *refs):
    outs = refs[:side]
    kept, come, added, in_sems, out_sems = refs[side:]
    n = kept.shape[1]
    arriving = []
    for t in range(side):
        rows = pl.ds(pl.multiple_of(lax.bitwise_xor(digit[0], t) * n, 16), n)
        arriving.append(
            [
                pltpu.make_async_copy(source.at[rows, :], target.at[t], in_sems.at[t, slot])
                for slot, (source, target) in enumerate(((keep, kept), (got, come)))
            ]
        )
    order = [*range(1, side), 0]
    for t in order:
        for copy in arriving[t]:
            copy.start()
    leaving = []
    for t in order:
        for copy in arriving[t]:
            copy.wait()
        added[t] = (kept[t].astype(F32) + come[t].astype(F32)).astype(BF)
        leaving.append(pltpu.make_async_copy(added.at[t], outs[t], out_sems.at[t]))
        leaving[-1].start()
    for copy in leaving:
        copy.wait()


def call_split(side, digit, keep, got):
    n = keep.shape[0] // side
    return pl.pallas_call(
        lambda *refs: split(side, *refs),
        in_specs=[scalar(), in_hbm(), in_hbm()],
        out_specs=[in_hbm()] * side,
        out_shape=[pltpu.HBM((n, 128), BF)] * side,
        scratch_shapes=[pltpu.VMEM((side, n, 128), BF)] * 3
        + [pltpu.SemaphoreType.DMA((side, 2)), pltpu.SemaphoreType.DMA((side,))],
        compiler_params=params(),
        cost_estimate=cost(3),
        name="split",
    )(digit, keep, got)


class Chain:
    def __init__(self, phase, rows):
        count = lax.axis_size("dp")
        side = math.isqrt(count)
        self.plain = side * side != count or side & (side - 1) != 0 or rows % (16 * count) != 0
        self.side = side = 1 if self.plain else side
        place = lax.axis_index("dp")
        low, high = place % side, (place // side) % side
        self.first, self.second = jnp.where(phase == 0, low, high), jnp.where(phase == 0, high, low)
        self.places = [low * side + high, high * side + low]
        self.count = count
        self.near, self.far = range(1, side), range(side, side * side, side)
        self.there, self.across = self.both(self.near, self.far), self.both(self.far, self.near)

    def both(self, core0, core1):
        return [
            [(core * self.count + i, core * self.count + (i ^ masks[core])) for core in range(2) for i in range(self.count)]
            for masks in zip(core0, core1)
        ]

    def trade(self, sends, routes):
        return [lax.ppermute(send, ("pipe", "dp"), route) for send, route in zip(sends, routes)]

    def start(self, keep, send):
        self.blocks = [keep, lax.ppermute(send, "pipe", SWAP)]

    def scatter_first(self):
        if self.plain:
            total = sum(block.astype(F32) for block in self.blocks)
            self.blocks = [lax.psum(total, "dp").astype(BF)]
            return
        digit = jnp.reshape(self.first, (1,)).astype(jnp.int32)
        mine, *sends = call_split(self.side, digit, *self.blocks)
        self.blocks = [mine] + self.trade(sends, self.there)

    def scatter_second(self):
        if self.plain:
            return
        block = plus(*self.blocks)
        pieces = block.reshape(self.side, block.shape[0] // self.side, 128)
        pick = lambda k: lax.dynamic_index_in_dim(pieces, self.second ^ k, 0, keepdims=False)
        self.blocks = [pick(0)] + self.trade([pick(k) for k in range(1, self.side)], self.across)

    def finish(self):
        if not self.plain:
            self.blocks = [plus(*self.blocks)]
        return self.blocks[0]


def together(*groups):
    return lax.optimization_barrier(groups)


def sum_chains(phase, dec, enc, late):
    dec.scatter_second()
    enc.scatter_first()
    dec.blocks, enc.blocks = together(dec.blocks, enc.blocks)
    enc.scatter_second()
    one, other = enc.finish(), dec.finish()
    mine = jnp.where(phase == 0, one, other)
    got = lax.ppermute(jnp.where(phase == 0, other, one), "pipe", SWAP)
    halves = [jnp.where(phase == 0, mine, got), jnp.where(phase == 0, got, mine)]
    if dec.plain:
        return [[half] for half in halves], late
    near, far = [dec.both(masks, masks) for masks in (dec.near, dec.far)]
    mixed_first, mixed_last = dec.both(dec.far, dec.near), dec.both(dec.near, dec.far)
    halves = together(*halves)
    more = dec.side - 1
    halves = [jnp.concatenate([half] + dec.trade([half] * more, routes), 0) for half, routes in zip(halves, (far, mixed_first))]
    *halves, late = together(*halves, late)
    return [[half] + dec.trade([half] * more, routes) for half, routes in zip(halves, (near, mixed_last))], late


def unpack(side, feed_rows, core, place, *refs):
    blocks, outs = refs[: 2 * side], refs[2 * side :]
    (w1_to, w2_to, joint_to, output_to, embed_to) = outs[:5]
    (place_out, place_bias_out, expand_bias_out, mask_out) = outs[5:9]
    rows_out = outs[9:15]
    held, w1_out, w2_out, joint_out, output_out, embed_out, small, in_sems, out_sems = outs[15:]
    width, ff = w1_out.shape
    hidden = embed_out.shape[0]
    half_rows = held.shape[1]
    n = half_rows // side**2

    def bring(half, act):
        for here in range(2):

            @pl.when(core[0] == here)
            def _(here=here):
                for a in range(side):
                    for b in range(side):
                        shift = b * side + a if half == 1 and here == 0 else a * side + b
                        piece = lax.bitwise_xor(place[half], shift)
                        to = held.at[half, pl.ds(pl.multiple_of(piece * n, 16), n), :]
                        act(pltpu.make_async_copy(blocks[half * side + a].at[pl.ds(b * n, n), :], to, in_sems.at[half]))

    for half in range(2):
        bring(half, lambda copy: copy.start())
    flying = []

    def send(slot, source, target):
        copy = pltpu.make_async_copy(source, target.at[0], out_sems.at[slot])
        copy.start()
        flying.append(copy)

    bring(0, lambda copy: copy.wait())
    for column in range(0, ff, 128):
        first = column // 128 * width
        w1_out[:, column : column + 128] = held[0, first : first + width, :].astype(F32)
    send(0, w1_out, w1_to)
    bring(1, lambda copy: copy.wait())
    for column in range(0, width, 128):
        first = column // 128 * ff
        w2_out[:, column : column + 128] = held[1, first : first + ff, :].astype(F32)
    send(1, w2_out, w2_to)
    targets = (joint_out, output_out, embed_out, small)
    for half, plan in enumerate(pack_plan(width, hidden, half_rows - feed_rows)):
        for which, column, first, rows, at in plan:
            lanes = slice(column * 128, column * 128 + 128)
            values = held[half, feed_rows + at : feed_rows + at + rows, :]
            targets[which][first : first + rows, lanes] = values.astype(F32)
    send(2, joint_out, joint_to)
    send(3, output_out, output_to)
    send(4, embed_out, embed_to)
    for out, row in zip(rows_out, (0, 1, 2, 8, 9, 10)):
        out[...] = small[row : row + 1, :]
    mask_out[...] = small[3:4, :]
    place_out[0] = small[4:7, 0:hidden]
    place_bias_out[...] = small[7:8, 0:hidden]
    for part in range(ff // width):
        expand_bias_out[:, part * width : (part + 1) * width] = small[11 + part : 12 + part, :]
    for copy in flying:
        copy.wait()


def call_unpack(core, place, halves, width, hidden, ff):
    side = len(halves[0])
    half_rows = halves[0][0].shape[0] * side
    large = [(1, width, ff), (1, ff, width), (1, width, 3 * width), (1, width, width), (1, hidden, width)]
    tiny = [(1, 3, hidden), (1, hidden), (1, ff), (1, width)] + [(1, width)] * 6
    return pl.pallas_call(
        lambda *refs: unpack(side, ff * width // 128, *refs),
        in_specs=[scalar()] * 2 + [anywhere()] * (2 * side),
        out_specs=[in_hbm()] * len(large) + [vmem()] * len(tiny),
        out_shape=[pltpu.HBM(shape, F32) for shape in large] + [sds(shape, F32) for shape in tiny],
        scratch_shapes=[pltpu.VMEM((2, half_rows, 128), BF)]
        + [pltpu.VMEM(shape[1:], F32) for shape in large]
        + [pltpu.VMEM((16, width), F32), pltpu.SemaphoreType.DMA((2,)), pltpu.SemaphoreType.DMA((5,))],
        compiler_params=pltpu.CompilerParams(vmem_limit_bytes=20 * 2**20),
        cost_estimate=cost(5),
        name="unpack",
    )(core, place, *halves[0], *halves[1])


def shards(
    tokens,
    centres,
    visible,
    lengths,
    cotangent,
    attend_gain,
    attend_shift,
    joint_weight,
    output_weight,
    output_bias,
    feed_gain,
    feed_shift,
    expand_weight,
    expand_bias,
    reduce_weight,
    reduce_bias,
    place_weight,
    place_bias,
    embed_weight,
    mask_token,
):
    phase = lax.axis_index("pipe")
    encoding = phase == 0
    micro, rows, width = tokens.shape
    half = micro // 2
    hidden = place_weight.shape[2]
    core = jnp.reshape(phase, (1,)).astype(jnp.int32)
    no_mask = jnp.zeros((1, width), F32)
    mask_row = mask_token[None, :]
    flat = lambda a: a.reshape(half * rows, a.shape[-1])
    here = lambda a: flat(lax.dynamic_slice_in_dim(a, phase * half, half, 0))
    given = here(cotangent)

    wide = lambda piece: jnp.pad(piece, ((0, 0), (0, width - hidden)))
    small = jnp.concatenate(
        [attend_gain, attend_shift, output_bias, feed_gain, feed_shift, reduce_bias, jnp.zeros((2, width), F32)]
        + [wide(place_weight[0]), wide(place_bias), expand_bias.reshape(-1, width)]
    )
    own = [small, joint_weight[0], output_weight[0], embed_weight[0], expand_weight[0], reduce_weight[0]]
    other = [lax.ppermute(piece, "pipe", SWAP) for piece in own]
    both = [pair for mine in zip(own, other) for pair in mine]
    attend_weights = both[:8]
    feed_weights_both = both[:2] + both[8:]

    unit = 256
    ff = expand_weight.shape[2]

    def joined(enc_part, dec_part):
        got = lax.ppermute(jnp.where(encoding, dec_part, enc_part), "pipe", SWAP)
        front = jnp.where(encoding, enc_part, got)
        second = jnp.where(encoding, got, dec_part)
        return jnp.concatenate([front, second], 0).reshape(1, micro, rows, width)

    ex, ej, ee, ei, em, emid = call_attend_forward(
        False, rows, core, lengths, here(tokens), centres, visible, mask_row, attend_weights
    )
    enc_out = call_feed_forward(core, emid, feed_weights_both)
    dx, dj, de, di, dm, dmid = call_attend_forward(
        True, rows, core, lengths, enc_out, centres, visible, mask_row, attend_weights
    )
    feed_rows = ff * width // 128
    attend_rows = packed_half_rows(width, hidden, unit)
    half_rows = feed_rows + attend_rows
    parts = [(half_rows, 128)] * 2
    dback, d_small, dec_out, *dec_halves = call_feed_backward(
        1, core, dmid, given, feed_weights_both, (parts, 0, feed_rows)
    )
    ddx, enc_back, d_mask, *dec_halves = call_attend_backward(
        True, rows, core, dback, dx, centres, visible, dj, de, di, dm, attend_weights, d_small, no_mask,
        (dec_halves, feed_rows, attend_rows),
    )
    dec = Chain(phase, half_rows)
    dec.start(*dec_halves)
    eback, e_small, *enc_halves = call_feed_backward(0, core, emid, enc_back, feed_weights_both, (parts, 0, feed_rows))
    phase_out = joined(enc_out, dec_out)
    eback, phase_out, dec.blocks = together(eback, phase_out, dec.blocks)
    dec.scatter_first()
    edx, _, _, *enc_halves = call_attend_backward(
        False, rows, core, eback, ex, centres, visible, ej, ee, ei, em, attend_weights, e_small, d_mask,
        (enc_halves, feed_rows, attend_rows),
    )
    enc = Chain(phase, half_rows)
    enc_halves, dec.blocks = together(enc_halves, dec.blocks)
    enc.start(*enc_halves)
    halves, (edx, ddx) = sum_chains(phase, dec, enc, (edx, ddx))
    phase_in_grad = joined(edx, ddx)
    halves, phase_in_grad = together(halves, phase_in_grad)
    place = jnp.stack(enc.places).astype(jnp.int32)
    (w1_grad, w2_grad, joint_grad, output_grad, embed_grad, place_grad, place_bias_grad, expand_bias_grad, mask_grad, *vectors) = (
        call_unpack(core, place, halves, width, hidden, ff)
    )
    attend_gain_grad, attend_shift_grad, output_bias_grad, feed_gain_grad, feed_shift_grad, reduce_bias_grad = vectors
    return (
        phase_out, phase_in_grad, attend_gain_grad, attend_shift_grad, joint_grad, output_grad, output_bias_grad,
        feed_gain_grad, feed_shift_grad, w1_grad, expand_bias_grad, w2_grad, reduce_bias_grad, place_grad,
        place_bias_grad, embed_grad, mask_grad.reshape(width),
    )


def solution(mesh):
    in_specs = (
        P(None, "dp", None),
        P(None, None, "dp"),
        P(None, "dp"),
        P(None, "dp"),
        P(None, "dp", None),
        P("pipe", None),
        P("pipe", None),
        P("pipe", None, None),
        P("pipe", None, None),
        P("pipe", None),
        P("pipe", None),
        P("pipe", None),
        P("pipe", None, None),
        P("pipe", None),
        P("pipe", None, None),
        P("pipe", None),
        P("pipe", None, None),
        P("pipe", None),
        P("pipe", None, None),
        P(),
    )
    out_specs = (
        P("pipe", None, "dp", None),
        P("pipe", None, "dp", None),
        P("pipe", None),
        P("pipe", None),
        P("pipe", None, None),
        P("pipe", None, None),
        P("pipe", None),
        P("pipe", None),
        P("pipe", None),
        P("pipe", None, None),
        P("pipe", None),
        P("pipe", None, None),
        P("pipe", None),
        P("pipe", None, None),
        P("pipe", None),
        P("pipe", None, None),
        P(),
    )
    return jax.shard_map(shards, mesh=mesh, in_specs=in_specs, out_specs=out_specs, check_vma=False)
```

```python
import math

import jax
import jax.numpy as jnp
from jax import lax
from jax.experimental import pallas as pl
from jax.experimental.pallas import tpu as pltpu
from jax.sharding import PartitionSpec as P

HEADS = 6
NEG_FILL = -1e30
NORM_EPS = 1e-05
GELU_A = math.sqrt(2.0 / math.pi)
GELU_B = GELU_A * 0.044715
BF = jnp.bfloat16
F32 = jnp.float32
VMEM_LIMIT = 16 * 2**20


def dot(a, b):
    return jnp.dot(a, b, preferred_element_type=F32)


def dot_rt(a, b):
    return lax.dot_general(a, b, (((1,), (1,)), ((), ())), preferred_element_type=F32)


def dot_lt(a, b):
    return lax.dot_general(a, b, (((0,), (0,)), ((), ())), preferred_element_type=F32)


def gelu_both(v):
    v2 = v * v
    h = 0.5 * jnp.tanh(v * (GELU_A + GELU_B * v2)) + 0.5
    slope = h + (h - h * h) * (v * (2.0 * GELU_A + 6.0 * GELU_B * v2))
    return v * h, slope


def gelu_only(v):
    return v * (0.5 * jnp.tanh(v * (GELU_A + GELU_B * (v * v))) + 0.5)


def norm_parts(x):
    scale = 1.0 / x.shape[-1]
    centred = x - jnp.sum(x, -1, keepdims=True) * scale
    var = jnp.sum(centred * centred, -1, keepdims=True) * scale
    inverse = lax.rsqrt(var + NORM_EPS)
    return centred * inverse, inverse


def norm_back(u, z, inverse, gain):
    scale = 1.0 / u.shape[-1]
    w = u * gain
    m1 = jnp.sum(w, -1, keepdims=True) * scale
    m2 = jnp.sum(w * z, -1, keepdims=True) * scale
    return inverse * (w - m1 - z * m2)


def three_parts(value):
    parts = []
    for _ in range(3):
        parts.append(value.astype(BF))
        value = value - parts[-1].astype(F32)
    return parts


def place_pre(centre, place_weight, place_bias):
    c, w = three_parts(centre), three_parts(place_weight)
    pairs = ((0, 0), (0, 1), (1, 0), (0, 2), (2, 0), (1, 1))
    left = jnp.concatenate([c[i].astype(F32) for i, _ in pairs], axis=0).astype(BF)
    right = jnp.concatenate([w[j].astype(F32) for _, j in pairs], axis=0).astype(BF)
    return dot_lt(left, right) + place_bias


def place_back(centre, dpre):
    c, d = three_parts(centre), three_parts(dpre)
    count, width = centre.shape[0], dpre.shape[1]
    left = jnp.concatenate([part.astype(F32) for part in c], axis=0).astype(BF)
    products = dot(left, jnp.concatenate(d, axis=1))
    block = lambda i, j: products[i * count : (i + 1) * count, j * width : (j + 1) * width]
    return block(0, 0) + ((block(0, 1) + block(1, 0)) + (block(0, 2) + block(2, 0) + block(1, 1)))


def column_of(row, width):
    rows = lax.broadcasted_iota(jnp.int32, (16, row.shape[1]), 0)
    top = jnp.where(rows == 0, jnp.broadcast_to(row, rows.shape), 0).astype(F32)
    return dot_lt(top.astype(BF), jnp.ones((16, width), BF))


def segments(lengths, micro_index, slots, places):
    total = jnp.int32(0)
    seg = jnp.zeros(places.shape, jnp.int32)
    for slot in range(slots):
        total = total + lengths[micro_index, slot]
        seg = seg + (places >= total).astype(jnp.int32)
    return seg


def lane_low(shape, half):
    return lax.broadcasted_iota(jnp.int32, shape, 1) < half


SMALL = ("attend_gain", "attend_shift", "output_bias", "feed_gain", "feed_shift", "reduce_bias")


def small_row(values, name):
    place = SMALL.index(name)
    return values[place : place + 1, :]


def place_rows(values, hidden):
    return values[8:11, :hidden], values[11:12, :hidden]


def expand_row(values, width, ff):
    return [values[12 + part : 13 + part, :] for part in range(ff // width)]


def chosen(mine, own, other):
    return jnp.where(mine, own[...], other[...])


def attend_forward(decoding, rows, core, lengths, *refs):
    (x_in, centres, visible, mask_token, small_own, small_other, wj_own, wj_other) = refs[:8]
    (wo_own, wo_other, we_own, we_other) = refs[8:12]
    (x_out, joint_out, e_out, inv_out, mixed_out, mid_out, bias) = refs[12:19]
    total, width = x_out.shape
    half = total // rows
    slots = lengths.shape[1]
    head = width // HEADS
    pair = 2 * head
    mine = core[0] == int(decoding)
    small = chosen(mine, small_own, small_other)
    ag, ash, bo = (small_row(small, name) for name in SMALL[:3])
    we = chosen(mine, we_own, we_other)
    pw, pb = place_rows(small, we.shape[0])

    for block in range(half):
        span = slice(block * rows, (block + 1) * rows)
        micro_index = core[0] * half + block
        embed = dot(gelu_only(place_pre(centres[micro_index], pw, pb)).astype(BF), we)
        seen = visible[pl.ds(micro_index, 1), :]
        source = x_in[span, :].astype(F32)
        if decoding:
            shown = column_of(seen, 128)[:, :1] > 0.5
            source = jnp.where(shown, source, mask_token[...])
        x_out[span, :] = source + embed
        places_k = lax.broadcasted_iota(jnp.int32, (1, rows), 1)
        seg_k = segments(lengths, micro_index, slots, places_k)
        allowed = column_of(seg_k, 128)[:, :1].astype(jnp.int32) == seg_k
        if not decoding:
            places_q = lax.broadcasted_iota(jnp.int32, (rows, rows), 0)
            places_kk = lax.broadcasted_iota(jnp.int32, (rows, rows), 1)
            allowed = allowed & ((seen > 0) | (places_q == places_kk))
        bias[block] = jnp.where(allowed, 0.0, NEG_FILL)

    z, _ = norm_parts(x_out[...])
    joint_out[...] = dot((z * ag + ash).astype(BF), chosen(mine, wj_own, wj_other)).astype(BF)

    low_k = lane_low((rows, pair), head)
    for block in range(half):
        span = slice(block * rows, (block + 1) * rows)
        for p in range(HEADS // 2):
            cols = slice(p * pair, (p + 1) * pair)
            qp = joint_out[span, cols] * BF(head**-0.5)
            kp = joint_out[span, width + p * pair : width + (p + 1) * pair]
            vp = joint_out[span, 2 * width + p * pair : 2 * width + (p + 1) * pair]
            out = []
            for side in range(2):
                mine_k = low_k == (side == 0)
                s = dot_rt(jnp.where(mine_k, qp, BF(0)), kp) + bias[block]
                e = jnp.exp(s - jnp.max(s, -1, keepdims=True)).astype(BF)
                e_out[block * HEADS + 2 * p + side] = e
                out.append(dot(e, jnp.where(mine_k, vp, BF(1))))
            inv = 1.0 / pltpu.roll(jnp.where(low_k, out[1], out[0]), head, 1)
            inv_out[span, cols] = inv.astype(BF)
            mixed_out[span, cols] = (jnp.where(low_k, out[0], out[1]) * inv).astype(BF)
    wo = chosen(mine, wo_own, wo_other)
    mid_out[...] = x_out[...] + (dot(mixed_out[...], wo) + bo)


def pack_plan(width, hidden, half_rows):
    plan = ([], [])
    place = 0
    for which, (rows, columns) in enumerate(((width, 3 * width), (width, width), (hidden, width), (16, width))):
        for column in range(columns // 128):
            done = 0
            while done < rows:
                half, at = divmod(place, half_rows)
                count = min(rows - done, half_rows - at)
                plan[half].append((which, column, done, count, at))
                done += count
                place += count
    return plan


def packed_half_rows(width, hidden, unit):
    total = (3 * width * width + width * width + hidden * width + 16 * width) // 128
    return -(-total // (2 * unit)) * unit


def attend_backward(decoding, rows, core, *refs):
    (dmid_in, x_in, centres, visible, joint_in, e_in, inv_in, mixed_in) = refs[:8]
    (small_own, small_other, wj_own, wj_other, wo_own, wo_other, we_own, we_other) = refs[8:16]
    (small_feed, extra) = refs[16:18]
    dx_out, send_back, mask_g, half0, half1, send_halves = refs[18:24]
    dl, mu, dj, ds, joint_g, output_g, embed_g, small_g = refs[24:]
    total, width = x_in.shape
    half = total // rows
    head = width // HEADS
    pair = 2 * head
    mine = core[0] == int(decoding)
    small = chosen(mine, small_own, small_other)
    ag, ash = (small_row(small, name) for name in SMALL[:2])
    we = chosen(mine, we_own, we_other)
    hidden = we.shape[0]
    pw, pb = place_rows(small, hidden)

    dm = dmid_in[...].astype(BF)
    output_g[...] = dot_lt(mixed_in[...], dm)
    low_dl = (dot_rt(dm, chosen(mine, wo_own, wo_other)) * inv_in[...].astype(F32)).astype(BF)
    dl[...] = low_dl
    mu[...] = (low_dl.astype(F32) * -mixed_in[...].astype(F32)).astype(BF)
    small_g[...] = jnp.zeros(small_g.shape, F32)
    small_g[2:3, :] = jnp.sum(dm.astype(F32), 0, keepdims=True)

    low_k = lane_low((rows, pair), head)
    ones = jnp.ones((rows, pair), BF)
    for block in range(half):
        span = slice(block * rows, (block + 1) * rows)
        for p in range(HEADS // 2):
            cols = slice(p * pair, (p + 1) * pair)
            qp = joint_in[span, cols] * BF(head**-0.5)
            kp = joint_in[span, width + p * pair : width + (p + 1) * pair]
            vp = joint_in[span, 2 * width + p * pair : 2 * width + (p + 1) * pair]
            v_ext = jnp.concatenate([vp, ones], axis=1)
            dlp = dl[span, cols]
            mup = mu[span, cols]
            dq = dk = dv = None
            for side in range(2):
                mine_k = low_k == (side == 0)
                place = 2 * p + side
                d_one = jnp.where(mine_k, dlp, BF(0))
                u_one = jnp.where(mine_k, mup, BF(0))
                dp = dot_rt(jnp.concatenate([d_one, u_one], axis=1), v_ext)
                ds[place % 2] = (e_in[block * HEADS + place].astype(F32) * dp).astype(BF)
                q_one = jnp.where(mine_k, qp, BF(0))
                k_one = jnp.where(mine_k, kp, BF(0))
                dv_one = dot_lt(e_in[block * HEADS + place], d_one)
                dk_one = dot_lt(ds[place % 2], q_one)
                dq_one = dot(ds[place % 2], k_one)
                dv = dv_one if dv is None else dv + dv_one
                dk = dk_one if dk is None else dk + dk_one
                dq = dq_one if dq is None else dq + dq_one
            dj[span, cols] = (dq * head**-0.5).astype(BF)
            dj[span, width + p * pair : width + (p + 1) * pair] = dk.astype(BF)
            dj[span, 2 * width + p * pair : 2 * width + (p + 1) * pair] = dv.astype(BF)

    z, inverse = norm_parts(x_in[...])
    joint_g[...] = dot_lt((z * ag + ash).astype(BF), dj[...])
    dn = dot_rt(dj[...], chosen(mine, wj_own, wj_other))
    small_g[0:1, :] = jnp.sum(dn * z, 0, keepdims=True)
    small_g[1:2, :] = jnp.sum(dn, 0, keepdims=True)
    dx = dmid_in[...] + norm_back(dn, z, inverse, ag)
    dx_out[...] = dx
    ge = dx.astype(BF)
    acts = []
    for block in range(half):
        span = slice(block * rows, (block + 1) * rows)
        micro_index = core[0] * half + block
        if decoding:
            shown = column_of(visible[pl.ds(micro_index, 1), :], 128)[:, :1] > 0.5
            send_back[span, :] = jnp.where(shown, dx[span], 0.0).astype(BF)
            small_g[3:4, :] += jnp.sum(jnp.where(shown, 0.0, dx[span]), 0, keepdims=True)
        act, slope = gelu_both(place_pre(centres[micro_index], pw, pb))
        acts.append(act.astype(BF))
        dpre = slope * dot_rt(ge[span], we)
        small_g[4:7, 0:hidden] += place_back(centres[micro_index], dpre)
        small_g[7:8, 0:hidden] += jnp.sum(dpre, 0, keepdims=True)
    embed_g[...] = dot_lt(jnp.concatenate(acts, axis=0), ge)

    mask_g[...] = small_g[3:4, :]
    if not decoding:
        small_g[3:4, :] = extra[...]
    small_g[8:15, :] = small_feed[0:7, :]
    sources = (joint_g, output_g, embed_g, small_g)
    for target, plan in zip((half0, half1), pack_plan(width, hidden, half0.shape[0])):
        for which, column, first, count, at in plan:
            lanes = slice(column * 128, column * 128 + 128)
            target[at : at + count, :] = sources[which][first : first + count, lanes].astype(BF)
    send_halves()


def feed_start(mid_in, small, low):
    z, _ = norm_parts(mid_in[...])
    low[...] = (z * small_row(small, "feed_gain") + small_row(small, "feed_shift")).astype(BF)


def feed_bias(small, width, first, chunk):
    rows = [small[12 + part : 13 + part, :] for part in range(first // width, (first + chunk) // width)]
    return jnp.concatenate(rows, axis=1) if len(rows) > 1 else rows[0]


def row_blocks(total, rows):
    return [slice(first, first + rows) for first in range(0, total, rows)]


def feed_forward(chunk, rows, core, mid_in, *refs):
    small_own, small_other, w1_own, w1_other, w2_own, w2_other, out, low, acc = refs
    total, width = mid_in.shape
    mine = core[0] == 0
    small = chosen(mine, small_own, small_other)
    feed_start(mid_in, small, low)
    acc[...] = mid_in[...] + small_row(small, "reduce_bias")
    for first in range(0, w1_own.shape[1], chunk):
        cols = slice(first, first + chunk)
        w1 = jnp.where(mine, w1_own[:, cols], w1_other[:, cols])
        w2 = jnp.where(mine, w2_own[cols, :], w2_other[cols, :])
        bias = feed_bias(small, width, first, chunk)
        for span in row_blocks(total, rows):
            acc[span, :] += dot(gelu_only(dot(low[span, :], w1) + bias).astype(BF), w2)
    out[...] = acc[...].astype(BF)


def feed_weight_grads(cols, low, act_low, dh, g, half0, half1, small_g):
    width = g.shape[1]
    ff = half0.shape[0] * 128 // width
    w1_g = dot_lt(low, dh).astype(BF)
    w2_g = dot_lt(act_low, g).astype(BF)
    for first in range(0, cols.stop - cols.start, 128):
        place = (cols.start + first) // 128 * width
        half0[place : place + width, :] = w1_g[:, first : first + 128]
    for first in range(0, width, 128):
        place = first // 128 * ff
        half1[place + cols.start : place + cols.stop, :] = w2_g[:, first : first + 128]
    column_sum = jnp.sum(dh.astype(F32), 0, keepdims=True)
    for first in range(0, cols.stop - cols.start, width):
        row = 3 + (cols.start + first) // width
        small_g[row : row + 1, :] = column_sum[:, first : first + width]


def feed_tail(g_in, dn_acc, mid_in, small, dmid_out, small_g, rows):
    total = mid_in.shape[0]
    sums = None
    for span in row_blocks(total, rows):
        z, inverse = norm_parts(mid_in[span, :])
        g = g_in[span, :].astype(F32)
        dn = dn_acc[span, :]
        dmid_out[span, :] = g + norm_back(dn, z, inverse, small_row(small, "feed_gain"))
        new = [jnp.sum(value, 0, keepdims=True) for value in (dn * z, dn, g)]
        sums = new if sums is None else [a + b for a, b in zip(sums, new)]
    for row, value in enumerate(sums):
        small_g[row : row + 1, :] = value


def feed_backward(block, chunk, rows, core, mid_in, g_in, *refs):
    small_own, small_other, w1_own, w1_other, w2_own, w2_other = refs[:6]
    refs = refs[6:]
    dmid_out, small_g = refs[:2]
    half0, half1, send_halves, low, dn_acc, act_low, dh = refs[2 + block : 9 + block]
    out, acc = (refs[2], dmid_out) if block else (None, None)
    total, width = mid_in.shape
    ff = w1_own.shape[1]
    mine = core[0] == block
    small = chosen(mine, small_own, small_other)
    feed_start(mid_in, small, low)
    if block:
        acc[...] = mid_in[...] + small_row(small, "reduce_bias")
    for first in range(0, ff, chunk):
        cols = slice(first, first + chunk)
        w1 = jnp.where(mine, w1_own[:, cols], w1_other[:, cols])
        w2 = jnp.where(mine, w2_own[cols, :], w2_other[cols, :])
        bias = feed_bias(small, width, first, chunk)
        for span in row_blocks(total, rows):
            act, slope = gelu_both(dot(low[span, :], w1) + bias)
            act = act.astype(BF)
            act_low[span, :] = act
            if block:
                acc[span, :] += dot(act, w2)
            dh_rows = (slope * dot_rt(g_in[span, :], w2)).astype(BF)
            dh[span, :] = dh_rows
            dn = dot_rt(dh_rows, w1)
            dn_acc[span, :] = dn if first == 0 else dn_acc[span, :] + dn
        feed_weight_grads(cols, low[...], act_low[...], dh[...], g_in[...], half0, half1, small_g)
    send_halves()
    if block:
        out[...] = acc[...].astype(BF)
    feed_tail(g_in, dn_acc, mid_in, small, dmid_out, small_g, rows)


def params():
    return pltpu.CompilerParams(vmem_limit_bytes=VMEM_LIMIT)


def sds(shape, kind):
    return jax.ShapeDtypeStruct(shape, kind)


def scalar():
    return pl.BlockSpec(memory_space=pltpu.SMEM)


def cost(microseconds):
    return pl.CostEstimate(flops=int(microseconds * 1e9), bytes_accessed=2**20, transcendentals=0)


def anywhere():
    return pl.BlockSpec(memory_space=pl.ANY)


def anywhere():
    return pl.BlockSpec(memory_space=pl.ANY)


def vmem():
    return pl.BlockSpec(memory_space=pltpu.VMEM)


def anywhere():
    return pl.BlockSpec(memory_space=pl.ANY)


def in_hbm():
    return pl.BlockSpec(memory_space=pltpu.HBM)


def kernel_call(body, scalars, arrays, outs, scratch, limit, time, name, rows):
    in_specs = [scalar() for _ in scalars] + [vmem() for _ in arrays]
    first = len(in_specs)

    def run(*refs):
        core = refs[0]
        results = refs[first : first + len(outs)]
        keep, send = refs[first + len(outs) : first + len(outs) + 2]
        *held, half0, half1, sems = refs[first + len(outs) + 2 :]

        def both(act):
            for n, pair in enumerate(((keep, send), (send, keep))):

                @pl.when(core[0] == n)
                def _(pair=pair):
                    for slot, half in enumerate((half0, half1)):
                        act(pltpu.make_async_copy(half, pair[slot], sems.at[slot]))

        body(*refs[:first], *results, half0, half1, lambda: both(lambda copy: copy.start()), *held)
        both(lambda copy: copy.wait())

    return pl.pallas_call(
        run,
        in_specs=in_specs,
        out_specs=[vmem() for _ in outs] + [in_hbm()] * 2,
        out_shape=[sds(shape, kind) for shape, kind in outs] + [pltpu.HBM((rows, 128), BF)] * 2,
        scratch_shapes=[pltpu.VMEM(shape, kind) for shape, kind in scratch]
        + [pltpu.VMEM((rows, 128), BF)] * 2
        + [pltpu.SemaphoreType.DMA((2,))],
        compiler_params=pltpu.CompilerParams(vmem_limit_bytes=limit * 2**20),
        cost_estimate=cost(time),
        name=name,
    )(*scalars, *arrays)


def plain_call(body, scalars, arrays, outs, scratch, limit, time, name):
    return pl.pallas_call(
        body,
        in_specs=[scalar() for _ in scalars] + [vmem() for _ in arrays],
        out_specs=[vmem() for _ in outs],
        out_shape=[sds(shape, kind) for shape, kind in outs],
        scratch_shapes=[pltpu.VMEM(shape, kind) for shape, kind in scratch],
        compiler_params=pltpu.CompilerParams(vmem_limit_bytes=limit * 2**20),
        cost_estimate=cost(time),
        name=name,
    )(*scalars, *arrays)


LIMITS = dict(af=8, ab=13, ff=6, fb=15)


def call_attend_forward(decoding, rows, core, lengths, x_in, centres, visible, mask_token, weights):
    total, width = x_in.shape
    half = total // rows
    return plain_call(
        lambda *refs: attend_forward(decoding, rows, *refs),
        [core, lengths],
        [x_in, centres, visible, mask_token, *weights],
        [
            ((total, width), F32),
            ((total, 3 * width), BF),
            ((half * HEADS, rows, rows), BF),
            ((total, width), BF),
            ((total, width), BF),
            ((total, width), F32),
        ],
        [((half, rows, rows), F32)],
        LIMITS["af"],
        9,
        "attend_forward_dec" if decoding else "attend_forward_enc",
    )


def call_attend_backward(decoding, rows, core, dmid, x, centres, visible, joint, e, inv, mixed, weights, small_feed, extra, shared):
    total, width = x.shape
    hidden = weights[6].shape[0]
    return kernel_call(
        lambda *refs: attend_backward(decoding, rows, *refs),
        [core],
        [dmid, x, centres, visible, joint, e, inv, mixed, *weights, small_feed, extra],
        [((total, width), F32), ((total, width) if decoding else (16, width), BF), ((1, width), F32)],
        [
            ((total, width), BF),
            ((total, width), BF),
            ((total, 3 * width), BF),
            ((2, rows, rows), BF),
            ((width, 3 * width), F32),
            ((width, width), F32),
            ((hidden, width), F32),
            ((16, width), F32),
        ],
        LIMITS["ab"],
        15,
        "attend_backward_dec" if decoding else "attend_backward_enc",
        shared,
    )


def call_feed_forward(core, mid, weights, chunk=768, rows=256):
    total, width = mid.shape
    return plain_call(
        lambda *refs: feed_forward(chunk, rows, *refs),
        [core],
        [mid, *weights],
        [((total, width), BF)],
        [((total, width), BF), ((total, width), F32)],
        LIMITS["ff"],
        6,
        "feed_forward_enc",
    )[0]


def call_feed_backward(block, core, mid, g, weights, shared, chunk=768, rows=256):
    total, width = mid.shape
    outs = [((total, width), F32), ((8, width), F32)]
    scratch = [((total, width), BF), ((total, width), F32), ((total, chunk), BF), ((total, chunk), BF)]
    if block:
        outs.append(((total, width), BF))
    return kernel_call(
        lambda *refs: feed_backward(block, chunk, rows, *refs),
        [core],
        [mid, g, *weights],
        outs,
        scratch,
        LIMITS["fb"],
        14,
        "feed_backward_dec" if block else "feed_backward_enc",
        shared,
    )


def plus(*parts):
    total = parts[0].astype(F32)
    for part in parts[1:]:
        total = total + part.astype(F32)
    return total.astype(BF)


SWAP = [(0, 1), (1, 0)]


def split(side, sources, digit, *refs):
    pairs = [refs[2 * n : 2 * n + 2] for n in range(sources)]
    outs = refs[2 * sources : 2 * sources + side]
    *kept, come, added, in_sems, out_sems = refs[2 * sources + side :]
    order = [*range(1, side), 0]
    cuts = []
    for t in range(side):
        at = 0
        cuts.append([])
        for n, (keep, got) in enumerate(pairs):
            count = kept[n].shape[1]
            rows = pl.ds(pl.multiple_of(lax.bitwise_xor(digit[0], t) * count, 16), count)
            copies = [pltpu.make_async_copy(keep.at[rows, :], kept[n].at[t], in_sems.at[t, n, 0])]
            if n == 0:
                copies.append(pltpu.make_async_copy(got.at[rows, :], come.at[t], in_sems.at[t, n, 1]))
            cuts[-1].append((copies, kept[n], got, rows, slice(at, at + count)))
            at += count
    for t in order:
        for copies, *_ in cuts[t]:
            for copy in copies:
                copy.start()
    leaving = []
    for t in order:
        for copies, mine, got, rows, to in cuts[t]:
            for copy in copies:
                copy.wait()
            other = come[t] if len(copies) > 1 else got[rows, :]
            added[t, to, :] = (mine[t].astype(F32) + other.astype(F32)).astype(BF)
        leaving.append(pltpu.make_async_copy(added.at[t], outs[t], out_sems.at[t]))
        leaving[-1].start()
    for copy in leaving:
        copy.wait()


def held(array):
    return pltpu.with_memory_space_constraint(array, pltpu.HBM)


def call_split(side, digit, pairs):
    counts = [keep.shape[0] // side for keep, _ in pairs]
    n = sum(counts)
    return pl.pallas_call(
        lambda *refs: split(side, len(pairs), *refs),
        in_specs=[scalar(), in_hbm(), in_hbm()] + [in_hbm(), vmem()] * (len(pairs) - 1),
        out_specs=[in_hbm()] * side,
        out_shape=[pltpu.HBM((n, 128), BF)] * side,
        scratch_shapes=[pltpu.VMEM((side, count, 128), BF) for count in counts]
        + [pltpu.VMEM((side, counts[0], 128), BF), pltpu.VMEM((side, n, 128), BF)]
        + [pltpu.SemaphoreType.DMA((side, len(pairs), 2)), pltpu.SemaphoreType.DMA((side,))],
        compiler_params=params(),
        cost_estimate=cost(3),
        name="split",
    )(digit, *[held(array) if n < 2 or n % 2 == 0 else array for n, array in enumerate(sum(map(list, pairs), []))])


class Chain:
    def __init__(self, phase, rows):
        self.pairs = []
        count = lax.axis_size("dp")
        side = math.isqrt(count)
        self.plain = side * side != count or side & (side - 1) != 0 or any(n % (16 * count) for n in rows)
        self.side = side = 1 if self.plain else side
        place = lax.axis_index("dp")
        low, high = place % side, (place // side) % side
        self.first, self.second = jnp.where(phase == 0, low, high), jnp.where(phase == 0, high, low)
        self.places = [low * side + high, high * side + low]
        self.count = count
        self.near, self.far = range(1, side), range(side, side * side, side)
        self.there, self.across = self.both(self.near, self.far), self.both(self.far, self.near)

    def both(self, core0, core1):
        return [
            [(core * self.count + i, core * self.count + (i ^ masks[core])) for core in range(2) for i in range(self.count)]
            for masks in zip(core0, core1)
        ]

    def trade(self, sends, routes):
        return [lax.ppermute(send, ("pipe", "dp"), route) for send, route in zip(sends, routes)]

    def start(self, keep, send):
        self.pairs.append((keep, lax.ppermute(send, "pipe", SWAP)))

    def scatter_first(self):
        if self.plain:
            total = jnp.concatenate([keep.astype(F32) + got.astype(F32) for keep, got in self.pairs], 0)
            self.blocks = [lax.psum(total, "dp").astype(BF)]
            return
        digit = jnp.reshape(self.first, (1,)).astype(jnp.int32)
        mine, *sends = call_split(self.side, digit, self.pairs)
        self.blocks = [mine] + self.trade(sends, self.there)

    def scatter_second(self):
        if self.plain:
            return
        block = plus(*self.blocks)
        pieces = block.reshape(self.side, block.shape[0] // self.side, 128)
        pick = lambda k: lax.dynamic_index_in_dim(pieces, self.second ^ k, 0, keepdims=False)
        self.blocks = [pick(0)] + self.trade([pick(k) for k in range(1, self.side)], self.across)

    def finish(self):
        if not self.plain:
            self.blocks = [plus(*self.blocks)]
        return self.blocks[0]


def together(*groups):
    return lax.optimization_barrier(groups)


def sum_chains(phase, dec, enc, late):
    dec.scatter_second()
    enc.scatter_first()
    dec.blocks, enc.blocks = together(dec.blocks, enc.blocks)
    enc.scatter_second()
    one, other = enc.finish(), dec.finish()
    mine = jnp.where(phase == 0, one, other)
    got = lax.ppermute(jnp.where(phase == 0, other, one), "pipe", SWAP)
    halves = [jnp.where(phase == 0, mine, got), jnp.where(phase == 0, got, mine)]
    if dec.plain:
        return [[half] for half in halves], late
    near, far = [dec.both(masks, masks) for masks in (dec.near, dec.far)]
    mixed_first, mixed_last = dec.both(dec.far, dec.near), dec.both(dec.near, dec.far)
    halves = together(*halves)
    more = dec.side - 1
    halves = [jnp.concatenate([half] + dec.trade([half] * more, routes), 0) for half, routes in zip(halves, (far, mixed_first))]
    *halves, late = together(*halves, late)
    return [[half] + dec.trade([half] * more, routes) for half, routes in zip(halves, (near, mixed_last))], late


def unpack(side, feed_rows, core, place, *refs):
    blocks, outs = refs[: 2 * side], refs[2 * side :]
    (w1_to, w2_to, joint_to, output_to, embed_to) = outs[:5]
    (place_out, place_bias_out, expand_bias_out, mask_out) = outs[5:9]
    rows_out = outs[9:15]
    held, w1_out, w2_out, joint_out, output_out, embed_out, small, out_sems = outs[15:]
    width, ff = w1_out.shape
    hidden = embed_out.shape[0]
    half_rows = held.shape[1]
    n = half_rows // side**2
    quarter, feed_part = half_rows // side, feed_rows // side
    attend_part = quarter - feed_part

    def feed_spans(first, rows):
        done = 0
        while done < rows:
            block, inner = divmod(first + done, feed_part)
            take = min(rows - done, feed_part - inner)
            yield block * quarter + inner, take, done
            done += take

    for here in range(2):

        @pl.when(core[0] == here)
        def _(here=here):
            for half in range(2):
                for a in range(side):
                    for b in range(side):
                        shift = b * side + a if half == 1 and here == 0 else a * side + b
                        piece = lax.bitwise_xor(place[half], shift)
                        rows = pl.ds(pl.multiple_of(piece * n, 16), n)
                        held[half, rows, :] = blocks[half * side + a][b * n : b * n + n, :]

    flying = []

    def send(slot, source, target):
        copy = pltpu.make_async_copy(source, target.at[0], out_sems.at[slot])
        copy.start()
        flying.append(copy)

    for column in range(0, ff, 128):
        for at, rows, done in feed_spans(column // 128 * width, width):
            w1_out[done : done + rows, column : column + 128] = held[0, at : at + rows, :].astype(F32)
    send(0, w1_out, w1_to)
    for column in range(0, width, 128):
        for at, rows, done in feed_spans(column // 128 * ff, ff):
            w2_out[done : done + rows, column : column + 128] = held[1, at : at + rows, :].astype(F32)
    send(1, w2_out, w2_to)
    targets = (joint_out, output_out, embed_out, small)
    for half, plan in enumerate(pack_plan(width, hidden, half_rows - feed_rows)):
        for which, column, first, rows, at in plan:
            lanes = slice(column * 128, column * 128 + 128)
            done = 0
            while done < rows:
                block, inner = divmod(at + done, attend_part)
                take = min(rows - done, attend_part - inner)
                start = block * quarter + feed_part + inner
                place_to = slice(first + done, first + done + take)
                targets[which][place_to, lanes] = held[half, start : start + take, :].astype(F32)
                done += take
    send(2, joint_out, joint_to)
    send(3, output_out, output_to)
    send(4, embed_out, embed_to)
    for out, row in zip(rows_out, (0, 1, 2, 8, 9, 10)):
        out[...] = small[row : row + 1, :]
    mask_out[...] = small[3:4, :]
    place_out[0] = small[4:7, 0:hidden]
    place_bias_out[...] = small[7:8, 0:hidden]
    for part in range(ff // width):
        expand_bias_out[:, part * width : (part + 1) * width] = small[11 + part : 12 + part, :]
    for copy in flying:
        copy.wait()


def call_unpack(core, place, halves, width, hidden, ff):
    side = len(halves[0])
    half_rows = halves[0][0].shape[0] * side
    large = [(1, width, ff), (1, ff, width), (1, width, 3 * width), (1, width, width), (1, hidden, width)]
    tiny = [(1, 3, hidden), (1, hidden), (1, ff), (1, width)] + [(1, width)] * 6
    return pl.pallas_call(
        lambda *refs: unpack(side, ff * width // 128, *refs),
        in_specs=[scalar()] * 2 + [vmem()] * (2 * side),
        out_specs=[in_hbm()] * len(large) + [vmem()] * len(tiny),
        out_shape=[pltpu.HBM(shape, F32) for shape in large] + [sds(shape, F32) for shape in tiny],
        scratch_shapes=[pltpu.VMEM((2, half_rows, 128), BF)]
        + [pltpu.VMEM(shape[1:], F32) for shape in large]
        + [pltpu.VMEM((16, width), F32), pltpu.SemaphoreType.DMA((5,))],
        compiler_params=pltpu.CompilerParams(vmem_limit_bytes=20 * 2**20),
        cost_estimate=cost(5),
        name="unpack",
    )(core, place, *halves[0], *halves[1])


def shards(
    tokens,
    centres,
    visible,
    lengths,
    cotangent,
    attend_gain,
    attend_shift,
    joint_weight,
    output_weight,
    output_bias,
    feed_gain,
    feed_shift,
    expand_weight,
    expand_bias,
    reduce_weight,
    reduce_bias,
    place_weight,
    place_bias,
    embed_weight,
    mask_token,
):
    phase = lax.axis_index("pipe")
    encoding = phase == 0
    micro, rows, width = tokens.shape
    half = micro // 2
    hidden = place_weight.shape[2]
    core = jnp.reshape(phase, (1,)).astype(jnp.int32)
    no_mask = jnp.zeros((1, width), F32)
    mask_row = mask_token[None, :]
    flat = lambda a: a.reshape(half * rows, a.shape[-1])
    here = lambda a: flat(lax.dynamic_slice_in_dim(a, phase * half, half, 0))
    given = here(cotangent)

    wide = lambda piece: jnp.pad(piece, ((0, 0), (0, width - hidden)))
    small = jnp.concatenate(
        [attend_gain, attend_shift, output_bias, feed_gain, feed_shift, reduce_bias, jnp.zeros((2, width), F32)]
        + [wide(place_weight[0]), wide(place_bias), expand_bias.reshape(-1, width)]
    )
    own = [small, joint_weight[0], output_weight[0], embed_weight[0], expand_weight[0], reduce_weight[0]]
    other = [lax.ppermute(piece, "pipe", SWAP) for piece in own]
    both = [pair for mine in zip(own, other) for pair in mine]
    attend_weights = both[:8]
    feed_weights_both = both[:2] + both[8:]

    unit = 256
    ff = expand_weight.shape[2]

    def joined(enc_part, dec_part):
        got = lax.ppermute(jnp.where(encoding, dec_part, enc_part), "pipe", SWAP)
        front = jnp.where(encoding, enc_part, got)
        second = jnp.where(encoding, got, dec_part)
        return jnp.concatenate([front, second], 0).reshape(1, micro, rows, width)

    ex, ej, ee, ei, em, emid = call_attend_forward(
        False, rows, core, lengths, here(tokens), centres, visible, mask_row, attend_weights
    )
    enc_out = call_feed_forward(core, emid, feed_weights_both)
    dx, dj, de, di, dm, dmid = call_attend_forward(
        True, rows, core, lengths, enc_out, centres, visible, mask_row, attend_weights
    )
    feed_rows = ff * width // 128
    attend_rows = packed_half_rows(width, hidden, unit)
    dec, enc = [Chain(phase, (feed_rows, attend_rows)) for _ in range(2)]
    dback, d_small, dec_out, *dec_halves = call_feed_backward(1, core, dmid, given, feed_weights_both, feed_rows)
    dec.start(*dec_halves)
    ddx, enc_back, d_mask, *dec_halves = call_attend_backward(
        True, rows, core, dback, dx, centres, visible, dj, de, di, dm, attend_weights, d_small, no_mask,
        attend_rows,
    )
    dec.start(*dec_halves)
    eback, e_small, *enc_halves = call_feed_backward(0, core, emid, enc_back, feed_weights_both, feed_rows)
    enc.start(*enc_halves)
    phase_out = joined(enc_out, dec_out)
    eback, phase_out, dec.pairs = together(eback, phase_out, dec.pairs)
    dec.scatter_first()
    edx, _, _, *enc_halves = call_attend_backward(
        False, rows, core, eback, ex, centres, visible, ej, ee, ei, em, attend_weights, e_small, d_mask,
        attend_rows,
    )
    enc_halves, dec.blocks, enc.pairs = together(enc_halves, dec.blocks, enc.pairs)
    enc.start(*enc_halves)
    halves, (edx, ddx) = sum_chains(phase, dec, enc, (edx, ddx))
    phase_in_grad = joined(edx, ddx)
    halves, phase_in_grad = together(halves, phase_in_grad)
    place = jnp.stack(enc.places).astype(jnp.int32)
    (w1_grad, w2_grad, joint_grad, output_grad, embed_grad, place_grad, place_bias_grad, expand_bias_grad, mask_grad, *vectors) = (
        call_unpack(core, place, halves, width, hidden, ff)
    )
    attend_gain_grad, attend_shift_grad, output_bias_grad, feed_gain_grad, feed_shift_grad, reduce_bias_grad = vectors
    return (
        phase_out, phase_in_grad, attend_gain_grad, attend_shift_grad, joint_grad, output_grad, output_bias_grad,
        feed_gain_grad, feed_shift_grad, w1_grad, expand_bias_grad, w2_grad, reduce_bias_grad, place_grad,
        place_bias_grad, embed_grad, mask_grad.reshape(width),
    )


def solution(mesh):
    in_specs = (
        P(None, "dp", None),
        P(None, None, "dp"),
        P(None, "dp"),
        P(None, "dp"),
        P(None, "dp", None),
        P("pipe", None),
        P("pipe", None),
        P("pipe", None, None),
        P("pipe", None, None),
        P("pipe", None),
        P("pipe", None),
        P("pipe", None),
        P("pipe", None, None),
        P("pipe", None),
        P("pipe", None, None),
        P("pipe", None),
        P("pipe", None, None),
        P("pipe", None),
        P("pipe", None, None),
        P(),
    )
    out_specs = (
        P("pipe", None, "dp", None),
        P("pipe", None, "dp", None),
        P("pipe", None),
        P("pipe", None),
        P("pipe", None, None),
        P("pipe", None, None),
        P("pipe", None),
        P("pipe", None),
        P("pipe", None),
        P("pipe", None, None),
        P("pipe", None),
        P("pipe", None, None),
        P("pipe", None),
        P("pipe", None, None),
        P("pipe", None),
        P("pipe", None, None),
        P(),
    )
    return jax.shard_map(shards, mesh=mesh, in_specs=in_specs, out_specs=out_specs, check_vma=False)
```

```python
import math

import jax
import jax.numpy as jnp
from jax import lax
from jax.experimental import pallas as pl
from jax.experimental.pallas import tpu as pltpu
from jax.sharding import PartitionSpec as P

HEADS = 6
NEG_FILL = -1e30
NORM_EPS = 1e-05
GELU_A = math.sqrt(2.0 / math.pi)
GELU_B = GELU_A * 0.044715
BF = jnp.bfloat16
F32 = jnp.float32
VMEM_LIMIT = 16 * 2**20


def dot(a, b):
    return jnp.dot(a, b, preferred_element_type=F32)


def dot_rt(a, b):
    return lax.dot_general(a, b, (((1,), (1,)), ((), ())), preferred_element_type=F32)


def dot_lt(a, b):
    return lax.dot_general(a, b, (((0,), (0,)), ((), ())), preferred_element_type=F32)


def gelu_both(v):
    v2 = v * v
    h = 0.5 * jnp.tanh(v * (GELU_A + GELU_B * v2)) + 0.5
    slope = h + (h - h * h) * (v * (2.0 * GELU_A + 6.0 * GELU_B * v2))
    return v * h, slope


def gelu_only(v):
    return v * (0.5 * jnp.tanh(v * (GELU_A + GELU_B * (v * v))) + 0.5)


def norm_parts(x):
    scale = 1.0 / x.shape[-1]
    centred = x - jnp.sum(x, -1, keepdims=True) * scale
    var = jnp.sum(centred * centred, -1, keepdims=True) * scale
    inverse = lax.rsqrt(var + NORM_EPS)
    return centred * inverse, inverse


def norm_back(u, z, inverse, gain):
    scale = 1.0 / u.shape[-1]
    w = u * gain
    m1 = jnp.sum(w, -1, keepdims=True) * scale
    m2 = jnp.sum(w * z, -1, keepdims=True) * scale
    return inverse * (w - m1 - z * m2)


def three_parts(value):
    parts = []
    for _ in range(3):
        parts.append(value.astype(BF))
        value = value - parts[-1].astype(F32)
    return parts


def place_pre(centre, place_weight, place_bias):
    c, w = three_parts(centre), three_parts(place_weight)
    pairs = ((0, 0), (0, 1), (1, 0), (0, 2), (2, 0), (1, 1))
    left = jnp.concatenate([c[i].astype(F32) for i, _ in pairs], axis=0).astype(BF)
    right = jnp.concatenate([w[j].astype(F32) for _, j in pairs], axis=0).astype(BF)
    return dot_lt(left, right) + place_bias


def place_back(centre, dpre):
    c, d = three_parts(centre), three_parts(dpre)
    count, width = centre.shape[0], dpre.shape[1]
    left = jnp.concatenate([part.astype(F32) for part in c], axis=0).astype(BF)
    products = dot(left, jnp.concatenate(d, axis=1))
    block = lambda i, j: products[i * count : (i + 1) * count, j * width : (j + 1) * width]
    return block(0, 0) + ((block(0, 1) + block(1, 0)) + (block(0, 2) + block(2, 0) + block(1, 1)))


def column_of(row, width):
    rows = lax.broadcasted_iota(jnp.int32, (16, row.shape[1]), 0)
    top = jnp.where(rows == 0, jnp.broadcast_to(row, rows.shape), 0).astype(F32)
    return dot_lt(top.astype(BF), jnp.ones((16, width), BF))


def segments(lengths, micro_index, slots, places):
    total = jnp.int32(0)
    seg = jnp.zeros(places.shape, jnp.int32)
    for slot in range(slots):
        total = total + lengths[micro_index, slot]
        seg = seg + (places >= total).astype(jnp.int32)
    return seg


def lane_low(shape, half):
    return lax.broadcasted_iota(jnp.int32, shape, 1) < half


SMALL = ("attend_gain", "attend_shift", "output_bias", "feed_gain", "feed_shift", "reduce_bias")


def small_row(values, name):
    place = SMALL.index(name)
    return values[place : place + 1, :]


def place_rows(values, hidden):
    return values[8:11, :hidden], values[11:12, :hidden]


def expand_row(values, width, ff):
    return [values[12 + part : 13 + part, :] for part in range(ff // width)]


def chosen(mine, own, other):
    return jnp.where(mine, own[...], other[...])


def attend_forward(decoding, rows, core, lengths, *refs):
    (x_in, centres, visible, mask_token, small_own, small_other, wj_own, wj_other) = refs[:8]
    (wo_own, wo_other, we_own, we_other) = refs[8:12]
    (x_out, joint_out, e_out, inv_out, mixed_out, mid_out, bias) = refs[12:19]
    total, width = x_out.shape
    half = total // rows
    slots = lengths.shape[1]
    head = width // HEADS
    pair = 2 * head
    mine = core[0] == int(decoding)
    small = chosen(mine, small_own, small_other)
    ag, ash, bo = (small_row(small, name) for name in SMALL[:3])
    we = chosen(mine, we_own, we_other)
    pw, pb = place_rows(small, we.shape[0])

    for block in range(half):
        span = slice(block * rows, (block + 1) * rows)
        micro_index = core[0] * half + block
        embed = dot(gelu_only(place_pre(centres[micro_index], pw, pb)).astype(BF), we)
        seen = visible[pl.ds(micro_index, 1), :]
        source = x_in[span, :].astype(F32)
        if decoding:
            shown = column_of(seen, 128)[:, :1] > 0.5
            source = jnp.where(shown, source, mask_token[...])
        x_out[span, :] = source + embed
        places_k = lax.broadcasted_iota(jnp.int32, (1, rows), 1)
        seg_k = segments(lengths, micro_index, slots, places_k)
        allowed = column_of(seg_k, 128)[:, :1].astype(jnp.int32) == seg_k
        if not decoding:
            places_q = lax.broadcasted_iota(jnp.int32, (rows, rows), 0)
            places_kk = lax.broadcasted_iota(jnp.int32, (rows, rows), 1)
            allowed = allowed & ((seen > 0) | (places_q == places_kk))
        bias[block] = jnp.where(allowed, 0.0, NEG_FILL)

    z, _ = norm_parts(x_out[...])
    joint_out[...] = dot((z * ag + ash).astype(BF), chosen(mine, wj_own, wj_other)).astype(BF)

    low_k = lane_low((rows, pair), head)
    for block in range(half):
        span = slice(block * rows, (block + 1) * rows)
        for p in range(HEADS // 2):
            cols = slice(p * pair, (p + 1) * pair)
            qp = joint_out[span, cols] * BF(head**-0.5)
            kp = joint_out[span, width + p * pair : width + (p + 1) * pair]
            vp = joint_out[span, 2 * width + p * pair : 2 * width + (p + 1) * pair]
            out = []
            for side in range(2):
                mine_k = low_k == (side == 0)
                s = dot_rt(jnp.where(mine_k, qp, BF(0)), kp) + bias[block]
                e = jnp.exp(s - jnp.max(s, -1, keepdims=True)).astype(BF)
                e_out[block * HEADS + 2 * p + side] = e
                out.append(dot(e, jnp.where(mine_k, vp, BF(1))))
            inv = 1.0 / pltpu.roll(jnp.where(low_k, out[1], out[0]), head, 1)
            inv_out[span, cols] = inv.astype(BF)
            mixed_out[span, cols] = (jnp.where(low_k, out[0], out[1]) * inv).astype(BF)
    wo = chosen(mine, wo_own, wo_other)
    mid_out[...] = x_out[...] + (dot(mixed_out[...], wo) + bo)


def pack_plan(width, hidden, half_rows):
    plan = ([], [])
    place = 0
    for which, (rows, columns) in enumerate(((width, 3 * width), (width, width), (hidden, width), (16, width))):
        for column in range(columns // 128):
            done = 0
            while done < rows:
                half, at = divmod(place, half_rows)
                count = min(rows - done, half_rows - at)
                plan[half].append((which, column, done, count, at))
                done += count
                place += count
    return plan


def packed_half_rows(width, hidden, unit):
    total = (3 * width * width + width * width + hidden * width + 16 * width) // 128
    return -(-total // (2 * unit)) * unit


def attend_backward(decoding, rows, core, *refs):
    (dmid_in, x_in, centres, visible, joint_in, e_in, inv_in, mixed_in) = refs[:8]
    (small_own, small_other, wj_own, wj_other, wo_own, wo_other, we_own, we_other) = refs[8:16]
    (small_feed, extra) = refs[16:18]
    dx_out, send_back, mask_g, half0, half1, send_halves = refs[18:24]
    dl, mu, dj, ds, joint_g, output_g, embed_g, small_g = refs[24:]
    total, width = x_in.shape
    half = total // rows
    head = width // HEADS
    pair = 2 * head
    mine = core[0] == int(decoding)
    small = chosen(mine, small_own, small_other)
    ag, ash = (small_row(small, name) for name in SMALL[:2])
    we = chosen(mine, we_own, we_other)
    hidden = we.shape[0]
    pw, pb = place_rows(small, hidden)

    dm = dmid_in[...].astype(BF)
    output_g[...] = dot_lt(mixed_in[...], dm)
    low_dl = (dot_rt(dm, chosen(mine, wo_own, wo_other)) * inv_in[...].astype(F32)).astype(BF)
    dl[...] = low_dl
    mu[...] = (low_dl.astype(F32) * -mixed_in[...].astype(F32)).astype(BF)
    small_g[...] = jnp.zeros(small_g.shape, F32)
    small_g[2:3, :] = jnp.sum(dm.astype(F32), 0, keepdims=True)

    low_k = lane_low((rows, pair), head)
    ones = jnp.ones((rows, pair), BF)
    for block in range(half):
        span = slice(block * rows, (block + 1) * rows)
        for p in range(HEADS // 2):
            cols = slice(p * pair, (p + 1) * pair)
            qp = joint_in[span, cols] * BF(head**-0.5)
            kp = joint_in[span, width + p * pair : width + (p + 1) * pair]
            vp = joint_in[span, 2 * width + p * pair : 2 * width + (p + 1) * pair]
            v_ext = jnp.concatenate([vp, ones], axis=1)
            dlp = dl[span, cols]
            mup = mu[span, cols]
            dq = dk = dv = None
            for side in range(2):
                mine_k = low_k == (side == 0)
                place = 2 * p + side
                d_one = jnp.where(mine_k, dlp, BF(0))
                u_one = jnp.where(mine_k, mup, BF(0))
                dp = dot_rt(jnp.concatenate([d_one, u_one], axis=1), v_ext)
                ds[place % 2] = (e_in[block * HEADS + place].astype(F32) * dp).astype(BF)
                q_one = jnp.where(mine_k, qp, BF(0))
                k_one = jnp.where(mine_k, kp, BF(0))
                dv_one = dot_lt(e_in[block * HEADS + place], d_one)
                dk_one = dot_lt(ds[place % 2], q_one)
                dq_one = dot(ds[place % 2], k_one)
                dv = dv_one if dv is None else dv + dv_one
                dk = dk_one if dk is None else dk + dk_one
                dq = dq_one if dq is None else dq + dq_one
            dj[span, cols] = (dq * head**-0.5).astype(BF)
            dj[span, width + p * pair : width + (p + 1) * pair] = dk.astype(BF)
            dj[span, 2 * width + p * pair : 2 * width + (p + 1) * pair] = dv.astype(BF)

    z, inverse = norm_parts(x_in[...])
    joint_g[...] = dot_lt((z * ag + ash).astype(BF), dj[...])
    dn = dot_rt(dj[...], chosen(mine, wj_own, wj_other))
    small_g[0:1, :] = jnp.sum(dn * z, 0, keepdims=True)
    small_g[1:2, :] = jnp.sum(dn, 0, keepdims=True)
    dx = dmid_in[...] + norm_back(dn, z, inverse, ag)
    dx_out[...] = dx
    ge = dx.astype(BF)
    acts = []
    for block in range(half):
        span = slice(block * rows, (block + 1) * rows)
        micro_index = core[0] * half + block
        if decoding:
            shown = column_of(visible[pl.ds(micro_index, 1), :], 128)[:, :1] > 0.5
            send_back[span, :] = jnp.where(shown, dx[span], 0.0).astype(BF)
            small_g[3:4, :] += jnp.sum(jnp.where(shown, 0.0, dx[span]), 0, keepdims=True)
        act, slope = gelu_both(place_pre(centres[micro_index], pw, pb))
        acts.append(act.astype(BF))
        dpre = slope * dot_rt(ge[span], we)
        small_g[4:7, 0:hidden] += place_back(centres[micro_index], dpre)
        small_g[7:8, 0:hidden] += jnp.sum(dpre, 0, keepdims=True)
    embed_g[...] = dot_lt(jnp.concatenate(acts, axis=0), ge)

    mask_g[...] = small_g[3:4, :]
    if not decoding:
        small_g[3:4, :] = extra[...]
    small_g[8:15, :] = small_feed[0:7, :]
    sources = (joint_g, output_g, embed_g, small_g)
    for target, plan in zip((half0, half1), pack_plan(width, hidden, half0.shape[0])):
        for which, column, first, count, at in plan:
            lanes = slice(column * 128, column * 128 + 128)
            target[at : at + count, :] = sources[which][first : first + count, lanes].astype(BF)
    send_halves()


def feed_start(mid_in, small, low):
    z, _ = norm_parts(mid_in[...])
    low[...] = (z * small_row(small, "feed_gain") + small_row(small, "feed_shift")).astype(BF)


def feed_bias(small, width, first, chunk):
    rows = [small[12 + part : 13 + part, :] for part in range(first // width, (first + chunk) // width)]
    return jnp.concatenate(rows, axis=1) if len(rows) > 1 else rows[0]


def row_blocks(total, rows):
    return [slice(first, first + rows) for first in range(0, total, rows)]


def feed_forward(chunk, rows, core, mid_in, *refs):
    small_own, small_other, w1_own, w1_other, w2_own, w2_other, out, low, acc = refs
    total, width = mid_in.shape
    mine = core[0] == 0
    small = chosen(mine, small_own, small_other)
    feed_start(mid_in, small, low)
    acc[...] = mid_in[...] + small_row(small, "reduce_bias")
    for first in range(0, w1_own.shape[1], chunk):
        cols = slice(first, first + chunk)
        w1 = jnp.where(mine, w1_own[:, cols], w1_other[:, cols])
        w2 = jnp.where(mine, w2_own[cols, :], w2_other[cols, :])
        bias = feed_bias(small, width, first, chunk)
        for span in row_blocks(total, rows):
            acc[span, :] += dot(gelu_only(dot(low[span, :], w1) + bias).astype(BF), w2)
    out[...] = acc[...].astype(BF)


def feed_weight_grads(cols, low, act_low, dh, g, half0, half1, small_g):
    width = g.shape[1]
    ff = half0.shape[0] * 128 // width
    w1_g = dot_lt(low, dh).astype(BF)
    w2_g = dot_lt(act_low, g).astype(BF)
    for first in range(0, cols.stop - cols.start, 128):
        place = (cols.start + first) // 128 * width
        half0[place : place + width, :] = w1_g[:, first : first + 128]
    for first in range(0, width, 128):
        place = first // 128 * ff
        half1[place + cols.start : place + cols.stop, :] = w2_g[:, first : first + 128]
    column_sum = jnp.sum(dh.astype(F32), 0, keepdims=True)
    for first in range(0, cols.stop - cols.start, width):
        row = 3 + (cols.start + first) // width
        small_g[row : row + 1, :] = column_sum[:, first : first + width]


def feed_tail(g_in, dn_acc, mid_in, small, dmid_out, small_g, rows):
    total = mid_in.shape[0]
    sums = None
    for span in row_blocks(total, rows):
        z, inverse = norm_parts(mid_in[span, :])
        g = g_in[span, :].astype(F32)
        dn = dn_acc[span, :]
        dmid_out[span, :] = g + norm_back(dn, z, inverse, small_row(small, "feed_gain"))
        new = [jnp.sum(value, 0, keepdims=True) for value in (dn * z, dn, g)]
        sums = new if sums is None else [a + b for a, b in zip(sums, new)]
    for row, value in enumerate(sums):
        small_g[row : row + 1, :] = value


def feed_backward(block, chunk, rows, core, mid_in, g_in, *refs):
    small_own, small_other, w1_own, w1_other, w2_own, w2_other = refs[:6]
    refs = refs[6:]
    dmid_out, small_g = refs[:2]
    half0, half1, send_halves, low, dn_acc, act_low, dh = refs[2 + block : 9 + block]
    out, acc = (refs[2], dmid_out) if block else (None, None)
    total, width = mid_in.shape
    ff = w1_own.shape[1]
    mine = core[0] == block
    small = chosen(mine, small_own, small_other)
    feed_start(mid_in, small, low)
    if block:
        acc[...] = mid_in[...] + small_row(small, "reduce_bias")
    for first in range(0, ff, chunk):
        cols = slice(first, first + chunk)
        w1 = jnp.where(mine, w1_own[:, cols], w1_other[:, cols])
        w2 = jnp.where(mine, w2_own[cols, :], w2_other[cols, :])
        bias = feed_bias(small, width, first, chunk)
        for span in row_blocks(total, rows):
            act, slope = gelu_both(dot(low[span, :], w1) + bias)
            act = act.astype(BF)
            act_low[span, :] = act
            if block:
                acc[span, :] += dot(act, w2)
            dh_rows = (slope * dot_rt(g_in[span, :], w2)).astype(BF)
            dh[span, :] = dh_rows
            dn = dot_rt(dh_rows, w1)
            dn_acc[span, :] = dn if first == 0 else dn_acc[span, :] + dn
        feed_weight_grads(cols, low[...], act_low[...], dh[...], g_in[...], half0, half1, small_g)
    send_halves()
    if block:
        out[...] = acc[...].astype(BF)
    feed_tail(g_in, dn_acc, mid_in, small, dmid_out, small_g, rows)


def params():
    return pltpu.CompilerParams(vmem_limit_bytes=VMEM_LIMIT)


def sds(shape, kind):
    return jax.ShapeDtypeStruct(shape, kind)


def scalar():
    return pl.BlockSpec(memory_space=pltpu.SMEM)


def cost(microseconds):
    return pl.CostEstimate(flops=int(microseconds * 1e9), bytes_accessed=2**20, transcendentals=0)


def anywhere():
    return pl.BlockSpec(memory_space=pl.ANY)


def anywhere():
    return pl.BlockSpec(memory_space=pl.ANY)


def vmem():
    return pl.BlockSpec(memory_space=pltpu.VMEM)


def anywhere():
    return pl.BlockSpec(memory_space=pl.ANY)


def in_hbm():
    return pl.BlockSpec(memory_space=pltpu.HBM)


def kernel_call(body, scalars, arrays, outs, scratch, limit, time, name, rows):
    in_specs = [scalar() for _ in scalars] + [vmem() for _ in arrays]
    first = len(in_specs)

    def run(*refs):
        core = refs[0]
        results = refs[first : first + len(outs)]
        keep, send = refs[first + len(outs) : first + len(outs) + 2]
        *held, half0, half1, sems = refs[first + len(outs) + 2 :]

        def both(act):
            for n, pair in enumerate(((keep, send), (send, keep))):

                @pl.when(core[0] == n)
                def _(pair=pair):
                    for slot, half in enumerate((half0, half1)):
                        act(pltpu.make_async_copy(half, pair[slot], sems.at[slot]))

        body(*refs[:first], *results, half0, half1, lambda: both(lambda copy: copy.start()), *held)
        both(lambda copy: copy.wait())

    return pl.pallas_call(
        run,
        in_specs=in_specs,
        out_specs=[vmem() for _ in outs] + [in_hbm()] * 2,
        out_shape=[sds(shape, kind) for shape, kind in outs] + [pltpu.HBM((rows, 128), BF)] * 2,
        scratch_shapes=[pltpu.VMEM(shape, kind) for shape, kind in scratch]
        + [pltpu.VMEM((rows, 128), BF)] * 2
        + [pltpu.SemaphoreType.DMA((2,))],
        compiler_params=pltpu.CompilerParams(vmem_limit_bytes=limit * 2**20),
        cost_estimate=cost(time),
        name=name,
    )(*scalars, *arrays)


def plain_call(body, scalars, arrays, outs, scratch, limit, time, name):
    return pl.pallas_call(
        body,
        in_specs=[scalar() for _ in scalars] + [vmem() for _ in arrays],
        out_specs=[vmem() for _ in outs],
        out_shape=[sds(shape, kind) for shape, kind in outs],
        scratch_shapes=[pltpu.VMEM(shape, kind) for shape, kind in scratch],
        compiler_params=pltpu.CompilerParams(vmem_limit_bytes=limit * 2**20),
        cost_estimate=cost(time),
        name=name,
    )(*scalars, *arrays)


LIMITS = dict(af=8, ab=13, ff=9, fb=22)


def call_attend_forward(decoding, rows, core, lengths, x_in, centres, visible, mask_token, weights):
    total, width = x_in.shape
    half = total // rows
    return plain_call(
        lambda *refs: attend_forward(decoding, rows, *refs),
        [core, lengths],
        [x_in, centres, visible, mask_token, *weights],
        [
            ((total, width), F32),
            ((total, 3 * width), BF),
            ((half * HEADS, rows, rows), BF),
            ((total, width), BF),
            ((total, width), BF),
            ((total, width), F32),
        ],
        [((half, rows, rows), F32)],
        LIMITS["af"],
        9,
        "attend_forward_dec" if decoding else "attend_forward_enc",
    )


def call_attend_backward(decoding, rows, core, dmid, x, centres, visible, joint, e, inv, mixed, weights, small_feed, extra, shared):
    total, width = x.shape
    hidden = weights[6].shape[0]
    return kernel_call(
        lambda *refs: attend_backward(decoding, rows, *refs),
        [core],
        [dmid, x, centres, visible, joint, e, inv, mixed, *weights, small_feed, extra],
        [((total, width), F32), ((total, width) if decoding else (16, width), BF), ((1, width), F32)],
        [
            ((total, width), BF),
            ((total, width), BF),
            ((total, 3 * width), BF),
            ((2, rows, rows), BF),
            ((width, 3 * width), F32),
            ((width, width), F32),
            ((hidden, width), F32),
            ((16, width), F32),
        ],
        LIMITS["ab"],
        15,
        "attend_backward_dec" if decoding else "attend_backward_enc",
        shared,
    )


def call_feed_forward(core, mid, weights, chunk=1536, rows=256):
    total, width = mid.shape
    return plain_call(
        lambda *refs: feed_forward(chunk, rows, *refs),
        [core],
        [mid, *weights],
        [((total, width), BF)],
        [((total, width), BF), ((total, width), F32)],
        LIMITS["ff"],
        6,
        "feed_forward_enc",
    )[0]


def call_feed_backward(block, core, mid, g, weights, shared, chunk=1536, rows=256):
    total, width = mid.shape
    outs = [((total, width), F32), ((8, width), F32)]
    scratch = [((total, width), BF), ((total, width), F32), ((total, chunk), BF), ((total, chunk), BF)]
    if block:
        outs.append(((total, width), BF))
    return kernel_call(
        lambda *refs: feed_backward(block, chunk, rows, *refs),
        [core],
        [mid, g, *weights],
        outs,
        scratch,
        LIMITS["fb"],
        14,
        "feed_backward_dec" if block else "feed_backward_enc",
        shared,
    )


def plus(*parts):
    total = parts[0].astype(F32)
    for part in parts[1:]:
        total = total + part.astype(F32)
    return total.astype(BF)


SWAP = [(0, 1), (1, 0)]


def split(side, by_copy, sources, digit, *refs):
    pairs = [refs[2 * n : 2 * n + 2] for n in range(sources)]
    outs = refs[2 * sources : 2 * sources + side]
    kept, come = refs[2 * sources + side :][:sources], refs[3 * sources + side :][:by_copy]
    added, in_sems, out_sems = refs[-3:]
    order = [*range(1, side), 0]
    cuts = []
    for t in range(side):
        at = 0
        cuts.append([])
        for n, (keep, got) in enumerate(pairs):
            count = kept[n].shape[1]
            rows = pl.ds(pl.multiple_of(lax.bitwise_xor(digit[0], t) * count, 16), count)
            copies = [pltpu.make_async_copy(keep.at[rows, :], kept[n].at[t], in_sems.at[t, n, 0])]
            if n < by_copy:
                copies.append(pltpu.make_async_copy(got.at[rows, :], come[n].at[t], in_sems.at[t, n, 1]))
            other = come[n].at[t] if n < by_copy else got.at[rows, :]
            cuts[-1].append((copies, kept[n], other, slice(at, at + count)))
            at += count
    for t in order:
        for copies, *_ in cuts[t]:
            for copy in copies:
                copy.start()
    leaving = []
    for t in order:
        for copies, mine, other, to in cuts[t]:
            for copy in copies:
                copy.wait()
            added[t, to, :] = (mine[t].astype(F32) + other[...].astype(F32)).astype(BF)
        leaving.append(pltpu.make_async_copy(added.at[t], outs[t], out_sems.at[t]))
        leaving[-1].start()
    for copy in leaving:
        copy.wait()


def held(array):
    return pltpu.with_memory_space_constraint(array, pltpu.HBM)


def call_split(side, digit, pairs, by_copy):
    counts = [keep.shape[0] // side for keep, _ in pairs]
    n = sum(counts)
    return pl.pallas_call(
        lambda *refs: split(side, by_copy, len(pairs), *refs),
        in_specs=[scalar()] + [in_hbm() if n % 2 == 0 or n // 2 < by_copy else vmem() for n in range(2 * len(pairs))],
        out_specs=[in_hbm()] * side,
        out_shape=[pltpu.HBM((n, 128), BF)] * side,
        scratch_shapes=[pltpu.VMEM((side, count, 128), BF) for count in counts]
        + [pltpu.VMEM((side, count, 128), BF) for count in counts[:by_copy]]
        + [pltpu.VMEM((side, n, 128), BF)]
        + [pltpu.SemaphoreType.DMA((side, len(pairs), 2)), pltpu.SemaphoreType.DMA((side,))],
        compiler_params=params(),
        cost_estimate=cost(3),
        name="split",
    )(digit, *[held(array) if n % 2 == 0 or n // 2 < by_copy else array for n, array in enumerate(sum(map(list, pairs), []))])


class Chain:
    def __init__(self, phase, rows):
        self.pairs = []
        count = lax.axis_size("dp")
        side = math.isqrt(count)
        self.plain = side * side != count or side & (side - 1) != 0 or any(n % (16 * count) for n in rows)
        self.side = side = 1 if self.plain else side
        place = lax.axis_index("dp")
        low, high = place % side, (place // side) % side
        self.first, self.second = jnp.where(phase == 0, low, high), jnp.where(phase == 0, high, low)
        self.places = [low * side + high, high * side + low]
        self.count = count
        self.near, self.far = range(1, side), range(side, side * side, side)
        self.there, self.across = self.both(self.near, self.far), self.both(self.far, self.near)

    def both(self, core0, core1):
        return [
            [(core * self.count + i, core * self.count + (i ^ masks[core])) for core in range(2) for i in range(self.count)]
            for masks in zip(core0, core1)
        ]

    def trade(self, sends, routes):
        return [lax.ppermute(send, ("pipe", "dp"), route) for send, route in zip(sends, routes)]

    def start(self, keep, send):
        self.pairs.append((keep, lax.ppermute(send, "pipe", SWAP)))

    def scatter_first(self, after=None):
        if self.plain:
            total = jnp.concatenate([keep.astype(F32) + got.astype(F32) for keep, got in self.pairs], 0)
            self.blocks = [lax.psum(total, "dp").astype(BF)]
            return
        digit = jnp.reshape(self.first, (1,)).astype(jnp.int32)
        mine, *sends = call_split(self.side, digit, self.pairs, len(self.pairs) - (after is not None))
        if after is not None:
            sends, after.blocks = together(sends, after.blocks)
        self.blocks = [mine] + self.trade(sends, self.there)

    def scatter_second(self):
        if self.plain:
            return
        block = plus(*self.blocks)
        pieces = block.reshape(self.side, block.shape[0] // self.side, 128)
        pick = lambda k: lax.dynamic_index_in_dim(pieces, self.second ^ k, 0, keepdims=False)
        self.blocks = [pick(0)] + self.trade([pick(k) for k in range(1, self.side)], self.across)

    def finish(self):
        if not self.plain:
            self.blocks = [plus(*self.blocks)]
        return self.blocks[0]


def together(*groups):
    return lax.optimization_barrier(groups)


def sum_chains(phase, dec, enc, late):
    dec.scatter_second()
    enc.scatter_first(dec)
    dec.blocks, enc.blocks = together(dec.blocks, enc.blocks)
    enc.scatter_second()
    one, other = enc.finish(), dec.finish()
    mine = jnp.where(phase == 0, one, other)
    got = lax.ppermute(jnp.where(phase == 0, other, one), "pipe", SWAP)
    halves = [jnp.where(phase == 0, mine, got), jnp.where(phase == 0, got, mine)]
    if dec.plain:
        return [[half] for half in halves], late
    near, far = [dec.both(masks, masks) for masks in (dec.near, dec.far)]
    mixed_first, mixed_last = dec.both(dec.far, dec.near), dec.both(dec.near, dec.far)
    halves = together(*halves)
    more = dec.side - 1
    halves = [jnp.concatenate([half] + dec.trade([half] * more, routes), 0) for half, routes in zip(halves, (far, mixed_first))]
    halves[0], late = together(halves[0], late)
    return [[half] + dec.trade([half] * more, routes) for half, routes in zip(halves, (near, mixed_last))], late


def unpack(side, feed_rows, core, place, *refs):
    blocks, outs = refs[: 2 * side], refs[2 * side :]
    (w1_to, w2_to, joint_to, output_to, embed_to) = outs[:5]
    (place_out, place_bias_out, expand_bias_out, mask_out) = outs[5:9]
    rows_out = outs[9:15]
    held, w1_out, w2_out, joint_out, output_out, embed_out, small, out_sems = outs[15:]
    width, ff = w1_out.shape
    hidden = embed_out.shape[0]
    half_rows = held.shape[1]
    n = half_rows // side**2
    quarter, feed_part = half_rows // side, feed_rows // side
    attend_part = quarter - feed_part

    def feed_spans(first, rows):
        done = 0
        while done < rows:
            block, inner = divmod(first + done, feed_part)
            take = min(rows - done, feed_part - inner)
            yield block * quarter + inner, take, done
            done += take

    for here in range(2):

        @pl.when(core[0] == here)
        def _(here=here):
            for half in range(2):
                for a in range(side):
                    for b in range(side):
                        shift = b * side + a if half == 1 and here == 0 else a * side + b
                        piece = lax.bitwise_xor(place[half], shift)
                        rows = pl.ds(pl.multiple_of(piece * n, 16), n)
                        held[half, rows, :] = blocks[half * side + a][b * n : b * n + n, :]

    flying = []

    def send(slot, source, target):
        copy = pltpu.make_async_copy(source, target.at[0], out_sems.at[slot])
        copy.start()
        flying.append(copy)

    for column in range(0, ff, 128):
        for at, rows, done in feed_spans(column // 128 * width, width):
            w1_out[done : done + rows, column : column + 128] = held[0, at : at + rows, :].astype(F32)
    send(0, w1_out, w1_to)
    for column in range(0, width, 128):
        for at, rows, done in feed_spans(column // 128 * ff, ff):
            w2_out[done : done + rows, column : column + 128] = held[1, at : at + rows, :].astype(F32)
    send(1, w2_out, w2_to)
    targets = (joint_out, output_out, embed_out, small)
    for half, plan in enumerate(pack_plan(width, hidden, half_rows - feed_rows)):
        for which, column, first, rows, at in plan:
            lanes = slice(column * 128, column * 128 + 128)
            done = 0
            while done < rows:
                block, inner = divmod(at + done, attend_part)
                take = min(rows - done, attend_part - inner)
                start = block * quarter + feed_part + inner
                place_to = slice(first + done, first + done + take)
                targets[which][place_to, lanes] = held[half, start : start + take, :].astype(F32)
                done += take
    send(2, joint_out, joint_to)
    send(3, output_out, output_to)
    send(4, embed_out, embed_to)
    for out, row in zip(rows_out, (0, 1, 2, 8, 9, 10)):
        out[...] = small[row : row + 1, :]
    mask_out[...] = small[3, :]
    place_out[0] = small[4:7, 0:hidden]
    place_bias_out[...] = small[7:8, 0:hidden]
    for part in range(ff // width):
        expand_bias_out[:, part * width : (part + 1) * width] = small[11 + part : 12 + part, :]
    for copy in flying:
        copy.wait()


def call_unpack(core, place, halves, width, hidden, ff):
    side = len(halves[0])
    half_rows = halves[0][0].shape[0] * side
    large = [(1, width, ff), (1, ff, width), (1, width, 3 * width), (1, width, width), (1, hidden, width)]
    tiny = [(1, 3, hidden), (1, hidden), (1, ff), (width,)] + [(1, width)] * 6
    return pl.pallas_call(
        lambda *refs: unpack(side, ff * width // 128, *refs),
        in_specs=[scalar()] * 2 + [vmem()] * (2 * side),
        out_specs=[in_hbm()] * len(large) + [vmem()] * len(tiny),
        out_shape=[pltpu.HBM(shape, F32) for shape in large] + [sds(shape, F32) for shape in tiny],
        scratch_shapes=[pltpu.VMEM((2, half_rows, 128), BF)]
        + [pltpu.VMEM(shape[1:], F32) for shape in large]
        + [pltpu.VMEM((16, width), F32), pltpu.SemaphoreType.DMA((5,))],
        compiler_params=pltpu.CompilerParams(vmem_limit_bytes=20 * 2**20),
        cost_estimate=cost(5),
        name="unpack",
    )(core, place, *halves[0], *halves[1])


def shards(
    tokens,
    centres,
    visible,
    lengths,
    cotangent,
    attend_gain,
    attend_shift,
    joint_weight,
    output_weight,
    output_bias,
    feed_gain,
    feed_shift,
    expand_weight,
    expand_bias,
    reduce_weight,
    reduce_bias,
    place_weight,
    place_bias,
    embed_weight,
    mask_token,
):
    phase = lax.axis_index("pipe")
    encoding = phase == 0
    micro, rows, width = tokens.shape
    half = micro // 2
    hidden = place_weight.shape[2]
    core = jnp.reshape(phase, (1,)).astype(jnp.int32)
    no_mask = jnp.zeros((1, width), F32)
    mask_row = mask_token[None, :]
    flat = lambda a: a.reshape(half * rows, a.shape[-1])
    here = lambda a: flat(lax.dynamic_slice_in_dim(a, phase * half, half, 0))
    given = here(cotangent)

    wide = lambda piece: jnp.pad(piece, ((0, 0), (0, width - hidden)))
    small = jnp.concatenate(
        [attend_gain, attend_shift, output_bias, feed_gain, feed_shift, reduce_bias, jnp.zeros((2, width), F32)]
        + [wide(place_weight[0]), wide(place_bias), expand_bias.reshape(-1, width)]
    )
    own = [small, joint_weight[0], output_weight[0], embed_weight[0], expand_weight[0], reduce_weight[0]]
    other = [lax.ppermute(piece, "pipe", SWAP) for piece in own]
    both = [pair for mine in zip(own, other) for pair in mine]
    attend_weights = both[:8]
    feed_weights_both = both[:2] + both[8:]

    unit = 256
    ff = expand_weight.shape[2]

    def joined(enc_part, dec_part):
        got = lax.ppermute(jnp.where(encoding, dec_part, enc_part), "pipe", SWAP)
        front = jnp.where(encoding, enc_part, got)
        second = jnp.where(encoding, got, dec_part)
        return jnp.concatenate([front, second], 0).reshape(1, micro, rows, width)

    ex, ej, ee, ei, em, emid = call_attend_forward(
        False, rows, core, lengths, here(tokens), centres, visible, mask_row, attend_weights
    )
    enc_out = call_feed_forward(core, emid, feed_weights_both)
    dx, dj, de, di, dm, dmid = call_attend_forward(
        True, rows, core, lengths, enc_out, centres, visible, mask_row, attend_weights
    )
    feed_rows = ff * width // 128
    attend_rows = packed_half_rows(width, hidden, unit)
    dec, enc = [Chain(phase, (feed_rows, attend_rows)) for _ in range(2)]
    dback, d_small, dec_out, *dec_halves = call_feed_backward(1, core, dmid, given, feed_weights_both, feed_rows)
    dec.start(*dec_halves)
    ddx, enc_back, d_mask, *dec_halves = call_attend_backward(
        True, rows, core, dback, dx, centres, visible, dj, de, di, dm, attend_weights, d_small, no_mask,
        attend_rows,
    )
    dec.start(*dec_halves)
    eback, e_small, *enc_halves = call_feed_backward(0, core, emid, enc_back, feed_weights_both, feed_rows)
    enc.start(*enc_halves)
    phase_out = joined(enc_out, dec_out)
    eback, phase_out, dec.pairs = together(eback, phase_out, dec.pairs)
    dec.scatter_first()
    edx, _, _, *enc_halves = call_attend_backward(
        False, rows, core, eback, ex, centres, visible, ej, ee, ei, em, attend_weights, e_small, d_mask,
        attend_rows,
    )
    enc_halves, dec.blocks, enc.pairs = together(enc_halves, dec.blocks, enc.pairs)
    enc.start(*enc_halves)
    halves, (edx, ddx) = sum_chains(phase, dec, enc, (edx, ddx))
    phase_in_grad = joined(edx, ddx)
    halves, phase_in_grad = together(halves, phase_in_grad)
    place = jnp.stack(enc.places).astype(jnp.int32)
    (w1_grad, w2_grad, joint_grad, output_grad, embed_grad, place_grad, place_bias_grad, expand_bias_grad, mask_grad, *vectors) = (
        call_unpack(core, place, halves, width, hidden, ff)
    )
    attend_gain_grad, attend_shift_grad, output_bias_grad, feed_gain_grad, feed_shift_grad, reduce_bias_grad = vectors
    return (
        phase_out, phase_in_grad, attend_gain_grad, attend_shift_grad, joint_grad, output_grad, output_bias_grad,
        feed_gain_grad, feed_shift_grad, w1_grad, expand_bias_grad, w2_grad, reduce_bias_grad, place_grad,
        place_bias_grad, embed_grad, mask_grad,
    )


def solution(mesh):
    in_specs = (
        P(None, "dp", None),
        P(None, None, "dp"),
        P(None, "dp"),
        P(None, "dp"),
        P(None, "dp", None),
        P("pipe", None),
        P("pipe", None),
        P("pipe", None, None),
        P("pipe", None, None),
        P("pipe", None),
        P("pipe", None),
        P("pipe", None),
        P("pipe", None, None),
        P("pipe", None),
        P("pipe", None, None),
        P("pipe", None),
        P("pipe", None, None),
        P("pipe", None),
        P("pipe", None, None),
        P(),
    )
    out_specs = (
        P("pipe", None, "dp", None),
        P("pipe", None, "dp", None),
        P("pipe", None),
        P("pipe", None),
        P("pipe", None, None),
        P("pipe", None, None),
        P("pipe", None),
        P("pipe", None),
        P("pipe", None),
        P("pipe", None, None),
        P("pipe", None),
        P("pipe", None, None),
        P("pipe", None),
        P("pipe", None, None),
        P("pipe", None),
        P("pipe", None, None),
        P(),
    )
    return jax.shard_map(shards, mesh=mesh, in_specs=in_specs, out_specs=out_specs, check_vma=False)
```

```python
import math

import jax
import jax.numpy as jnp
from jax import lax
from jax.experimental import pallas as pl
from jax.experimental.pallas import tpu as pltpu
from jax.sharding import PartitionSpec as P

HEADS = 6
NEG_FILL = -1e30
NORM_EPS = 1e-05
GELU_A = math.sqrt(2.0 / math.pi)
GELU_B = GELU_A * 0.044715
BF = jnp.bfloat16
F32 = jnp.float32
VMEM_LIMIT = 16 * 2**20


def dot(a, b):
    return jnp.dot(a, b, preferred_element_type=F32)


def dot_rt(a, b):
    return lax.dot_general(a, b, (((1,), (1,)), ((), ())), preferred_element_type=F32)


def dot_lt(a, b):
    return lax.dot_general(a, b, (((0,), (0,)), ((), ())), preferred_element_type=F32)


def gelu_both(v):
    v2 = v * v
    h = 0.5 * jnp.tanh(v * (GELU_A + GELU_B * v2)) + 0.5
    slope = h + (h - h * h) * (v * (2.0 * GELU_A + 6.0 * GELU_B * v2))
    return v * h, slope


def gelu_only(v):
    return v * (0.5 * jnp.tanh(v * (GELU_A + GELU_B * (v * v))) + 0.5)


def norm_parts(x):
    scale = 1.0 / x.shape[-1]
    centred = x - jnp.sum(x, -1, keepdims=True) * scale
    var = jnp.sum(centred * centred, -1, keepdims=True) * scale
    inverse = lax.rsqrt(var + NORM_EPS)
    return centred * inverse, inverse


def norm_back(u, z, inverse, gain):
    scale = 1.0 / u.shape[-1]
    w = u * gain
    m1 = jnp.sum(w, -1, keepdims=True) * scale
    m2 = jnp.sum(w * z, -1, keepdims=True) * scale
    return inverse * (w - m1 - z * m2)


def three_parts(value):
    parts = []
    for _ in range(3):
        parts.append(value.astype(BF))
        value = value - parts[-1].astype(F32)
    return parts


def place_pre(centre, place_weight, place_bias):
    c, w = three_parts(centre), three_parts(place_weight)
    pairs = ((0, 0), (0, 1), (1, 0), (0, 2), (2, 0), (1, 1))
    left = jnp.concatenate([c[i].astype(F32) for i, _ in pairs], axis=0).astype(BF)
    right = jnp.concatenate([w[j].astype(F32) for _, j in pairs], axis=0).astype(BF)
    return dot_lt(left, right) + place_bias


def place_back(centre, dpre):
    c, d = three_parts(centre), three_parts(dpre)
    count, width = centre.shape[0], dpre.shape[1]
    left = jnp.concatenate([part.astype(F32) for part in c], axis=0).astype(BF)
    products = dot(left, jnp.concatenate(d, axis=1))
    block = lambda i, j: products[i * count : (i + 1) * count, j * width : (j + 1) * width]
    return block(0, 0) + ((block(0, 1) + block(1, 0)) + (block(0, 2) + block(2, 0) + block(1, 1)))


def column_of(row, width):
    rows = lax.broadcasted_iota(jnp.int32, (16, row.shape[1]), 0)
    top = jnp.where(rows == 0, jnp.broadcast_to(row, rows.shape), 0).astype(F32)
    return dot_lt(top.astype(BF), jnp.ones((16, width), BF))


def segments(lengths, micro_index, slots, places):
    total = jnp.int32(0)
    seg = jnp.zeros(places.shape, jnp.int32)
    for slot in range(slots):
        total = total + lengths[micro_index, slot]
        seg = seg + (places >= total).astype(jnp.int32)
    return seg


def lane_low(shape, half):
    return lax.broadcasted_iota(jnp.int32, shape, 1) < half


SMALL = ("attend_gain", "attend_shift", "output_bias", "feed_gain", "feed_shift", "reduce_bias")


def small_row(values, name):
    place = SMALL.index(name)
    return values[place : place + 1, :]


def place_rows(values, hidden):
    return values[8:11, :hidden], values[11:12, :hidden]


def expand_row(values, width, ff):
    return [values[12 + part : 13 + part, :] for part in range(ff // width)]


def chosen(mine, own, other):
    return jnp.where(mine, own[...], other[...])


def attend_forward(decoding, rows, core, lengths, *refs):
    (x_in, centres, visible, mask_token, small_own, small_other, wj_own, wj_other) = refs[:8]
    (wo_own, wo_other, we_own, we_other) = refs[8:12]
    (x_out, joint_out, e_out, inv_out, mixed_out, mid_out, bias) = refs[12:19]
    total, width = x_out.shape
    half = total // rows
    slots = lengths.shape[1]
    head = width // HEADS
    pair = 2 * head
    mine = core[0] == int(decoding)
    small = chosen(mine, small_own, small_other)
    ag, ash, bo = (small_row(small, name) for name in SMALL[:3])
    we = chosen(mine, we_own, we_other)
    pw, pb = place_rows(small, we.shape[0])

    for block in range(half):
        span = slice(block * rows, (block + 1) * rows)
        micro_index = core[0] * half + block
        embed = dot(gelu_only(place_pre(centres[micro_index], pw, pb)).astype(BF), we)
        seen = visible[pl.ds(micro_index, 1), :]
        source = x_in[span, :].astype(F32)
        if decoding:
            shown = column_of(seen, 128)[:, :1] > 0.5
            source = jnp.where(shown, source, mask_token[...])
        x_out[span, :] = source + embed
        places_k = lax.broadcasted_iota(jnp.int32, (1, rows), 1)
        seg_k = segments(lengths, micro_index, slots, places_k)
        allowed = column_of(seg_k, 128)[:, :1].astype(jnp.int32) == seg_k
        if not decoding:
            places_q = lax.broadcasted_iota(jnp.int32, (rows, rows), 0)
            places_kk = lax.broadcasted_iota(jnp.int32, (rows, rows), 1)
            allowed = allowed & ((seen > 0) | (places_q == places_kk))
        bias[block] = jnp.where(allowed, 0.0, NEG_FILL)

    z, _ = norm_parts(x_out[...])
    joint_out[...] = dot((z * ag + ash).astype(BF), chosen(mine, wj_own, wj_other)).astype(BF)

    low_k = lane_low((rows, pair), head)
    for block in range(half):
        span = slice(block * rows, (block + 1) * rows)
        for p in range(HEADS // 2):
            cols = slice(p * pair, (p + 1) * pair)
            qp = joint_out[span, cols] * BF(head**-0.5)
            kp = joint_out[span, width + p * pair : width + (p + 1) * pair]
            vp = joint_out[span, 2 * width + p * pair : 2 * width + (p + 1) * pair]
            out = []
            for side in range(2):
                mine_k = low_k == (side == 0)
                s = dot_rt(jnp.where(mine_k, qp, BF(0)), kp) + bias[block]
                e = jnp.exp(s - jnp.max(s, -1, keepdims=True)).astype(BF)
                e_out[block * HEADS + 2 * p + side] = e
                out.append(dot(e, jnp.where(mine_k, vp, BF(1))))
            inv = 1.0 / pltpu.roll(jnp.where(low_k, out[1], out[0]), head, 1)
            inv_out[span, cols] = inv.astype(BF)
            mixed_out[span, cols] = (jnp.where(low_k, out[0], out[1]) * inv).astype(BF)
    wo = chosen(mine, wo_own, wo_other)
    mid_out[...] = x_out[...] + (dot(mixed_out[...], wo) + bo)


def pack_plan(width, hidden, half_rows):
    plan = ([], [])
    place = 0
    for which, (rows, columns) in enumerate(((width, 3 * width), (width, width), (hidden, width), (16, width))):
        for column in range(columns // 128):
            done = 0
            while done < rows:
                half, at = divmod(place, half_rows)
                count = min(rows - done, half_rows - at)
                plan[half].append((which, column, done, count, at))
                done += count
                place += count
    return plan


def packed_half_rows(width, hidden, unit):
    total = (3 * width * width + width * width + hidden * width + 16 * width) // 128
    return -(-total // (2 * unit)) * unit


def attend_backward(decoding, rows, core, *refs):
    (dmid_in, x_in, centres, visible, joint_in, e_in, inv_in, mixed_in) = refs[:8]
    (small_own, small_other, wj_own, wj_other, wo_own, wo_other, we_own, we_other) = refs[8:16]
    (small_feed, extra) = refs[16:18]
    dx_out, send_back, mask_g, half0, half1, send_halves = refs[18:24]
    dl, mu, dj, ds, joint_g, output_g, embed_g, small_g = refs[24:]
    total, width = x_in.shape
    half = total // rows
    head = width // HEADS
    pair = 2 * head
    mine = core[0] == int(decoding)
    small = chosen(mine, small_own, small_other)
    ag, ash = (small_row(small, name) for name in SMALL[:2])
    we = chosen(mine, we_own, we_other)
    hidden = we.shape[0]
    pw, pb = place_rows(small, hidden)

    dm = dmid_in[...].astype(BF)
    output_g[...] = dot_lt(mixed_in[...], dm)
    low_dl = (dot_rt(dm, chosen(mine, wo_own, wo_other)) * inv_in[...].astype(F32)).astype(BF)
    dl[...] = low_dl
    mu[...] = (low_dl.astype(F32) * -mixed_in[...].astype(F32)).astype(BF)
    small_g[...] = jnp.zeros(small_g.shape, F32)
    small_g[2:3, :] = jnp.sum(dm.astype(F32), 0, keepdims=True)

    low_k = lane_low((rows, pair), head)
    ones = jnp.ones((rows, pair), BF)
    for block in range(half):
        span = slice(block * rows, (block + 1) * rows)
        for p in range(HEADS // 2):
            cols = slice(p * pair, (p + 1) * pair)
            qp = joint_in[span, cols] * BF(head**-0.5)
            kp = joint_in[span, width + p * pair : width + (p + 1) * pair]
            vp = joint_in[span, 2 * width + p * pair : 2 * width + (p + 1) * pair]
            v_ext = jnp.concatenate([vp, ones], axis=1)
            dlp = dl[span, cols]
            mup = mu[span, cols]
            dq = dk = dv = None
            for side in range(2):
                mine_k = low_k == (side == 0)
                place = 2 * p + side
                d_one = jnp.where(mine_k, dlp, BF(0))
                u_one = jnp.where(mine_k, mup, BF(0))
                dp = dot_rt(jnp.concatenate([d_one, u_one], axis=1), v_ext)
                ds[place % 2] = (e_in[block * HEADS + place].astype(F32) * dp).astype(BF)
                q_one = jnp.where(mine_k, qp, BF(0))
                k_one = jnp.where(mine_k, kp, BF(0))
                dv_one = dot_lt(e_in[block * HEADS + place], d_one)
                dk_one = dot_lt(ds[place % 2], q_one)
                dq_one = dot(ds[place % 2], k_one)
                dv = dv_one if dv is None else dv + dv_one
                dk = dk_one if dk is None else dk + dk_one
                dq = dq_one if dq is None else dq + dq_one
            dj[span, cols] = (dq * head**-0.5).astype(BF)
            dj[span, width + p * pair : width + (p + 1) * pair] = dk.astype(BF)
            dj[span, 2 * width + p * pair : 2 * width + (p + 1) * pair] = dv.astype(BF)

    z, inverse = norm_parts(x_in[...])
    joint_g[...] = dot_lt((z * ag + ash).astype(BF), dj[...])
    dn = dot_rt(dj[...], chosen(mine, wj_own, wj_other))
    small_g[0:1, :] = jnp.sum(dn * z, 0, keepdims=True)
    small_g[1:2, :] = jnp.sum(dn, 0, keepdims=True)
    dx = dmid_in[...] + norm_back(dn, z, inverse, ag)
    dx_out[...] = dx
    ge = dx.astype(BF)
    acts = []
    for block in range(half):
        span = slice(block * rows, (block + 1) * rows)
        micro_index = core[0] * half + block
        if decoding:
            shown = column_of(visible[pl.ds(micro_index, 1), :], 128)[:, :1] > 0.5
            send_back[span, :] = jnp.where(shown, dx[span], 0.0).astype(BF)
            small_g[3:4, :] += jnp.sum(jnp.where(shown, 0.0, dx[span]), 0, keepdims=True)
        act, slope = gelu_both(place_pre(centres[micro_index], pw, pb))
        acts.append(act.astype(BF))
        dpre = slope * dot_rt(ge[span], we)
        small_g[4:7, 0:hidden] += place_back(centres[micro_index], dpre)
        small_g[7:8, 0:hidden] += jnp.sum(dpre, 0, keepdims=True)
    embed_g[...] = dot_lt(jnp.concatenate(acts, axis=0), ge)

    mask_g[...] = small_g[3:4, :]
    if not decoding:
        small_g[3:4, :] = extra[...]
    small_g[8:15, :] = small_feed[0:7, :]
    sources = (joint_g, output_g, embed_g, small_g)
    for target, plan in zip((half0, half1), pack_plan(width, hidden, half0.shape[0])):
        for which, column, first, count, at in plan:
            lanes = slice(column * 128, column * 128 + 128)
            target[at : at + count, :] = sources[which][first : first + count, lanes].astype(BF)
    send_halves()


def feed_start(mid_in, small, low):
    z, _ = norm_parts(mid_in[...])
    low[...] = (z * small_row(small, "feed_gain") + small_row(small, "feed_shift")).astype(BF)


def feed_bias(small, width, first, chunk):
    rows = [small[12 + part : 13 + part, :] for part in range(first // width, (first + chunk) // width)]
    return jnp.concatenate(rows, axis=1) if len(rows) > 1 else rows[0]


def row_blocks(total, rows):
    return [slice(first, first + rows) for first in range(0, total, rows)]


def feed_forward(chunk, rows, core, mid_in, *refs):
    small_own, small_other, w1_own, w1_other, w2_own, w2_other, out, low, acc = refs
    total, width = mid_in.shape
    mine = core[0] == 0
    small = chosen(mine, small_own, small_other)
    feed_start(mid_in, small, low)
    acc[...] = mid_in[...] + small_row(small, "reduce_bias")
    for first in range(0, w1_own.shape[1], chunk):
        cols = slice(first, first + chunk)
        w1 = jnp.where(mine, w1_own[:, cols], w1_other[:, cols])
        w2 = jnp.where(mine, w2_own[cols, :], w2_other[cols, :])
        bias = feed_bias(small, width, first, chunk)
        for span in row_blocks(total, rows):
            acc[span, :] += dot(gelu_only(dot(low[span, :], w1) + bias).astype(BF), w2)
    out[...] = acc[...].astype(BF)


def feed_weight_grads(cols, low, act_low, dh, g, half0, half1, small_g):
    width = g.shape[1]
    ff = half0.shape[0] * 128 // width
    w1_g = dot_lt(low, dh).astype(BF)
    w2_g = dot_lt(act_low, g).astype(BF)
    for first in range(0, cols.stop - cols.start, 128):
        place = (cols.start + first) // 128 * width
        half0[place : place + width, :] = w1_g[:, first : first + 128]
    for first in range(0, width, 128):
        place = first // 128 * ff
        half1[place + cols.start : place + cols.stop, :] = w2_g[:, first : first + 128]
    column_sum = jnp.sum(dh.astype(F32), 0, keepdims=True)
    for first in range(0, cols.stop - cols.start, width):
        row = 3 + (cols.start + first) // width
        small_g[row : row + 1, :] = column_sum[:, first : first + width]


def feed_tail(g_in, dn_acc, mid_in, small, dmid_out, small_g, rows):
    total = mid_in.shape[0]
    sums = None
    for span in row_blocks(total, rows):
        z, inverse = norm_parts(mid_in[span, :])
        g = g_in[span, :].astype(F32)
        dn = dn_acc[span, :]
        dmid_out[span, :] = g + norm_back(dn, z, inverse, small_row(small, "feed_gain"))
        new = [jnp.sum(value, 0, keepdims=True) for value in (dn * z, dn, g)]
        sums = new if sums is None else [a + b for a, b in zip(sums, new)]
    for row, value in enumerate(sums):
        small_g[row : row + 1, :] = value


def feed_backward(block, chunk, rows, core, mid_in, g_in, *refs):
    small_own, small_other, w1_own, w1_other, w2_own, w2_other = refs[:6]
    refs = refs[6:]
    dmid_out, small_g = refs[:2]
    half0, half1, send_halves, low, dn_acc, act_low, dh = refs[2 + block : 9 + block]
    out, acc = (refs[2], dmid_out) if block else (None, None)
    total, width = mid_in.shape
    ff = w1_own.shape[1]
    mine = core[0] == block
    small = chosen(mine, small_own, small_other)
    feed_start(mid_in, small, low)
    if block:
        acc[...] = mid_in[...] + small_row(small, "reduce_bias")
    for first in range(0, ff, chunk):
        cols = slice(first, first + chunk)
        w1 = jnp.where(mine, w1_own[:, cols], w1_other[:, cols])
        w2 = jnp.where(mine, w2_own[cols, :], w2_other[cols, :])
        bias = feed_bias(small, width, first, chunk)
        for span in row_blocks(total, rows):
            act, slope = gelu_both(dot(low[span, :], w1) + bias)
            act = act.astype(BF)
            act_low[span, :] = act
            if block:
                acc[span, :] += dot(act, w2)
            dh_rows = (slope * dot_rt(g_in[span, :], w2)).astype(BF)
            dh[span, :] = dh_rows
            dn = dot_rt(dh_rows, w1)
            dn_acc[span, :] = dn if first == 0 else dn_acc[span, :] + dn
        feed_weight_grads(cols, low[...], act_low[...], dh[...], g_in[...], half0, half1, small_g)
    send_halves()
    if block:
        out[...] = acc[...].astype(BF)
    feed_tail(g_in, dn_acc, mid_in, small, dmid_out, small_g, rows)


def params():
    return pltpu.CompilerParams(vmem_limit_bytes=VMEM_LIMIT)


def sds(shape, kind):
    return jax.ShapeDtypeStruct(shape, kind)


def scalar():
    return pl.BlockSpec(memory_space=pltpu.SMEM)


def cost(microseconds):
    return pl.CostEstimate(flops=int(microseconds * 1e9), bytes_accessed=2**20, transcendentals=0)


def anywhere():
    return pl.BlockSpec(memory_space=pl.ANY)


def anywhere():
    return pl.BlockSpec(memory_space=pl.ANY)


def vmem():
    return pl.BlockSpec(memory_space=pltpu.VMEM)


def anywhere():
    return pl.BlockSpec(memory_space=pl.ANY)


def in_hbm():
    return pl.BlockSpec(memory_space=pltpu.HBM)


def kernel_call(body, scalars, arrays, outs, scratch, limit, time, name, rows, carry=()):
    in_specs = [scalar() for _ in scalars] + [vmem() for _ in arrays]
    first = len(in_specs)

    def run(*refs):
        core = refs[0]
        carried, refs = refs[first : first + len(carry)], refs[:first] + refs[first + len(carry) :]
        results = refs[first : first + len(outs)]
        keep, send = refs[first + len(outs) : first + len(outs) + 2]
        joined = refs[first + len(outs) + 2 :][: bool(carry)]
        *held, half0, half1, sems = refs[first + len(outs) + 2 + bool(carry) :]

        def move(act):
            for n in range(2 if carry else 0):

                @pl.when(core[0] == n)
                def _(n=n):
                    count = carried[0].shape[0]
                    for slot, (source, at) in enumerate(((carried[n], n), (carried[2], 1 - n))):
                        act(pltpu.make_async_copy(source, joined[0].at[pl.ds(at * count, count), :], sems.at[2 + slot]))

        move(lambda copy: copy.start())

        def both(act):
            for n, pair in enumerate(((keep, send), (send, keep))):

                @pl.when(core[0] == n)
                def _(pair=pair):
                    for slot, half in enumerate((half0, half1)):
                        act(pltpu.make_async_copy(half, pair[slot], sems.at[slot]))

        body(*refs[:first], *results, half0, half1, lambda: both(lambda copy: copy.start()), *held)
        both(lambda copy: copy.wait())
        move(lambda copy: copy.wait())

    more = [pltpu.HBM((2 * carry[0].shape[0], carry[0].shape[1]), BF)] if carry else []
    return pl.pallas_call(
        run,
        in_specs=in_specs + [vmem() for _ in carry],
        out_specs=[vmem() for _ in outs] + [in_hbm()] * (2 + len(more)),
        out_shape=[sds(shape, kind) for shape, kind in outs] + [pltpu.HBM((rows, 128), BF)] * 2 + more,
        scratch_shapes=[pltpu.VMEM(shape, kind) for shape, kind in scratch]
        + [pltpu.VMEM((rows, 128), BF)] * 2
        + [pltpu.SemaphoreType.DMA((4,))],
        compiler_params=pltpu.CompilerParams(vmem_limit_bytes=limit * 2**20),
        cost_estimate=cost(time),
        name=name,
    )(*scalars, *arrays, *carry)


def plain_call(body, scalars, arrays, outs, scratch, limit, time, name):
    return pl.pallas_call(
        body,
        in_specs=[scalar() for _ in scalars] + [vmem() for _ in arrays],
        out_specs=[vmem() for _ in outs],
        out_shape=[sds(shape, kind) for shape, kind in outs],
        scratch_shapes=[pltpu.VMEM(shape, kind) for shape, kind in scratch],
        compiler_params=pltpu.CompilerParams(vmem_limit_bytes=limit * 2**20),
        cost_estimate=cost(time),
        name=name,
    )(*scalars, *arrays)


LIMITS = dict(af=8, ab=13, ff=9, fb=22)


def call_attend_forward(decoding, rows, core, lengths, x_in, centres, visible, mask_token, weights):
    total, width = x_in.shape
    half = total // rows
    return plain_call(
        lambda *refs: attend_forward(decoding, rows, *refs),
        [core, lengths],
        [x_in, centres, visible, mask_token, *weights],
        [
            ((total, width), F32),
            ((total, 3 * width), BF),
            ((half * HEADS, rows, rows), BF),
            ((total, width), BF),
            ((total, width), BF),
            ((total, width), F32),
        ],
        [((half, rows, rows), F32)],
        LIMITS["af"],
        9,
        "attend_forward_dec" if decoding else "attend_forward_enc",
    )


def call_attend_backward(decoding, rows, core, dmid, x, centres, visible, joint, e, inv, mixed, weights, small_feed, extra, shared):
    total, width = x.shape
    hidden = weights[6].shape[0]
    return kernel_call(
        lambda *refs: attend_backward(decoding, rows, *refs),
        [core],
        [dmid, x, centres, visible, joint, e, inv, mixed, *weights, small_feed, extra],
        [((total, width), F32), ((total, width) if decoding else (16, width), BF), ((1, width), F32)],
        [
            ((total, width), BF),
            ((total, width), BF),
            ((total, 3 * width), BF),
            ((2, rows, rows), BF),
            ((width, 3 * width), F32),
            ((width, width), F32),
            ((hidden, width), F32),
            ((16, width), F32),
        ],
        LIMITS["ab"],
        15,
        "attend_backward_dec" if decoding else "attend_backward_enc",
        shared,
    )


def call_feed_forward(core, mid, weights, chunk=1536, rows=256):
    total, width = mid.shape
    return plain_call(
        lambda *refs: feed_forward(chunk, rows, *refs),
        [core],
        [mid, *weights],
        [((total, width), BF)],
        [((total, width), BF), ((total, width), F32)],
        LIMITS["ff"],
        6,
        "feed_forward_enc",
    )[0]


def call_feed_backward(block, core, mid, g, weights, shared, carry=(), chunk=1536, rows=256):
    total, width = mid.shape
    outs = [((total, width), F32), ((8, width), F32)]
    scratch = [((total, width), BF), ((total, width), F32), ((total, chunk), BF), ((total, chunk), BF)]
    if block:
        outs.append(((total, width), BF))
    return kernel_call(
        lambda *refs: feed_backward(block, chunk, rows, *refs),
        [core],
        [mid, g, *weights],
        outs,
        scratch,
        LIMITS["fb"],
        14,
        "feed_backward_dec" if block else "feed_backward_enc",
        shared,
        carry,
    )


def plus(*parts):
    total = parts[0].astype(F32)
    for part in parts[1:]:
        total = total + part.astype(F32)
    return total.astype(BF)


SWAP = [(0, 1), (1, 0)]


def split(side, by_copy, sources, digit, *refs):
    pairs = [refs[2 * n : 2 * n + 2] for n in range(sources)]
    outs = refs[2 * sources : 2 * sources + side]
    kept, come = refs[2 * sources + side :][:sources], refs[3 * sources + side :][:by_copy]
    added, in_sems, out_sems = refs[-3:]
    order = [*range(1, side), 0]
    cuts = []
    for t in range(side):
        at = 0
        cuts.append([])
        for n, (keep, got) in enumerate(pairs):
            count = kept[n].shape[1]
            rows = pl.ds(pl.multiple_of(lax.bitwise_xor(digit[0], t) * count, 16), count)
            copies = [pltpu.make_async_copy(keep.at[rows, :], kept[n].at[t], in_sems.at[t, n, 0])]
            if n < by_copy:
                copies.append(pltpu.make_async_copy(got.at[rows, :], come[n].at[t], in_sems.at[t, n, 1]))
            other = come[n].at[t] if n < by_copy else got.at[rows, :]
            cuts[-1].append((copies, kept[n], other, slice(at, at + count)))
            at += count
    for t in order:
        for copies, *_ in cuts[t]:
            for copy in copies:
                copy.start()
    leaving = []
    for t in order:
        for copies, mine, other, to in cuts[t]:
            for copy in copies:
                copy.wait()
            added[t, to, :] = (mine[t].astype(F32) + other[...].astype(F32)).astype(BF)
        leaving.append(pltpu.make_async_copy(added.at[t], outs[t], out_sems.at[t]))
        leaving[-1].start()
    for copy in leaving:
        copy.wait()


def held(array):
    return pltpu.with_memory_space_constraint(array, pltpu.HBM)


def call_split(side, digit, pairs, by_copy):
    counts = [keep.shape[0] // side for keep, _ in pairs]
    n = sum(counts)
    return pl.pallas_call(
        lambda *refs: split(side, by_copy, len(pairs), *refs),
        in_specs=[scalar()] + [in_hbm() if n % 2 == 0 or n // 2 < by_copy else vmem() for n in range(2 * len(pairs))],
        out_specs=[in_hbm()] * side,
        out_shape=[pltpu.HBM((n, 128), BF)] * side,
        scratch_shapes=[pltpu.VMEM((side, count, 128), BF) for count in counts]
        + [pltpu.VMEM((side, count, 128), BF) for count in counts[:by_copy]]
        + [pltpu.VMEM((side, n, 128), BF)]
        + [pltpu.SemaphoreType.DMA((side, len(pairs), 2)), pltpu.SemaphoreType.DMA((side,))],
        compiler_params=params(),
        cost_estimate=cost(3),
        name="split",
    )(digit, *[held(array) if n % 2 == 0 or n // 2 < by_copy else array for n, array in enumerate(sum(map(list, pairs), []))])


class Chain:
    def __init__(self, phase, rows):
        self.pairs = []
        count = lax.axis_size("dp")
        side = math.isqrt(count)
        self.plain = side * side != count or side & (side - 1) != 0 or any(n % (16 * count) for n in rows)
        self.side = side = 1 if self.plain else side
        place = lax.axis_index("dp")
        low, high = place % side, (place // side) % side
        self.first, self.second = jnp.where(phase == 0, low, high), jnp.where(phase == 0, high, low)
        self.places = [low * side + high, high * side + low]
        self.count = count
        self.near, self.far = range(1, side), range(side, side * side, side)
        self.there, self.across = self.both(self.near, self.far), self.both(self.far, self.near)

    def both(self, core0, core1):
        return [
            [(core * self.count + i, core * self.count + (i ^ masks[core])) for core in range(2) for i in range(self.count)]
            for masks in zip(core0, core1)
        ]

    def trade(self, sends, routes):
        return [lax.ppermute(send, ("pipe", "dp"), route) for send, route in zip(sends, routes)]

    def start(self, keep, send):
        self.pairs.append((keep, lax.ppermute(send, "pipe", SWAP)))

    def scatter_first(self, after=None):
        if self.plain:
            total = jnp.concatenate([keep.astype(F32) + got.astype(F32) for keep, got in self.pairs], 0)
            self.blocks = [lax.psum(total, "dp").astype(BF)]
            return
        digit = jnp.reshape(self.first, (1,)).astype(jnp.int32)
        mine, *sends = call_split(self.side, digit, self.pairs, int(after is not None))
        if after is not None:
            sends, after.blocks = together(sends, after.blocks)
        self.blocks = [mine] + self.trade(sends, self.there)

    def scatter_second(self):
        if self.plain:
            return
        block = plus(*self.blocks)
        pieces = block.reshape(self.side, block.shape[0] // self.side, 128)
        pick = lambda k: lax.dynamic_index_in_dim(pieces, self.second ^ k, 0, keepdims=False)
        self.blocks = [pick(0)] + self.trade([pick(k) for k in range(1, self.side)], self.across)

    def finish(self):
        if not self.plain:
            self.blocks = [plus(*self.blocks)]
        return self.blocks[0]


def together(*groups):
    return lax.optimization_barrier(groups)


def sum_chains(phase, dec, enc, late):
    dec.scatter_second()
    enc.scatter_first(dec)
    dec.blocks, enc.blocks = together(dec.blocks, enc.blocks)
    enc.scatter_second()
    one, other = enc.finish(), dec.finish()
    mine = jnp.where(phase == 0, one, other)
    got = lax.ppermute(jnp.where(phase == 0, other, one), "pipe", SWAP)
    halves = [jnp.where(phase == 0, mine, got), jnp.where(phase == 0, got, mine)]
    if dec.plain:
        return [[half] for half in halves], late
    near, far = [dec.both(masks, masks) for masks in (dec.near, dec.far)]
    mixed_first, mixed_last = dec.both(dec.far, dec.near), dec.both(dec.near, dec.far)
    halves = together(*halves)
    more = dec.side - 1
    halves = [jnp.concatenate([half] + dec.trade([half] * more, routes), 0) for half, routes in zip(halves, (far, mixed_first))]
    halves[0], late = together(halves[0], late)
    return [[half] + dec.trade([half] * more, routes) for half, routes in zip(halves, (near, mixed_last))], late


def unpack(side, feed_rows, core, place, *refs):
    blocks, outs = refs[: 2 * side], refs[2 * side :]
    (w1_to, w2_to, joint_to, output_to, embed_to) = outs[:5]
    (place_out, place_bias_out, expand_bias_out, mask_out) = outs[5:9]
    rows_out = outs[9:15]
    held, w1_out, w2_out, joint_out, output_out, embed_out, small, out_sems = outs[15:]
    width, ff = w1_out.shape
    hidden = embed_out.shape[0]
    half_rows = held.shape[1]
    n = half_rows // side**2
    quarter, feed_part = half_rows // side, feed_rows // side
    attend_part = quarter - feed_part

    def feed_spans(first, rows):
        done = 0
        while done < rows:
            block, inner = divmod(first + done, feed_part)
            take = min(rows - done, feed_part - inner)
            yield block * quarter + inner, take, done
            done += take

    for here in range(2):

        @pl.when(core[0] == here)
        def _(here=here):
            for half in range(2):
                for a in range(side):
                    for b in range(side):
                        shift = b * side + a if half == 1 and here == 0 else a * side + b
                        piece = lax.bitwise_xor(place[half], shift)
                        rows = pl.ds(pl.multiple_of(piece * n, 16), n)
                        held[half, rows, :] = blocks[half * side + a][b * n : b * n + n, :]

    flying = []

    def send(slot, source, target):
        copy = pltpu.make_async_copy(source, target.at[0], out_sems.at[slot])
        copy.start()
        flying.append(copy)

    for column in range(0, ff, 128):
        for at, rows, done in feed_spans(column // 128 * width, width):
            w1_out[done : done + rows, column : column + 128] = held[0, at : at + rows, :].astype(F32)
    send(0, w1_out, w1_to)
    for column in range(0, width, 128):
        for at, rows, done in feed_spans(column // 128 * ff, ff):
            w2_out[done : done + rows, column : column + 128] = held[1, at : at + rows, :].astype(F32)
    send(1, w2_out, w2_to)
    targets = (joint_out, output_out, embed_out, small)
    for half, plan in enumerate(pack_plan(width, hidden, half_rows - feed_rows)):
        for which, column, first, rows, at in plan:
            lanes = slice(column * 128, column * 128 + 128)
            done = 0
            while done < rows:
                block, inner = divmod(at + done, attend_part)
                take = min(rows - done, attend_part - inner)
                start = block * quarter + feed_part + inner
                place_to = slice(first + done, first + done + take)
                targets[which][place_to, lanes] = held[half, start : start + take, :].astype(F32)
                done += take
    send(2, joint_out, joint_to)
    send(3, output_out, output_to)
    send(4, embed_out, embed_to)
    for out, row in zip(rows_out, (0, 1, 2, 8, 9, 10)):
        out[...] = small[row : row + 1, :]
    mask_out[...] = small[3, :]
    place_out[0] = small[4:7, 0:hidden]
    place_bias_out[...] = small[7:8, 0:hidden]
    for part in range(ff // width):
        expand_bias_out[:, part * width : (part + 1) * width] = small[11 + part : 12 + part, :]
    for copy in flying:
        copy.wait()


def call_unpack(core, place, halves, width, hidden, ff):
    side = len(halves[0])
    half_rows = halves[0][0].shape[0] * side
    large = [(1, width, ff), (1, ff, width), (1, width, 3 * width), (1, width, width), (1, hidden, width)]
    tiny = [(1, 3, hidden), (1, hidden), (1, ff), (width,)] + [(1, width)] * 6
    return pl.pallas_call(
        lambda *refs: unpack(side, ff * width // 128, *refs),
        in_specs=[scalar()] * 2 + [vmem()] * (2 * side),
        out_specs=[in_hbm()] * len(large) + [vmem()] * len(tiny),
        out_shape=[pltpu.HBM(shape, F32) for shape in large] + [sds(shape, F32) for shape in tiny],
        scratch_shapes=[pltpu.VMEM((2, half_rows, 128), BF)]
        + [pltpu.VMEM(shape[1:], F32) for shape in large]
        + [pltpu.VMEM((16, width), F32), pltpu.SemaphoreType.DMA((5,))],
        compiler_params=pltpu.CompilerParams(vmem_limit_bytes=20 * 2**20),
        cost_estimate=cost(5),
        name="unpack",
    )(core, place, *halves[0], *halves[1])


def shards(
    tokens,
    centres,
    visible,
    lengths,
    cotangent,
    attend_gain,
    attend_shift,
    joint_weight,
    output_weight,
    output_bias,
    feed_gain,
    feed_shift,
    expand_weight,
    expand_bias,
    reduce_weight,
    reduce_bias,
    place_weight,
    place_bias,
    embed_weight,
    mask_token,
):
    phase = lax.axis_index("pipe")
    encoding = phase == 0
    micro, rows, width = tokens.shape
    half = micro // 2
    hidden = place_weight.shape[2]
    core = jnp.reshape(phase, (1,)).astype(jnp.int32)
    no_mask = jnp.zeros((1, width), F32)
    mask_row = mask_token[None, :]
    flat = lambda a: a.reshape(half * rows, a.shape[-1])
    here = lambda a: flat(lax.dynamic_slice_in_dim(a, phase * half, half, 0))
    given = here(cotangent)

    wide = lambda piece: jnp.pad(piece, ((0, 0), (0, width - hidden)))
    small = jnp.concatenate(
        [attend_gain, attend_shift, output_bias, feed_gain, feed_shift, reduce_bias, jnp.zeros((2, width), F32)]
        + [wide(place_weight[0]), wide(place_bias), expand_bias.reshape(-1, width)]
    )
    own = [small, joint_weight[0], output_weight[0], embed_weight[0], expand_weight[0], reduce_weight[0]]
    other = [lax.ppermute(piece, "pipe", SWAP) for piece in own]
    both = [pair for mine in zip(own, other) for pair in mine]
    attend_weights = both[:8]
    feed_weights_both = both[:2] + both[8:]

    unit = 256
    ff = expand_weight.shape[2]

    def joined(enc_part, dec_part):
        got = lax.ppermute(jnp.where(encoding, dec_part, enc_part), "pipe", SWAP)
        front = jnp.where(encoding, enc_part, got)
        second = jnp.where(encoding, got, dec_part)
        return jnp.concatenate([front, second], 0).reshape(1, micro, rows, width)

    ex, ej, ee, ei, em, emid = call_attend_forward(
        False, rows, core, lengths, here(tokens), centres, visible, mask_row, attend_weights
    )
    enc_out = call_feed_forward(core, emid, feed_weights_both)
    dx, dj, de, di, dm, dmid = call_attend_forward(
        True, rows, core, lengths, enc_out, centres, visible, mask_row, attend_weights
    )
    feed_rows = ff * width // 128
    attend_rows = packed_half_rows(width, hidden, unit)
    dec, enc = [Chain(phase, (feed_rows, attend_rows)) for _ in range(2)]
    dback, d_small, dec_out, *dec_halves = call_feed_backward(1, core, dmid, given, feed_weights_both, feed_rows)
    dec.start(*dec_halves)
    ddx, enc_back, d_mask, *dec_halves = call_attend_backward(
        True, rows, core, dback, dx, centres, visible, dj, de, di, dm, attend_weights, d_small, no_mask,
        attend_rows,
    )
    dec.start(*dec_halves)
    carry = (enc_out, dec_out, lax.ppermute(jnp.where(encoding, dec_out, enc_out), "pipe", SWAP))
    eback, e_small, *enc_halves, phase_out = call_feed_backward(
        0, core, emid, enc_back, feed_weights_both, feed_rows, carry
    )
    phase_out = phase_out.reshape(1, micro, rows, width)
    enc.start(*enc_halves)
    eback, dec.pairs = together(eback, dec.pairs)
    dec.scatter_first()
    edx, _, _, *enc_halves = call_attend_backward(
        False, rows, core, eback, ex, centres, visible, ej, ee, ei, em, attend_weights, e_small, d_mask,
        attend_rows,
    )
    enc_halves, dec.blocks, enc.pairs = together(enc_halves, dec.blocks, enc.pairs)
    enc.start(*enc_halves)
    halves, (edx, ddx) = sum_chains(phase, dec, enc, (edx, ddx))
    phase_in_grad = joined(edx, ddx)
    halves, phase_in_grad = together(halves, phase_in_grad)
    place = jnp.stack(enc.places).astype(jnp.int32)
    (w1_grad, w2_grad, joint_grad, output_grad, embed_grad, place_grad, place_bias_grad, expand_bias_grad, mask_grad, *vectors) = (
        call_unpack(core, place, halves, width, hidden, ff)
    )
    attend_gain_grad, attend_shift_grad, output_bias_grad, feed_gain_grad, feed_shift_grad, reduce_bias_grad = vectors
    return (
        phase_out, phase_in_grad, attend_gain_grad, attend_shift_grad, joint_grad, output_grad, output_bias_grad,
        feed_gain_grad, feed_shift_grad, w1_grad, expand_bias_grad, w2_grad, reduce_bias_grad, place_grad,
        place_bias_grad, embed_grad, mask_grad,
    )


def solution(mesh):
    in_specs = (
        P(None, "dp", None),
        P(None, None, "dp"),
        P(None, "dp"),
        P(None, "dp"),
        P(None, "dp", None),
        P("pipe", None),
        P("pipe", None),
        P("pipe", None, None),
        P("pipe", None, None),
        P("pipe", None),
        P("pipe", None),
        P("pipe", None),
        P("pipe", None, None),
        P("pipe", None),
        P("pipe", None, None),
        P("pipe", None),
        P("pipe", None, None),
        P("pipe", None),
        P("pipe", None, None),
        P(),
    )
    out_specs = (
        P("pipe", None, "dp", None),
        P("pipe", None, "dp", None),
        P("pipe", None),
        P("pipe", None),
        P("pipe", None, None),
        P("pipe", None, None),
        P("pipe", None),
        P("pipe", None),
        P("pipe", None),
        P("pipe", None, None),
        P("pipe", None),
        P("pipe", None, None),
        P("pipe", None),
        P("pipe", None, None),
        P("pipe", None),
        P("pipe", None, None),
        P(),
    )
    return jax.shard_map(shards, mesh=mesh, in_specs=in_specs, out_specs=out_specs, check_vma=False)
```
